256 devices in a mesh: lat: 16 (over z, x_hi), lon: 16 (over x_lo, y, core).
Axes of the slice: x: 4 (x_hi: 2, x_lo: 2; x = x_hi * 2 + x_lo), y: 4, z: 8, core: 2. Of those that a mesh axis runs over, the one named last changes fastest.
Arguments:
- latents: bfloat16 [4, 96, 384, 512], P(None, 'lat', 'lon'), may hold values from -6 to 6
- mask_ids: int32 [96, 384], P('lat', 'lon'), may hold values from 0 to 3
- w_qkv: bfloat16 [512, 1536], replicated, may hold values from -0.35355339 to 0.35355339
- w_out: bfloat16 [512, 512], replicated, may hold values from -0.25 to 0.25
- w_kv: bfloat16 [512, 1024], replicated, may hold values from -0.25 to 0.25
- level_queries: bfloat16 [13, 512], replicated, may hold values from -12 to 12
- w_o: bfloat16 [512, 512], replicated, may hold values from -0.25 to 0.25
- w_head: bfloat16 [512, 80], replicated, may hold values from -0.25 to 0.25
- field_cotangent: bfloat16 [96, 384, 1040], P('lat', 'lon'), may hold values from -6 to 6
Outputs:
- mixed_latents: bfloat16 [4, 96, 384, 512], P(None, 'lat', 'lon')
- decoded: bfloat16 [96, 384, 1040], P('lat', 'lon')
- grad_kv: float32 [512, 1024], replicated
- grad_queries: float32 [13, 512], replicated
- grad_o: float32 [512, 512], replicated
- grad_head: float32 [512, 80], replicated
The draws below stay inside these ranges and needn't reach their ends.
All inputs are finite; a program needn't handle non-finite values.
Results may differ from the reference program's by a relative error of at most 0.025.
Values may be sent and summed in bfloat16 or wider, within the bound.
No kernel may reach another device: no remote copies, remote signals or barrier semaphores. Data moves between devices by JAX's collectives and lax.ppermute only.
A program may use at most 128 MiB of HBM per device.

```python
import math
import jax
import jax.numpy as jnp
from jax import lax

D = 512
HEADS = 8
LEV = 4
PLEV = 13
OUTS = 80
WL = 2
WH = 6
WW = 12
NLAT = 96
NLON = 384


def draw_w_qkv(key, part):
    key = jax.random.fold_in(key, 11)
    values = jax.random.truncated_normal(key, -4.0, 4.0, (D, 3 * D), jnp.float32) / jnp.sqrt(jnp.float32(D))
    return values.astype(jnp.bfloat16)


def draw_level_queries(key, part):
    key = jax.random.fold_in(key, 12)
    values = jax.random.truncated_normal(key, -4.0, 4.0, (PLEV, D), jnp.float32)
    return values.astype(jnp.bfloat16)


def plant(values, key, smallest, largest):
    index_at = [jax.random.randint(jax.random.fold_in(key, axis), (), 0, length) for axis, length in enumerate(values.shape)]
    longest = values.shape.index(max(values.shape))
    neighbour = index_at[:longest] + [(index_at[longest] + 1) % values.shape[longest]] + index_at[longest + 1:]
    return values.at[tuple(index_at)].set(smallest).at[tuple(neighbour)].set(largest)


def shard_levels(stream_key, shape, cuts, least, top_value):
    gain = 1.0
    for dim, parts in cuts:
        heights = jax.random.uniform(jax.random.fold_in(jax.random.fold_in(stream_key, 6), dim), (parts,), jnp.float32, least / len(cuts), top_value / len(cuts))
        gain = gain * jnp.repeat(jnp.exp(heights), shape[dim] // parts).reshape((-1,) + (1,) * (len(shape) - 1 - dim))
    return gain


def centred(own_key, extent, deviation, limit, cuts=(), dtype=jnp.bfloat16):
    values = jax.random.normal(own_key, extent, jnp.float32) * deviation
    if len(cuts) > 0:
        values = shard_levels(own_key, extent, cuts, -0.22, 0.18) * values
    return jnp.clip(values, min=-limit, max=limit).astype(dtype)


def setup_inputs(seed: int = 0) -> dict:
    splits = jax.random.split(jax.random.key(seed), 10)
    latents = centred(splits[0], (LEV, NLAT, NLON, D), 1.0, 6.0, ((1, 16), (2, 16)))
    mask_ids = plant(jax.random.randint(splits[1], (NLAT, NLON), 0, 4), jax.random.fold_in(splits[1], 1), 0, 3).astype(jnp.int32)
    w_qkv = draw_w_qkv(jax.random.fold_in(splits[9], 71), 0)
    w_out = centred(splits[3], (D, D), D ** -0.5, 0.25)
    w_kv = centred(splits[4], (D, 2 * D), D ** -0.5, 0.25)
    level_queries = draw_level_queries(jax.random.fold_in(splits[9], 71), 0)
    w_o = centred(splits[6], (D, D), D ** -0.5, 0.25)
    w_head = centred(splits[7], (D, OUTS), D ** -0.5, 0.25)
    field_cotangent = centred(splits[8], (NLAT, NLON, PLEV * OUTS), 1.0, 6.0, ((0, 16), (1, 16)))
    return dict(latents=latents, mask_ids=mask_ids, w_qkv=w_qkv, w_out=w_out, w_kv=w_kv, level_queries=level_queries, w_o=w_o, w_head=w_head, field_cotangent=field_cotangent)


norm_eps = 1e-05
clip_eps = 1e-06

def layer_norm(values):
    wide = values.astype(jnp.float32)
    center = wide - lax.optimization_barrier(jnp.mean(wide, axis=-1, keepdims=True))
    spread = lax.optimization_barrier(jnp.mean(center * center, axis=-1, keepdims=True))
    return (center * lax.rsqrt(spread + norm_eps)).astype(jnp.bfloat16)

def window_attention(block_tile, region, w_qkv, w_out):
    levels, height, across, features = block_tile.shape
    head_size = features // HEADS
    normed = layer_norm(block_tile).reshape(-1, features)
    projected = jnp.dot(normed, w_qkv, preferred_element_type=jnp.float32).astype(jnp.bfloat16)
    grid_shape = (levels // WL, WL, height // WH, WH, across // WW, WW)
    grouped = projected.reshape(grid_shape + (3, HEADS, head_size)).transpose(0, 2, 4, 1, 3, 5, 6, 7, 8)
    grouped = grouped.reshape(-1, WL * WH * WW, 3, HEADS, head_size)
    labels = region.reshape(grid_shape).transpose(0, 2, 4, 1, 3, 5).reshape(-1, WL * WH * WW)
    query_vecs = grouped[:, :, 0].astype(jnp.float32)
    key_vecs = grouped[:, :, 1].astype(jnp.float32)
    value_vecs = grouped[:, :, 2].astype(jnp.float32)
    scores = jnp.einsum('wqhe,wkhe->whqk', query_vecs, key_vecs) / math.sqrt(head_size)
    allowed = labels[:, None, :, None] == labels[:, None, None, :]
    scores = jnp.where(allowed, scores, -jnp.inf)
    weights = jax.nn.softmax(scores, axis=-1).astype(jnp.bfloat16)
    context = jnp.einsum('whqk,wkhe->wqhe', weights.astype(jnp.float32), value_vecs).astype(jnp.bfloat16)
    context = context.reshape(levels // WL, height // WH, across // WW, WL, WH, WW, features)
    context = context.transpose(0, 3, 1, 4, 2, 5, 6).reshape(-1, features)
    mixed = block_tile.reshape(-1, features).astype(jnp.float32) + jnp.dot(context, w_out, preferred_element_type=jnp.float32)
    return mixed.astype(jnp.bfloat16).reshape(levels, height, across, features)

def decode_block(latent_block, cot_block, w_kv, level_queries, w_o, w_head):
    levels, patches, features = latent_block.shape
    head_size = features // HEADS
    scale = 1.0 / math.sqrt(head_size)
    normed = layer_norm(latent_block).reshape(levels * patches, features)
    projected = jnp.dot(normed, w_kv, preferred_element_type=jnp.float32).astype(jnp.bfloat16)
    split_kv = projected.reshape(levels, patches, 2, HEADS, head_size).astype(jnp.float32)
    key_vecs = split_kv[:, :, 0]
    value_vecs = split_kv[:, :, 1]
    query_vecs = level_queries.astype(jnp.float32).reshape(PLEV, HEADS, head_size)
    scores = jnp.einsum('ahe,lphe->phal', query_vecs, key_vecs) * scale
    weights = jax.nn.softmax(scores, axis=-1)
    context = jnp.einsum('phal,lphe->pahe', weights, value_vecs).astype(jnp.bfloat16).reshape(patches * PLEV, features)
    hidden = jnp.dot(context, w_o, preferred_element_type=jnp.float32).reshape(patches, PLEV, features)
    hidden = (hidden + level_queries.astype(jnp.float32)[None]).astype(jnp.bfloat16).reshape(patches * PLEV, features)
    fields = jnp.dot(hidden, w_head, preferred_element_type=jnp.float32).astype(jnp.bfloat16)
    upstream = cot_block.reshape(patches * PLEV, OUTS)
    grad_head = jnp.dot(hidden.T, upstream, preferred_element_type=jnp.float32)
    d_hidden = jnp.dot(upstream, w_head.T, preferred_element_type=jnp.float32).astype(jnp.bfloat16)
    grad_out = jnp.dot(context.T, d_hidden, preferred_element_type=jnp.float32)
    d_context = jnp.dot(d_hidden, w_o.T, preferred_element_type=jnp.float32).reshape(patches, PLEV, HEADS, head_size)
    d_weights = jnp.einsum('pahe,lphe->phal', d_context, value_vecs)
    d_scores = weights * (d_weights - lax.optimization_barrier(jnp.sum(weights * d_weights, axis=-1, keepdims=True))) * scale
    d_values = jnp.einsum('phal,pahe->lphe', weights, d_context)
    d_keys = jnp.einsum('phal,ahe->lphe', d_scores, query_vecs)
    grad_query = jnp.einsum('phal,lphe->ahe', d_scores, key_vecs).reshape(PLEV, features)
    grad_query = grad_query + lax.optimization_barrier(jnp.sum(d_hidden.astype(jnp.float32).reshape(patches, PLEV, features), axis=0))
    d_pair = jnp.stack([d_keys, d_values], axis=2).astype(jnp.bfloat16).reshape(levels * patches, 2 * features)
    grad_kv = jnp.dot(normed.T, d_pair, preferred_element_type=jnp.float32)
    return (fields.reshape(patches, PLEV * OUTS), grad_kv, grad_query, grad_out, grad_head)

def reference(latents, mask_ids, w_qkv, w_out, w_kv, level_queries, w_o, w_head, field_cotangent):
    shift_levels = WL // 2
    shift_rows = WH // 2
    shift_cols = WW // 2
    shifted = jnp.roll(latents, (-shift_levels, -shift_rows, -shift_cols), axis=(0, 1, 2))
    labels = jnp.roll(mask_ids, (-shift_rows, -shift_cols), axis=(0, 1)).astype(jnp.int32)
    lat_flag = (jnp.arange(NLAT) + shift_rows >= NLAT).astype(jnp.int32)
    lev_flag = (jnp.arange(LEV) + shift_levels >= LEV).astype(jnp.int32)
    region = labels[None] + 4 * lat_flag[None, :, None] + 8 * lev_flag[:, None, None]
    bands = NLAT // WH
    tiles = shifted.reshape(LEV, bands, WH, NLON, D).transpose(1, 0, 2, 3, 4)
    band_labels = region.reshape(LEV, bands, WH, NLON).transpose(1, 0, 2, 3)
    mixed = lax.map(lambda band_pair: window_attention(band_pair[0], band_pair[1], w_qkv, w_out), (tiles, band_labels))
    mixed = mixed.transpose(1, 0, 2, 3, 4).reshape(LEV, NLAT, NLON, D)
    mixed = jnp.roll(mixed, (shift_levels, shift_rows, shift_cols), axis=(0, 1, 2))
    blocks = mixed.reshape(LEV, bands, WH * NLON, D).transpose(1, 0, 2, 3)
    cotangents = field_cotangent.reshape(bands, WH * NLON, PLEV * OUTS)
    zero_sums = (jnp.zeros((D, 2 * D), jnp.float32), jnp.zeros((PLEV, D), jnp.float32), jnp.zeros((D, D), jnp.float32), jnp.zeros((D, OUTS), jnp.float32))

    def scan_step(running, band_pair):
        fields, grad_kv, grad_query, grad_out, grad_head = decode_block(band_pair[0], band_pair[1], w_kv, level_queries, w_o, w_head)
        return ((running[0] + grad_kv, running[1] + grad_query, running[2] + grad_out, running[3] + grad_head), fields)
    totals, fields = lax.scan(scan_step, zero_sums, (blocks, cotangents))
    decoded = fields.reshape(NLAT, NLON, PLEV * OUTS)
    squares = jnp.sum(totals[0] * totals[0]) + jnp.sum(totals[1] * totals[1]) + jnp.sum(totals[2] * totals[2]) + jnp.sum(totals[3] * totals[3])
    entries = D * 2 * D + PLEV * D + D * D + D * OUTS
    factor = jnp.minimum(1.0, math.sqrt(entries) * lax.rsqrt(squares + clip_eps))
    return (mixed, decoded, totals[0] * factor, totals[1] * factor, totals[2] * factor, totals[3] * factor)
```

```python
import math

import jax
import jax.numpy as jnp
import numpy as np
from jax import lax
from jax.experimental import pallas as pl
from jax.experimental.pallas import tpu as pltpu
from jax.sharding import PartitionSpec as P

D = 512
HEADS = 8
LEV = 4
PLEV = 13
OUTS = 80
WL = 2
WH = 6
WW = 12
PATCHES = WH * 2 * WW
TOKENS = LEV * PATCHES
MAIN = 224
SIDE = 80
PACKED = 2 * MAIN + 2 * SIDE
ROWS = 768
LANES = 128

norm_eps = 1e-05
clip_eps = 1e-06
BF = jnp.bfloat16
F32 = jnp.float32


def window_order():
    level_pairs = ((1, 2), (3, 0))

    def rows_of(levels, rows, cols):
        return [(l * WH + r) * 2 * WW + c for l in levels for r in rows for c in cols]

    order = []
    for rows in ((3, 4, 5), (0, 1, 2)):
        for pair in level_pairs:
            order += rows_of(pair, rows, range(6, 18))
        for pair in level_pairs:
            order += rows_of(pair, rows, range(18, 24)) + [-1] * 4
    for rows in ((3, 4, 5), (0, 1, 2)):
        for pair in level_pairs:
            order += rows_of(pair, rows, range(0, 6)) + [-1] * 4
    return np.array(order)


def pack_matrix():
    order = window_order()
    return (order[:, None] == np.arange(TOKENS)[None, :]).astype(np.float32)


def dot(a, b, contract):
    return lax.dot_general(a, b, (contract, ((), ())), preferred_element_type=F32)


def mm(a, b):
    return dot(a, b, ((1,), (0,)))


def layer_norm(wide):
    center = wide - jnp.mean(wide, axis=-1, keepdims=True)
    spread = jnp.mean(center * center, axis=-1, keepdims=True)
    return (center * lax.rsqrt(spread + norm_eps)).astype(BF)


def pack_kernel(x_ref, perm_ref, main_ref, north_ref, west_ref, corner_ref):
    x = x_ref[...]
    north_ref[...] = mm(perm_ref[MAIN : 2 * MAIN], x).astype(BF)
    west_ref[...] = mm(perm_ref[2 * MAIN : 2 * MAIN + SIDE], x).astype(BF)
    corner_ref[...] = mm(perm_ref[2 * MAIN + SIDE :], x).astype(BF)
    main_ref[...] = mm(perm_ref[:MAIN], x).astype(BF)


def attention_kernel(
    main_ref, north_ref, west_ref, corner_ref, row_ref, col_ref, wqkv_ref, wout_ref,
    main_out, north_out, west_out, corner_out, proj, context,
):
    pieces = (main_ref, north_ref, west_ref, corner_ref)
    wide = jnp.concatenate([ref[...].astype(F32) for ref in pieces], axis=0)
    proj[...] = mm(layer_norm(wide), wqkv_ref[...])
    n, w, c = MAIN, 2 * MAIN, 2 * MAIN + SIDE
    windows = (
        (0, 144, ((0, 72), (n, 72))),
        (1, 144, ((72, 72), (n + 72, 72))),
        (2, 160, ((144, 40), (n + 144, 40), (w, 40), (c, 40))),
        (3, 160, ((184, 40), (n + 184, 40), (w + 40, 40), (c + 40, 40))),
    )
    low = lax.broadcasted_iota(jnp.int32, (1, LANES), 1) < D // HEADS
    for index, size, parts in windows:
        allowed = col_ref[:size, index : index + 1] == row_ref[index : index + 1, :size]
        bias = jnp.where(allowed, 0.0, -jnp.inf)
        bias = jnp.concatenate([bias, bias], axis=0)

        def take(start):
            return jnp.concatenate([proj[at : at + count, start : start + LANES] for at, count in parts], axis=0)

        for pair in range(HEADS // 2):
            lane = pair * LANES
            query = take(lane).astype(BF).astype(F32) * 0.125
            key = take(D + lane).astype(BF)
            value = take(2 * D + lane).astype(BF)
            both = jnp.concatenate([jnp.where(low, query, 0.0), jnp.where(low, 0.0, query)], axis=0).astype(BF)
            scores = dot(both, key, ((1,), (1,))) + bias
            weights = jnp.exp(scores - jnp.max(scores, axis=-1, keepdims=True))
            scale = 1.0 / jnp.sum(weights, axis=-1, keepdims=True)
            mixed = mm(weights.astype(BF), value) * scale
            result = jnp.where(low, mixed[:size], mixed[size:])
            start = 0
            for at, count in parts:
                context[at : at + count, lane : lane + LANES] = result[start : start + count]
                start += count
    mixed = wide + mm(context[...].astype(BF), wout_ref[...])
    mixed = mixed.astype(BF)
    main_out[...] = mixed[:n]
    north_out[...] = mixed[n:w]
    west_out[...] = mixed[w:c]
    corner_out[...] = mixed[c:]


def expand_matrix(level):
    c = lax.broadcasted_iota(jnp.int32, (LANES, D), 0)
    j = lax.broadcasted_iota(jnp.int32, (LANES, D), 1)
    return (c == level * HEADS + j // (D // HEADS)).astype(F32).astype(BF)


def shift_matrix(offset, width):
    i = lax.broadcasted_iota(jnp.int32, (width, LANES), 0)
    j = lax.broadcasted_iota(jnp.int32, (width, LANES), 1)
    return ((i - offset == j) & (j < OUTS)).astype(F32).astype(BF)


def spot(level):
    first = level * OUTS // LANES * LANES
    return first, level * OUTS - first, min(2 * LANES, PLEV * OUTS - first)


def spread_queries(queries):
    parts = [jnp.broadcast_to(queries[a : a + 1], (HEADS, D)) for a in range(PLEV)]
    parts.append(jnp.zeros((LANES - HEADS * PLEV, D), F32))
    tall = jnp.concatenate(parts, axis=0)
    c = lax.broadcasted_iota(jnp.int32, (LANES, D), 0)
    j = lax.broadcasted_iota(jnp.int32, (LANES, D), 1)
    return jnp.where(c % HEADS == j // (D // HEADS), tall, 0.0)


def pre_kernel(cot_ref, queries_ref, wo_ref, whead_ref, up_ref, dctx_ref, map_ref, base_ref):
    head = whead_ref[...]
    both = mm(wo_ref[...], head).astype(BF)
    map_ref[...] = both
    base_ref[...] = jnp.concatenate(
        [mm(queries_ref[...], head), jnp.zeros((16 - PLEV, LANES), F32)], axis=0
    )
    for level in range(PLEV):
        first, offset, width = spot(level)
        up = mm(cot_ref[:, first : first + width], shift_matrix(offset, width)).astype(BF)
        up_ref[level] = up
        dctx_ref[level] = dot(up, both, ((1,), (1,))).astype(BF)


def decode_kernel(
    main_ref, north_ref, west_ref, corner_ref, perm_ref, wkv_ref, queries_ref, up_ref, dctx_ref, map_ref, base_ref,
    owned_ref, fields_ref, sums_ref,
    pair, weights, dweights, dvalues, context, fields,
):
    pieces = (main_ref, north_ref, west_ref, corner_ref)
    packed = jnp.concatenate([ref[...] for ref in pieces], axis=0)
    wide = dot(perm_ref[...], packed, ((0,), (0,)))
    owned_ref[...] = wide.astype(BF)
    normed = layer_norm(wide)
    pair[...] = mm(normed, wkv_ref[...]).astype(BF).astype(F32)
    queries = spread_queries(queries_ref[...].astype(F32)).astype(BF)
    scores = dot(pair[:, :D].astype(BF), queries, ((1,), (1,))) * 0.125
    slabs = [scores[l * PATCHES : (l + 1) * PATCHES] for l in range(LEV)]
    top = jnp.maximum(jnp.maximum(slabs[0], slabs[1]), jnp.maximum(slabs[2], slabs[3]))
    slabs = [jnp.exp(s - top) for s in slabs]
    scale = 1.0 / (slabs[0] + slabs[1] + slabs[2] + slabs[3])
    for l in range(LEV):
        weights[l * PATCHES : (l + 1) * PATCHES] = slabs[l] * scale
    dweights[...] = jnp.zeros_like(dweights)
    dvalues[...] = jnp.zeros_like(dvalues)
    fields[...] = jnp.zeros_like(fields)
    narrow = weights[...].astype(BF)
    for level in range(PLEV):
        expand = expand_matrix(level)
        spread = mm(narrow, expand)
        upstream = dctx_ref[level].astype(F32)
        total = jnp.zeros((PATCHES, D), F32)
        for l in range(LEV):
            at = slice(l * PATCHES, (l + 1) * PATCHES)
            value = pair[at, D:]
            part = spread[at]
            total += part * value
            dvalues[at] += part * upstream
            dweights[at] += dot((upstream * value).astype(BF), expand, ((1,), (1,)))
        total = total.astype(BF)
        context[level * PATCHES : (level + 1) * PATCHES] = total
        first, offset, width = spot(level)
        decoded = (mm(total, map_ref[...]) + base_ref[level : level + 1]).astype(BF)
        fields[:, first : first + width] += dot(decoded, shift_matrix(offset, width), ((1,), (1,)))
    fields_ref[...] = fields[...].astype(BF)
    parts = [weights[l * PATCHES : (l + 1) * PATCHES] for l in range(LEV)]
    slopes = [dweights[l * PATCHES : (l + 1) * PATCHES] for l in range(LEV)]
    mean = sum(p * d for p, d in zip(parts, slopes))
    dscores = jnp.concatenate([p * (d - mean) * 0.125 for p, d in zip(parts, slopes)], axis=0).astype(BF)
    sums_ref[:D] = dot(normed, dvalues[...].astype(BF), ((0,), (0,))).astype(BF)
    sums_ref[D : D + LANES] = dot(dscores, normed, ((0,), (0,))).astype(BF)
    up = jnp.concatenate([up_ref[a] for a in range(PLEV)], axis=0)
    outer = dot(up, context[...], ((0,), (0,)))
    sums_ref[D + LANES : D + LANES + OUTS] = outer[:OUTS].astype(BF)
    totals = [jnp.sum(up_ref[a].astype(F32), axis=0, keepdims=True) for a in range(PLEV)]
    totals.append(jnp.zeros((LANES - OUTS - PLEV, LANES), F32))
    totals = jnp.concatenate(totals, axis=0)
    totals = jnp.concatenate([totals, jnp.zeros((LANES - OUTS, D - LANES), F32)], axis=1)
    sums_ref[D + LANES + OUTS :] = totals.astype(BF)


def final_kernel(gathered_ref, order_ref, wkv_ref, queries_ref, wo_ref, whead_ref, kv_ref, query_ref, o_ref, head_ref):
    sums = mm(order_ref[...], gathered_ref[...]).astype(BF)
    queries = queries_ref[...]
    head = whead_ref[...]
    keyed = sums[D : D + LANES]
    outer = sums[D + LANES :]
    level_sums = outer[OUTS : OUTS + 16, :LANES]
    spread = spread_queries(queries.astype(F32)).astype(BF)
    values = sums[:D].astype(F32)
    keys = dot(keyed, spread, ((0,), (0,)))
    c = lax.broadcasted_iota(jnp.int32, (LANES, D), 0)
    j = lax.broadcasted_iota(jnp.int32, (LANES, D), 1)
    grouped = jnp.where(c % HEADS == j // (D // HEADS), mm(keyed, wkv_ref[:, :D]), 0.0)
    grouped = jnp.sum(grouped.reshape(LANES // HEADS, HEADS, D), axis=1)
    level = grouped[:PLEV] + dot(level_sums, head, ((1,), (1,)))[:PLEV]
    clean = outer[:OUTS]
    out = dot(clean, head[:, :OUTS], ((0,), (1,)))
    pixels = dot(wo_ref[...], clean, ((0,), (1,)))
    pixels = pixels + dot(queries, level_sums[:PLEV, :OUTS], ((0,), (0,)))
    squares = jnp.sum(values * values) + jnp.sum(keys * keys) + jnp.sum(level * level)
    squares = squares + jnp.sum(out * out) + jnp.sum(pixels * pixels)
    limit = math.sqrt(2 * D * D + PLEV * D + D * D + D * OUTS)
    factor = jnp.minimum(1.0, limit * lax.rsqrt(jnp.full((1, 1), squares + clip_eps, F32)))
    kv_ref[:, :D] = keys * factor
    kv_ref[:, D:] = values * factor
    query_ref[...] = level * factor
    o_ref[...] = out * factor
    head_ref[...] = pixels * factor


def call(kernel, outs, scratch=()):
    return pl.pallas_call(
        kernel,
        out_shape=outs,
        scratch_shapes=list(scratch),
        compiler_params=pltpu.CompilerParams(vmem_limit_bytes=56 * 2**20),
    )


def struct(shape, dtype=BF):
    return jax.ShapeDtypeStruct(shape, dtype)


def move(array, lat_step, lon_step):
    lats, lons = lax.axis_size("lat"), lax.axis_size("lon")
    route = [
        (i * lons + j, (i + lat_step) % lats * lons + (j + lon_step) % lons)
        for i in range(lats)
        for j in range(lons)
    ]
    return lax.ppermute(array, ("lat", "lon"), route)


def sum_over_all(packed):
    rows, width = packed.shape
    lats, lons = lax.axis_size("lat"), lax.axis_size("lon")
    part = rows // lons
    chunks = lax.all_to_all(packed.reshape(lons, part, width), "lon", 0, 0, tiled=True)
    mine = jnp.sum(chunks.astype(F32), axis=0).astype(BF)
    chunks = lax.all_to_all(mine.reshape(lats, part // lats, width), "lat", 0, 0, tiled=True)
    mine = jnp.sum(chunks.astype(F32), axis=0).astype(BF)
    return lax.all_gather(mine, ("lat", "lon")).reshape(rows, width)


def gathered_order():
    lats, lons = lax.axis_size("lat"), lax.axis_size("lon")
    count = ROWS // lats // lons
    row = np.arange(ROWS)
    lon, lat, at = row // (lats * count), row // count % lats, row % count
    return ((lat * lons + lon) * count + at)[:, None] == row[None, :]


def window_labels(own, north, west, corner):
    lat_flag = jnp.where(lax.axis_index("lat") == lax.axis_size("lat") - 1, 4, 0)
    own, west = own.astype(jnp.int32), west.astype(jnp.int32)
    north, corner = north.astype(jnp.int32) + lat_flag, corner.astype(jnp.int32) + lat_flag

    def flat(block, jump, pad):
        block = block.reshape(-1)
        return jnp.concatenate([block, block + jump, jnp.full((pad,), -1, jnp.int32)])

    rows = []
    for jump in (0, 8):
        pieces = [flat(own[:, :WW], jump, 0), flat(north[:, :WW], jump, 0), jnp.full((16,), -1, jnp.int32)]
        rows.append(jnp.concatenate(pieces))
    for jump in (0, 8):
        pieces = (own[:, WW:], north[:, WW:], west, corner)
        rows.append(jnp.concatenate([flat(piece, jump, 4) for piece in pieces]))
    return jnp.stack(rows)


def per_device(latents, mask_ids, w_qkv, w_out, w_kv, level_queries, w_o, w_head, field_cotangent):
    perm = jnp.asarray(pack_matrix(), BF)
    shapes = [struct((MAIN, D)), struct((MAIN, D)), struct((SIDE, D)), struct((SIDE, D))]
    main, north, west, corner = call(pack_kernel, shapes)(latents.reshape(TOKENS, D), perm)
    north, west, corner = move(north, -1, 0), move(west, 0, -1), move(corner, -1, -1)
    labels = window_labels(
        mask_ids[3:, 6:],
        move(mask_ids[:3, 6:], -1, 0),
        move(mask_ids[3:, :6], 0, -1),
        move(mask_ids[:3, :6], -1, -1),
    )
    head = jnp.pad(w_head, ((0, 0), (0, LANES - OUTS)))
    up, dctx, both, base = call(
        pre_kernel,
        [
            struct((PLEV, PATCHES, LANES)),
            struct((PLEV, PATCHES, D)),
            struct((D, LANES)),
            struct((16, LANES), F32),
        ],
    )(field_cotangent.reshape(PATCHES, PLEV * OUTS), level_queries, w_o, head)
    main, north, west, corner = call(
        attention_kernel,
        shapes,
        [pltpu.VMEM((PACKED, 3 * D), F32), pltpu.VMEM((PACKED, D), F32)],
    )(main, north, west, corner, labels, labels.T, w_qkv, w_out)
    north, west, corner = move(north, 1, 0), move(west, 0, 1), move(corner, 1, 1)
    owned, fields, sums = call(
        decode_kernel,
        [struct((TOKENS, D)), struct((PATCHES, PLEV * OUTS)), struct((ROWS, D))],
        [
            pltpu.VMEM((TOKENS, 2 * D), F32),
            pltpu.VMEM((TOKENS, LANES), F32),
            pltpu.VMEM((TOKENS, LANES), F32),
            pltpu.VMEM((TOKENS, D), F32),
            pltpu.VMEM((PLEV * PATCHES, D), BF),
            pltpu.VMEM((PATCHES, PLEV * OUTS), F32),
        ],
    )(main, north, west, corner, perm, w_kv, level_queries, up, dctx, both, base)
    sums = sum_over_all(sums)
    grads = call(
        final_kernel,
        [struct((D, 2 * D), F32), struct((PLEV, D), F32), struct((D, D), F32), struct((D, OUTS), F32)],
    )(sums, jnp.asarray(gathered_order(), BF), w_kv, level_queries, w_o, head)
    shape = latents.shape
    return (owned.reshape(shape), fields.reshape(shape[1], shape[2], PLEV * OUTS), *grads)


def solution(mesh):
    in_specs = (
        P(None, "lat", "lon", None),
        P("lat", "lon"),
        P(),
        P(),
        P(),
        P(),
        P(),
        P(),
        P("lat", "lon", None),
    )
    out_specs = (P(None, "lat", "lon", None), P("lat", "lon", None), P(), P(), P(), P())
    return jax.shard_map(per_device, mesh=mesh, in_specs=in_specs, out_specs=out_specs, check_vma=False)
```

```python
import math

import jax
import jax.numpy as jnp
import numpy as np
from jax import lax
from jax.experimental import pallas as pl
from jax.experimental.pallas import tpu as pltpu
from jax.sharding import PartitionSpec as P

D = 512
HEADS = 8
LEV = 4
PLEV = 13
OUTS = 80
WL = 2
WH = 6
WW = 12
PATCHES = WH * 2 * WW
TOKENS = LEV * PATCHES
MAIN = 224
SIDE = 80
PACKED = 2 * MAIN + 2 * SIDE
ROWS = 768
LANES = 128

SPAN = 256
PIECES = (
    {0: (0, 72, 0), 1: (72, 72, 0), 2: (144, 40, 0), 3: (184, 40, 0)},
    {0: (224, 72, 72), 1: (296, 72, 72), 2: (368, 40, 40), 3: (408, 40, 40)},
    {2: (448, 40, 80), 3: (488, 40, 80)},
    {2: (528, 40, 120), 3: (568, 40, 120)},
)

norm_eps = 1e-05
clip_eps = 1e-06
BF = jnp.bfloat16
F32 = jnp.float32


def window_order():
    level_pairs = ((1, 2), (3, 0))

    def rows_of(levels, rows, cols):
        return [(l * WH + r) * 2 * WW + c for l in levels for r in rows for c in cols]

    order = []
    for rows in ((3, 4, 5), (0, 1, 2)):
        for pair in level_pairs:
            order += rows_of(pair, rows, range(6, 18))
        for pair in level_pairs:
            order += rows_of(pair, rows, range(18, 24)) + [-1] * 4
    for rows in ((3, 4, 5), (0, 1, 2)):
        for pair in level_pairs:
            order += rows_of(pair, rows, range(0, 6)) + [-1] * 4
    return np.array(order)


def pack_matrix():
    order = window_order()
    return (order[:, None] == np.arange(TOKENS)[None, :]).astype(np.float32)


def label_tables():
    order = window_order()
    row, col, level = order // (2 * WW) % WH, order % (2 * WW), order // PATCHES
    columns = np.zeros((2 * WW, 12 * SPAN), np.float32)
    rows = np.zeros((8, 12 * SPAN), np.float32)
    extra = np.zeros((8, SPAN), np.float32)
    segment = 0
    for starts, far in zip(PIECES, (False, True, False, True)):
        for window, (at, count, place) in starts.items():
            for i in range(count):
                lane, token = place + i, at + i
                if order[token] < 0:
                    extra[window, lane] = -1
                    continue
                columns[col[token], segment * SPAN + lane] = 1
                rows[row[token], segment * SPAN + lane] = 1
                extra[window, lane] = 8 * (level[token] == 0)
                extra[4 + window, lane] = 4 * far
            segment += 1
    return columns, rows, extra


def dot(a, b, contract):
    return lax.dot_general(a, b, (contract, ((), ())), preferred_element_type=F32)


def mm(a, b):
    return dot(a, b, ((1,), (0,)))


def layer_norm(wide):
    center = wide - jnp.mean(wide, axis=-1, keepdims=True)
    spread = jnp.mean(center * center, axis=-1, keepdims=True)
    return (center * lax.rsqrt(spread + norm_eps)).astype(BF)


def pack_kernel(x_ref, ids_ref, perm_ref, columns_ref, rows_ref, main_ref, north_ref, west_ref, corner_ref):
    ids = ids_ref[...].astype(F32).astype(BF)
    lines = jnp.sum(mm(ids, columns_ref[...]) * rows_ref[:WH], axis=0, keepdims=True)
    x = x_ref[...]
    segment = 0
    for ref, windows in zip((main_ref, north_ref, west_ref, corner_ref), PIECES):
        height = ref.shape[0]
        first = min(at for at, _, _ in windows.values())
        packed = mm(perm_ref[first : first + height], x)
        bottom = [jnp.zeros((12, SPAN), F32)]
        for window in range(4):
            if window in windows:
                bottom.append(lines[:, segment * SPAN : (segment + 1) * SPAN])
                segment += 1
            else:
                bottom.append(jnp.zeros((1, SPAN), F32))
        bottom = jnp.concatenate(bottom, axis=0)
        bottom = jnp.concatenate([bottom, jnp.zeros((16, D - SPAN), F32)], axis=1)
        ref[: height - 16] = packed[: height - 16].astype(BF)
        ref[height - 16 :] = (packed[height - 16 :] + bottom).astype(BF)


def attention_kernel(
    flag_ref, main_ref, north_ref, west_ref, corner_ref, extra_ref, wqkv_ref, wout_ref,
    main_out, north_out, west_out, corner_out, proj, context,
):
    pieces = (main_ref, north_ref, west_ref, corner_ref)
    wide = jnp.concatenate([ref[...].astype(F32) for ref in pieces], axis=0)
    proj[...] = mm(layer_norm(wide), wqkv_ref[...])
    lines = sum(ref[ref.shape[0] - 16 :, :SPAN].astype(F32) for ref in pieces)[12:]
    lines = lines + extra_ref[:4] + jnp.where(flag_ref[0, 0] > 0, extra_ref[4:], 0.0)
    lines = jnp.concatenate([lines, lines], axis=0)
    i = lax.broadcasted_iota(jnp.int32, (SPAN, SPAN), 0)
    j = lax.broadcasted_iota(jnp.int32, (SPAN, SPAN), 1)
    standing = dot((i == j).astype(F32).astype(BF), lines.astype(BF), ((1,), (1,)))
    n, w, c = MAIN, 2 * MAIN, 2 * MAIN + SIDE
    windows = (
        (0, 144, ((0, 72), (n, 72))),
        (1, 144, ((72, 72), (n + 72, 72))),
        (2, 160, ((144, 40), (n + 144, 40), (w, 40), (c, 40))),
        (3, 160, ((184, 40), (n + 184, 40), (w + 40, 40), (c + 40, 40))),
    )
    low = lax.broadcasted_iota(jnp.int32, (1, LANES), 1) < D // HEADS
    for index, size, parts in windows:
        allowed = standing[:size, index : index + 1] == lines[index : index + 1, :size]
        bias = jnp.where(allowed, 0.0, -jnp.inf)
        bias = jnp.concatenate([bias, bias], axis=0)

        def take(start):
            return jnp.concatenate([proj[at : at + count, start : start + LANES] for at, count in parts], axis=0)

        for pair in range(HEADS // 2):
            lane = pair * LANES
            query = take(lane).astype(BF).astype(F32) * 0.125
            key = take(D + lane).astype(BF)
            value = take(2 * D + lane).astype(BF)
            both = jnp.concatenate([jnp.where(low, query, 0.0), jnp.where(low, 0.0, query)], axis=0).astype(BF)
            scores = dot(both, key, ((1,), (1,))) + bias
            weights = jnp.exp(scores - jnp.max(scores, axis=-1, keepdims=True))
            scale = 1.0 / jnp.sum(weights, axis=-1, keepdims=True)
            mixed = mm(weights.astype(BF), value) * scale
            result = jnp.where(low, mixed[:size], mixed[size:])
            start = 0
            for at, count in parts:
                context[at : at + count, lane : lane + LANES] = result[start : start + count]
                start += count
    mixed = wide + mm(context[...].astype(BF), wout_ref[...])
    mixed = mixed.astype(BF)
    main_out[...] = mixed[:n]
    north_out[...] = mixed[n:w]
    west_out[...] = mixed[w:c]
    corner_out[...] = mixed[c:]


def expand_matrix(level):
    c = lax.broadcasted_iota(jnp.int32, (LANES, D), 0)
    j = lax.broadcasted_iota(jnp.int32, (LANES, D), 1)
    return (c == level * HEADS + j // (D // HEADS)).astype(F32).astype(BF)


def shift_matrix(offset, width):
    i = lax.broadcasted_iota(jnp.int32, (width, LANES), 0)
    j = lax.broadcasted_iota(jnp.int32, (width, LANES), 1)
    return ((i - offset == j) & (j < OUTS)).astype(F32).astype(BF)


def spot(level):
    first = level * OUTS // LANES * LANES
    return first, level * OUTS - first, min(2 * LANES, PLEV * OUTS - first)


def spread_queries(queries):
    parts = [jnp.broadcast_to(queries[a : a + 1], (HEADS, D)) for a in range(PLEV)]
    parts.append(jnp.zeros((LANES - HEADS * PLEV, D), F32))
    tall = jnp.concatenate(parts, axis=0)
    c = lax.broadcasted_iota(jnp.int32, (LANES, D), 0)
    j = lax.broadcasted_iota(jnp.int32, (LANES, D), 1)
    return jnp.where(c % HEADS == j // (D // HEADS), tall, 0.0)


def pre_kernel(cot_ref, queries_ref, wo_ref, whead_ref, up_ref, dctx_ref, map_ref, base_ref):
    head = whead_ref[...]
    both = dot(wo_ref[...], head, ((1,), (1,))).astype(BF)
    map_ref[...] = both
    base_ref[...] = jnp.concatenate(
        [dot(queries_ref[...], head, ((1,), (1,))), jnp.zeros((16 - PLEV, LANES), F32)], axis=0
    )
    for level in range(PLEV):
        first, offset, width = spot(level)
        up = mm(cot_ref[:, first : first + width], shift_matrix(offset, width)).astype(BF)
        up_ref[level] = up
        dctx_ref[level] = dot(up, both, ((1,), (1,))).astype(BF)


def decode_kernel(
    main_ref, north_ref, west_ref, corner_ref, perm_ref, wkv_ref, queries_ref, up_ref, dctx_ref, map_ref, base_ref,
    owned_ref, fields_ref, sums_ref,
    pair, weights, dweights, dvalues, context, fields,
):
    pieces = (main_ref, north_ref, west_ref, corner_ref)
    packed = jnp.concatenate([ref[...] for ref in pieces], axis=0)
    wide = dot(perm_ref[...], packed, ((0,), (0,)))
    owned_ref[...] = wide.astype(BF)
    normed = layer_norm(wide)
    pair[...] = mm(normed, wkv_ref[...]).astype(BF).astype(F32)
    queries = spread_queries(queries_ref[...].astype(F32)).astype(BF)
    scores = dot(pair[:, :D].astype(BF), queries, ((1,), (1,))) * 0.125
    slabs = [scores[l * PATCHES : (l + 1) * PATCHES] for l in range(LEV)]
    top = jnp.maximum(jnp.maximum(slabs[0], slabs[1]), jnp.maximum(slabs[2], slabs[3]))
    slabs = [jnp.exp(s - top) for s in slabs]
    scale = 1.0 / (slabs[0] + slabs[1] + slabs[2] + slabs[3])
    for l in range(LEV):
        weights[l * PATCHES : (l + 1) * PATCHES] = slabs[l] * scale
    dweights[...] = jnp.zeros_like(dweights)
    dvalues[...] = jnp.zeros_like(dvalues)
    fields[...] = jnp.zeros_like(fields)
    narrow = weights[...].astype(BF)
    for level in range(PLEV):
        expand = expand_matrix(level)
        spread = mm(narrow, expand)
        upstream = dctx_ref[level].astype(F32)
        total = jnp.zeros((PATCHES, D), F32)
        for l in range(LEV):
            at = slice(l * PATCHES, (l + 1) * PATCHES)
            value = pair[at, D:]
            part = spread[at]
            total += part * value
            dvalues[at] += part * upstream
            dweights[at] += dot((upstream * value).astype(BF), expand, ((1,), (1,)))
        total = total.astype(BF)
        context[level * PATCHES : (level + 1) * PATCHES] = total
        first, offset, width = spot(level)
        decoded = (mm(total, map_ref[...]) + base_ref[level : level + 1]).astype(BF)
        fields[:, first : first + width] += dot(decoded, shift_matrix(offset, width), ((1,), (1,)))
    fields_ref[...] = fields[...].astype(BF)
    parts = [weights[l * PATCHES : (l + 1) * PATCHES] for l in range(LEV)]
    slopes = [dweights[l * PATCHES : (l + 1) * PATCHES] for l in range(LEV)]
    mean = sum(p * d for p, d in zip(parts, slopes))
    dscores = jnp.concatenate([p * (d - mean) * 0.125 for p, d in zip(parts, slopes)], axis=0).astype(BF)
    sums_ref[:D] = dot(normed, dvalues[...].astype(BF), ((0,), (0,))).astype(BF)
    sums_ref[D : D + LANES] = dot(dscores, normed, ((0,), (0,))).astype(BF)
    up = jnp.concatenate([up_ref[a] for a in range(PLEV)], axis=0)
    outer = dot(up, context[...], ((0,), (0,)))
    sums_ref[D + LANES : D + LANES + OUTS] = outer[:OUTS].astype(BF)
    totals = [jnp.sum(up_ref[a].astype(F32), axis=0, keepdims=True) for a in range(PLEV)]
    totals.append(jnp.zeros((LANES - OUTS - PLEV, LANES), F32))
    totals = jnp.concatenate(totals, axis=0)
    totals = jnp.concatenate([totals, jnp.zeros((LANES - OUTS, D - LANES), F32)], axis=1)
    sums_ref[D + LANES + OUTS :] = totals.astype(BF)


def final_kernel(sums_ref, wkv_ref, queries_ref, wo_ref, whead_ref, kv_ref, query_ref, o_ref, head_ref):
    sums = sums_ref[...]
    queries = queries_ref[...]
    head = whead_ref[...]
    keyed = sums[D : D + LANES]
    outer = sums[D + LANES :]
    level_sums = outer[OUTS : OUTS + 16, :LANES]
    spread = spread_queries(queries.astype(F32)).astype(BF)
    values = sums[:D].astype(F32)
    keys = dot(keyed, spread, ((0,), (0,)))
    c = lax.broadcasted_iota(jnp.int32, (LANES, D), 0)
    j = lax.broadcasted_iota(jnp.int32, (LANES, D), 1)
    grouped = jnp.where(c % HEADS == j // (D // HEADS), mm(keyed, wkv_ref[:, :D]), 0.0)
    grouped = jnp.sum(grouped.reshape(LANES // HEADS, HEADS, D), axis=1)
    level = grouped[:PLEV] + mm(level_sums, head)[:PLEV]
    clean = outer[:OUTS]
    out = dot(clean, head[:OUTS], ((0,), (0,)))
    pixels = mm(clean, wo_ref[...])
    pixels = pixels + dot(level_sums[:PLEV, :OUTS], queries, ((0,), (0,)))
    squares = jnp.sum(values * values) + jnp.sum(keys * keys) + jnp.sum(level * level)
    squares = squares + jnp.sum(out * out) + jnp.sum(pixels * pixels)
    limit = math.sqrt(2 * D * D + PLEV * D + D * D + D * OUTS)
    factor = jnp.minimum(1.0, limit * lax.rsqrt(jnp.full((1, 1), squares + clip_eps, F32)))
    kv_ref[:, :D] = keys * factor
    kv_ref[:, D:] = values * factor
    query_ref[...] = level * factor
    o_ref[...] = out * factor
    head_ref[...] = pixels * factor


def call(kernel, outs, scratch=(), smem=False):
    more = {}
    if smem:
        whole = pl.BlockSpec(memory_space=pltpu.VMEM)
        more["in_specs"] = [pl.BlockSpec(memory_space=pltpu.SMEM)] + [whole] * 7
    return pl.pallas_call(
        kernel,
        **more,
        out_shape=outs,
        scratch_shapes=list(scratch),
        compiler_params=pltpu.CompilerParams(vmem_limit_bytes=56 * 2**20),
    )


def struct(shape, dtype=BF):
    return jax.ShapeDtypeStruct(shape, dtype)


def move(array, lat_step, lon_step):
    lats, lons = lax.axis_size("lat"), lax.axis_size("lon")
    route = [
        (i * lons + j, (i + lat_step) % lats * lons + (j + lon_step) % lons)
        for i in range(lats)
        for j in range(lons)
    ]
    return lax.ppermute(array, ("lat", "lon"), route)


def lat_groups(count, stride):
    lats = lax.axis_size("lat")
    return [
        [first + stride * i for i in range(count)]
        for first in range(lats)
        if first // stride % count == 0
    ]


def sum_over_lat(mine):
    lats = lax.axis_size("lat")
    low = min(4, lats)
    high = lats // low
    copies = jnp.broadcast_to(mine[None], (low,) + mine.shape)
    copies = lax.all_to_all(copies, "lat", 0, 0, axis_index_groups=lat_groups(low, 1), tiled=True)
    mine = jnp.sum(copies.astype(F32), axis=0).astype(BF)
    others = [move(mine, low * step, 0) for step in range(1, high)]
    return sum((other.astype(F32) for other in others), mine.astype(F32)).astype(BF)


def sum_over_all(packed):
    rows, width = packed.shape
    lons = lax.axis_size("lon")
    part = rows // lons
    chunks = lax.all_to_all(packed.reshape(lons, part, width), "lon", 0, 0, tiled=True)
    mine = sum_over_lat(jnp.sum(chunks.astype(F32), axis=0).astype(BF))
    copies = jnp.broadcast_to(mine[None], (lons, part, width))
    return lax.all_to_all(copies, "lon", 0, 0, tiled=True).reshape(rows, width)


def per_device(latents, mask_ids, w_qkv, w_out, w_kv, level_queries, w_o, w_head, field_cotangent):
    perm = jnp.asarray(pack_matrix(), BF)
    columns, rows, extra = label_tables()
    flag = (lax.axis_index("lat") == lax.axis_size("lat") - 1).astype(jnp.int32).reshape(1, 1)
    shapes = [struct((MAIN, D)), struct((MAIN, D)), struct((SIDE, D)), struct((SIDE, D))]
    main, north, west, corner = call(pack_kernel, shapes)(
        latents.reshape(TOKENS, D), mask_ids, perm, jnp.asarray(columns, BF), jnp.asarray(rows)
    )
    north, west, corner = move(north, -1, 0), move(west, 0, -1), move(corner, -1, -1)
    head = jnp.pad(w_head.T, ((0, LANES - OUTS), (0, 0)))
    up, dctx, both, base = call(
        pre_kernel,
        [
            struct((PLEV, PATCHES, LANES)),
            struct((PLEV, PATCHES, D)),
            struct((D, LANES)),
            struct((16, LANES), F32),
        ],
    )(field_cotangent.reshape(PATCHES, PLEV * OUTS), level_queries, w_o, head)
    main, north, west, corner = call(
        attention_kernel,
        shapes,
        [pltpu.VMEM((PACKED, 3 * D), F32), pltpu.VMEM((PACKED, D), F32)],
        smem=True,
    )(flag, main, north, west, corner, jnp.asarray(extra), w_qkv, w_out)
    north, west, corner = move(north, 1, 0), move(west, 0, 1), move(corner, 1, 1)
    owned, fields, sums = call(
        decode_kernel,
        [struct((TOKENS, D)), struct((PATCHES, PLEV * OUTS)), struct((ROWS, D))],
        [
            pltpu.VMEM((TOKENS, 2 * D), F32),
            pltpu.VMEM((TOKENS, LANES), F32),
            pltpu.VMEM((TOKENS, LANES), F32),
            pltpu.VMEM((TOKENS, D), F32),
            pltpu.VMEM((PLEV * PATCHES, D), BF),
            pltpu.VMEM((PATCHES, PLEV * OUTS), F32),
        ],
    )(main, north, west, corner, perm, w_kv, level_queries, up, dctx, both, base)
    sums = sum_over_all(sums)
    kv, query, out, pixels = call(
        final_kernel,
        [struct((D, 2 * D), F32), struct((PLEV, D), F32), struct((D, D), F32), struct((OUTS, D), F32)],
    )(sums, w_kv, level_queries, w_o, head)
    shape = latents.shape
    return (owned.reshape(shape), fields.reshape(shape[1], shape[2], PLEV * OUTS), kv, query, out, pixels.T)


def solution(mesh):
    in_specs = (
        P(None, "lat", "lon", None),
        P("lat", "lon"),
        P(),
        P(),
        P(),
        P(),
        P(),
        P(),
        P("lat", "lon", None),
    )
    out_specs = (P(None, "lat", "lon", None), P("lat", "lon", None), P(), P(), P(), P())
    return jax.shard_map(per_device, mesh=mesh, in_specs=in_specs, out_specs=out_specs, check_vma=False)
```

```python
import math

import jax
import jax.numpy as jnp
import numpy as np
from jax import lax
from jax.experimental import pallas as pl
from jax.experimental.pallas import tpu as pltpu
from jax.sharding import PartitionSpec as P

D = 512
HEADS = 8
LEV = 4
PLEV = 13
OUTS = 80
WL = 2
WH = 6
WW = 12
PATCHES = WH * 2 * WW
TOKENS = LEV * PATCHES
MAIN = 224
SIDE = 80
PACKED = 2 * MAIN + 2 * SIDE
ROWS = 768
BLOCK = 48
LANES = 128

SPAN = 256
PIECES = (
    {0: (0, 72, 0), 1: (72, 72, 0), 2: (144, 40, 0), 3: (184, 40, 0)},
    {0: (224, 72, 72), 1: (296, 72, 72), 2: (368, 40, 40), 3: (408, 40, 40)},
    {2: (448, 40, 80), 3: (488, 40, 80)},
    {2: (528, 40, 120), 3: (568, 40, 120)},
)

LAT = ("z", "x_hi")
LON = ("x_lo", "y", "core")
PLANE = ("x_hi", "x_lo", "y")

norm_eps = 1e-05
clip_eps = 1e-06
BF = jnp.bfloat16
F32 = jnp.float32


def window_order():
    level_pairs = ((1, 2), (3, 0))

    def rows_of(levels, rows, cols):
        return [(l * WH + r) * 2 * WW + c for l in levels for r in rows for c in cols]

    order = []
    for rows in ((3, 4, 5), (0, 1, 2)):
        for pair in level_pairs:
            order += rows_of(pair, rows, range(6, 18))
        for pair in level_pairs:
            order += rows_of(pair, rows, range(18, 24)) + [-1] * 4
    for rows in ((3, 4, 5), (0, 1, 2)):
        for pair in level_pairs:
            order += rows_of(pair, rows, range(0, 6)) + [-1] * 4
    return np.array(order)


def pack_matrix():
    order = window_order()
    return (order[:, None] == np.arange(TOKENS)[None, :]).astype(np.float32)


def label_tables():
    order = window_order()
    row, col, level = order // (2 * WW) % WH, order % (2 * WW), order // PATCHES
    columns = np.zeros((2 * WW, 12 * SPAN), np.float32)
    rows = np.zeros((8, 12 * SPAN), np.float32)
    extra = np.zeros((8, SPAN), np.float32)
    segment = 0
    for starts, far in zip(PIECES, (False, True, False, True)):
        for window, (at, count, place) in starts.items():
            for i in range(count):
                lane, token = place + i, at + i
                if order[token] < 0:
                    extra[window, lane] = -1
                    continue
                columns[col[token], segment * SPAN + lane] = 1
                rows[row[token], segment * SPAN + lane] = 1
                extra[window, lane] = 8 * (level[token] == 0)
                extra[4 + window, lane] = 4 * far
            segment += 1
    return columns, rows, extra


def dot(a, b, contract):
    return lax.dot_general(a, b, (contract, ((), ())), preferred_element_type=F32)


def mm(a, b):
    return dot(a, b, ((1,), (0,)))


def layer_norm(wide):
    center = wide - jnp.mean(wide, axis=-1, keepdims=True)
    spread = jnp.mean(center * center, axis=-1, keepdims=True)
    return (center * lax.rsqrt(spread + norm_eps)).astype(BF)


def pack_kernel(x_ref, ids_ref, perm_ref, columns_ref, rows_ref, main_ref, north_ref, west_ref, corner_ref):
    ids = ids_ref[...].astype(F32).astype(BF)
    lines = jnp.sum(mm(ids, columns_ref[...]) * rows_ref[:WH], axis=0, keepdims=True)
    x = x_ref[...]
    segment = 0
    for ref, windows in zip((main_ref, north_ref, west_ref, corner_ref), PIECES):
        height = ref.shape[0]
        first = min(at for at, _, _ in windows.values())
        packed = mm(perm_ref[first : first + height], x)
        bottom = [jnp.zeros((12, SPAN), F32)]
        for window in range(4):
            if window in windows:
                bottom.append(lines[:, segment * SPAN : (segment + 1) * SPAN])
                segment += 1
            else:
                bottom.append(jnp.zeros((1, SPAN), F32))
        bottom = jnp.concatenate(bottom, axis=0)
        bottom = jnp.concatenate([bottom, jnp.zeros((16, D - SPAN), F32)], axis=1)
        ref[: height - 16] = packed[: height - 16].astype(BF)
        ref[height - 16 :] = (packed[height - 16 :] + bottom).astype(BF)


def attention_kernel(
    flag_ref, main_ref, north_ref, west_ref, corner_ref, extra_ref, wqkv_ref, wout_ref,
    main_out, north_out, west_out, corner_out, proj, context,
):
    pieces = (main_ref, north_ref, west_ref, corner_ref)
    wide = jnp.concatenate([ref[...].astype(F32) for ref in pieces], axis=0)
    proj[...] = mm(layer_norm(wide), wqkv_ref[...])
    lines = sum(ref[ref.shape[0] - 16 :, :SPAN].astype(F32) for ref in pieces)[12:]
    lines = lines + extra_ref[:4] + jnp.where(flag_ref[0, 0] > 0, extra_ref[4:], 0.0)
    lines = jnp.concatenate([lines, lines], axis=0)
    i = lax.broadcasted_iota(jnp.int32, (SPAN, SPAN), 0)
    j = lax.broadcasted_iota(jnp.int32, (SPAN, SPAN), 1)
    standing = dot((i == j).astype(F32).astype(BF), lines.astype(BF), ((1,), (1,)))
    n, w, c = MAIN, 2 * MAIN, 2 * MAIN + SIDE
    windows = (
        (0, 144, ((0, 72), (n, 72))),
        (1, 144, ((72, 72), (n + 72, 72))),
        (2, 160, ((144, 40), (n + 144, 40), (w, 40), (c, 40))),
        (3, 160, ((184, 40), (n + 184, 40), (w + 40, 40), (c + 40, 40))),
    )
    low = lax.broadcasted_iota(jnp.int32, (1, LANES), 1) < D // HEADS
    for index, size, parts in windows:
        allowed = standing[:size, index : index + 1] == lines[index : index + 1, :size]
        bias = jnp.where(allowed, 0.0, -jnp.inf)
        bias = jnp.concatenate([bias, bias], axis=0)

        def take(start):
            return jnp.concatenate([proj[at : at + count, start : start + LANES] for at, count in parts], axis=0)

        for pair in range(HEADS // 2):
            lane = pair * LANES
            query = take(lane).astype(BF).astype(F32) * 0.125
            key = take(D + lane).astype(BF)
            value = take(2 * D + lane).astype(BF)
            both = jnp.concatenate([jnp.where(low, query, 0.0), jnp.where(low, 0.0, query)], axis=0).astype(BF)
            scores = dot(both, key, ((1,), (1,))) + bias
            weights = jnp.exp(scores - jnp.max(scores, axis=-1, keepdims=True))
            scale = 1.0 / jnp.sum(weights, axis=-1, keepdims=True)
            mixed = mm(weights.astype(BF), value) * scale
            result = jnp.where(low, mixed[:size], mixed[size:])
            start = 0
            for at, count in parts:
                context[at : at + count, lane : lane + LANES] = result[start : start + count]
                start += count
    mixed = wide + mm(context[...].astype(BF), wout_ref[...])
    mixed = mixed.astype(BF)
    main_out[...] = mixed[:n]
    north_out[...] = mixed[n:w]
    west_out[...] = mixed[w:c]
    corner_out[...] = mixed[c:]


def expand_matrices():
    c = lax.broadcasted_iota(jnp.int32, (LANES, D), 0)
    j = lax.broadcasted_iota(jnp.int32, (LANES, D), 1)
    gap = c - j // (D // HEADS)
    return [jnp.where(gap == level * HEADS, 1.0, 0.0).astype(BF) for level in range(PLEV)]


def shift_matrix(offset, width):
    i = lax.broadcasted_iota(jnp.int32, (width, LANES), 0)
    j = lax.broadcasted_iota(jnp.int32, (width, LANES), 1)
    return ((i - offset == j) & (j < OUTS)).astype(F32).astype(BF)


def spot(level):
    first = level * OUTS // LANES * LANES
    return first, level * OUTS - first, min(2 * LANES, PLEV * OUTS - first)


def spread_queries(queries):
    parts = [jnp.broadcast_to(queries[a : a + 1], (HEADS, D)) for a in range(PLEV)]
    parts.append(jnp.zeros((LANES - HEADS * PLEV, D), F32))
    tall = jnp.concatenate(parts, axis=0)
    c = lax.broadcasted_iota(jnp.int32, (LANES, D), 0)
    j = lax.broadcasted_iota(jnp.int32, (LANES, D), 1)
    return jnp.where(c % HEADS == j // (D // HEADS), tall, 0.0)


def pre_kernel(cot_ref, queries_ref, wo_ref, whead_ref, up_ref, dctx_ref, dsum_ref, map_ref, base_ref):
    head = whead_ref[...]
    both = dot(wo_ref[...], head, ((1,), (1,))).astype(BF)
    map_ref[...] = both
    base_ref[...] = jnp.concatenate(
        [dot(queries_ref[...], head, ((1,), (1,))), jnp.zeros((16 - PLEV, LANES), F32)], axis=0
    )
    dsum = jnp.zeros((PATCHES, D), F32)
    for level in range(PLEV):
        first, offset, width = spot(level)
        up = mm(cot_ref[:, first : first + width], shift_matrix(offset, width)).astype(BF)
        up_ref[level] = up
        dctx = dot(up, both, ((1,), (1,))).astype(BF)
        dctx_ref[level] = dctx
        dsum = dsum + dctx.astype(F32)
    dsum_ref[...] = dsum


def decode_kernel(
    flag_ref, main_ref, north_ref, west_ref, corner_ref, perm_ref, wkv_ref, queries_ref, up_ref, dctx_ref, dsum_ref,
    map_ref, base_ref,
    owned_ref, fields_ref, keep_ref, send_ref,
    value, weights, dvalues, context, products, fields, sums,
):
    pieces = (main_ref, north_ref, west_ref, corner_ref)
    packed = jnp.concatenate([ref[...] for ref in pieces], axis=0)
    wide = dot(perm_ref[...], packed, ((0,), (0,)))
    owned_ref[...] = wide.astype(BF)
    normed = layer_norm(wide)
    key = mm(normed, wkv_ref[:, :D]).astype(BF)
    value[...] = mm(normed, wkv_ref[:, D:]).astype(BF).astype(F32)
    queries = spread_queries(queries_ref[...].astype(F32)).astype(BF)
    scores = dot(key, queries, ((1,), (1,))) * 0.125
    slabs = [scores[l * PATCHES : (l + 1) * PATCHES] for l in range(LEV)]
    top = jnp.maximum(jnp.maximum(slabs[0], slabs[1]), jnp.maximum(slabs[2], slabs[3]))
    slabs = [jnp.exp(s - top) for s in slabs]
    scale = 1.0 / (slabs[0] + slabs[1] + slabs[2] + slabs[3])
    slabs = [s * scale for s in slabs]
    for l in range(LEV):
        weights[l * PATCHES : (l + 1) * PATCHES] = slabs[l]
    half = lax.broadcasted_iota(jnp.int32, (BLOCK, LANES), 1) // (D // HEADS)
    for tile in range(D // LANES):
        lanes = slice(tile * LANES, (tile + 1) * LANES)
        for start in range(0, PATCHES, BLOCK):
            at = [slice(l * PATCHES + start, l * PATCHES + start + BLOCK) for l in range(LEV)]
            last = value[at[LEV - 1], lanes]
            gaps = [value[at[l], lanes] - last for l in range(LEV - 1)]
            heads = [weights[at[l]] for l in range(LEV - 1)]
            found = [jnp.zeros((BLOCK, LANES), F32) for _ in range(LEV - 1)]
            for level in range(PLEV):
                index = half + (level * HEADS + 2 * tile)
                upstream = dctx_ref[level, start : start + BLOCK, lanes].astype(F32)
                total = last
                for l in range(LEV - 1):
                    spread = jnp.take_along_axis(heads[l], index, axis=1)
                    total = total + spread * gaps[l]
                    found[l] = found[l] + spread * upstream
                    products[level, at[l], lanes] = (upstream * gaps[l]).astype(BF)
                context[level * PATCHES + start : level * PATCHES + start + BLOCK, lanes] = total.astype(BF)
            for l in range(LEV - 1):
                dvalues[at[l], lanes] = found[l]
            dvalues[at[LEV - 1], lanes] = dsum_ref[start : start + BLOCK, lanes] - (found[0] + found[1] + found[2])
    fields[...] = jnp.zeros_like(fields)
    slopes = jnp.zeros(((LEV - 1) * PATCHES, LANES), F32)
    expand = expand_matrices()
    for level in range(PLEV):
        slopes = slopes + dot(products[level], expand[level], ((1,), (1,)))
        first, offset, width = spot(level)
        decoded = mm(context[level * PATCHES : (level + 1) * PATCHES], map_ref[...]) + base_ref[level : level + 1]
        fields[:, first : first + width] += dot(decoded.astype(BF), shift_matrix(offset, width), ((1,), (1,)))
    fields_ref[...] = fields[...].astype(BF)
    slopes = [slopes[l * PATCHES : (l + 1) * PATCHES] for l in range(LEV - 1)]
    mean = sum(p * d for p, d in zip(slabs, slopes))
    dscores = [p * (d - mean) * 0.125 for p, d in zip(slabs, slopes)]
    dscores.append(slabs[LEV - 1] * mean * -0.125)
    dscores = jnp.concatenate(dscores, axis=0).astype(BF)
    sums[:D] = dot(normed, dvalues[...].astype(BF), ((0,), (0,)))
    sums[D : D + LANES] = dot(dscores, normed, ((0,), (0,)))
    up = jnp.concatenate([up_ref[a] for a in range(PLEV)], axis=0)
    outer = dot(up, context[...], ((0,), (0,)))
    sums[D + LANES : D + LANES + OUTS] = outer[:OUTS]
    totals = [jnp.sum(up_ref[a].astype(F32), axis=0, keepdims=True) for a in range(PLEV)]
    totals.append(jnp.zeros((LANES - OUTS - PLEV, LANES), F32))
    totals = jnp.concatenate(totals, axis=0)
    sums[D + LANES + OUTS :] = jnp.concatenate([totals, jnp.zeros((LANES - OUTS, D - LANES), F32)], axis=1)
    second = flag_ref[0, 0] > 0
    top, bottom = sums[: ROWS // 2], sums[ROWS // 2 :]
    keep_ref[...] = jnp.where(second, bottom, top).astype(BF)
    send_ref[...] = jnp.where(second, top, bottom).astype(BF)


def final_kernel(flag_ref, mine_ref, other_ref, wkv_ref, queries_ref, wo_ref, whead_ref, kv_ref, query_ref, o_ref, head_ref):
    second = flag_ref[0, 0] > 0
    mine, other = mine_ref[...].astype(F32), other_ref[...].astype(F32)
    sums = jnp.concatenate([jnp.where(second, other, mine), jnp.where(second, mine, other)], axis=0).astype(BF)
    queries = queries_ref[...]
    head = whead_ref[...]
    keyed = sums[D : D + LANES]
    outer = sums[D + LANES :]
    level_sums = outer[OUTS : OUTS + 16, :LANES]
    spread = spread_queries(queries.astype(F32)).astype(BF)
    values = sums[:D].astype(F32)
    keys = dot(keyed, spread, ((0,), (0,)))
    c = lax.broadcasted_iota(jnp.int32, (LANES, D), 0)
    j = lax.broadcasted_iota(jnp.int32, (LANES, D), 1)
    grouped = jnp.where(c % HEADS == j // (D // HEADS), mm(keyed, wkv_ref[:, :D]), 0.0)
    grouped = jnp.sum(grouped.reshape(LANES // HEADS, HEADS, D), axis=1)
    level = grouped[:PLEV] + mm(level_sums, head)[:PLEV]
    clean = outer[:OUTS]
    out = dot(clean, head[:OUTS], ((0,), (0,)))
    pixels = mm(clean, wo_ref[...])
    pixels = pixels + dot(level_sums[:PLEV, :OUTS], queries, ((0,), (0,)))
    squares = jnp.sum(values * values) + jnp.sum(keys * keys) + jnp.sum(level * level)
    squares = squares + jnp.sum(out * out) + jnp.sum(pixels * pixels)
    limit = math.sqrt(2 * D * D + PLEV * D + D * D + D * OUTS)
    factor = jnp.minimum(1.0, limit * lax.rsqrt(jnp.full((1, 1), squares + clip_eps, F32)))
    kv_ref[:, :D] = keys * factor
    kv_ref[:, D:] = values * factor
    query_ref[...] = level * factor
    o_ref[...] = out * factor
    head_ref[...] = pixels * factor


def call(kernel, outs, scratch=(), smem=0):
    more = {}
    if smem:
        whole = pl.BlockSpec(memory_space=pltpu.VMEM)
        more["in_specs"] = [pl.BlockSpec(memory_space=pltpu.SMEM)] + [whole] * smem
    return pl.pallas_call(
        kernel,
        **more,
        out_shape=outs,
        scratch_shapes=list(scratch),
        compiler_params=pltpu.CompilerParams(vmem_limit_bytes=56 * 2**20),
    )


def struct(shape, dtype=BF):
    return jax.ShapeDtypeStruct(shape, dtype)


def move(array, lat_step, lon_step):
    lats, lons = lax.axis_size(LAT), lax.axis_size(LON)
    route = [
        (i * lons + j, (i + lat_step) % lats * lons + (j + lon_step) % lons)
        for i in range(lats)
        for j in range(lons)
    ]
    return lax.ppermute(array, LAT + LON, route)


def swap(array):
    count = lax.axis_size("core")
    return lax.ppermute(array, "core", [(i, (i + 1) % count) for i in range(count)])


def add_up(blocks):
    return jnp.sum(blocks.astype(F32), axis=0).astype(BF)


def copies(block, axes):
    return jnp.broadcast_to(block[None], (lax.axis_size(axes),) + block.shape)


def sum_over_all(keep, send):
    rows, width = keep.shape
    mine = (keep.astype(F32) + swap(send).astype(F32)).astype(BF)
    chips = lax.axis_size(PLANE)
    mine = add_up(lax.all_to_all(mine.reshape(chips, rows // chips, width), PLANE, 0, 0, tiled=True))
    mine = add_up(lax.all_to_all(copies(mine, "z"), "z", 0, 0, tiled=True))
    mine = lax.all_to_all(copies(mine, PLANE), PLANE, 0, 0, tiled=True).reshape(rows, width)
    return mine, swap(mine)


def per_device(latents, mask_ids, w_qkv, w_out, w_kv, level_queries, w_o, w_head, field_cotangent):
    perm = jnp.asarray(pack_matrix(), BF)
    columns, rows, extra = label_tables()
    flag = (lax.axis_index(LAT) == lax.axis_size(LAT) - 1).astype(jnp.int32).reshape(1, 1)
    shapes = [struct((MAIN, D)), struct((MAIN, D)), struct((SIDE, D)), struct((SIDE, D))]
    main, north, west, corner = call(pack_kernel, shapes)(
        latents.reshape(TOKENS, D), mask_ids, perm, jnp.asarray(columns, BF), jnp.asarray(rows)
    )
    north, west, corner = move(north, -1, 0), move(west, 0, -1), move(corner, -1, -1)
    head = jnp.pad(w_head.T, ((0, LANES - OUTS), (0, 0)))
    up, dctx, dsum, both, base = call(
        pre_kernel,
        [
            struct((PLEV, PATCHES, LANES)),
            struct((PLEV, PATCHES, D)),
            struct((PATCHES, D), F32),
            struct((D, LANES)),
            struct((16, LANES), F32),
        ],
    )(field_cotangent.reshape(PATCHES, PLEV * OUTS), level_queries, w_o, head)
    main, north, west, corner = call(
        attention_kernel,
        shapes,
        [pltpu.VMEM((PACKED, 3 * D), F32), pltpu.VMEM((PACKED, D), F32)],
        smem=7,
    )(flag, main, north, west, corner, jnp.asarray(extra), w_qkv, w_out)
    north, west, corner = move(north, 1, 0), move(west, 0, 1), move(corner, 1, 1)
    core = lax.axis_index("core").astype(jnp.int32).reshape(1, 1)
    share = struct((ROWS // 2, D))
    owned, fields, keep, send = call(
        decode_kernel,
        [struct((TOKENS, D)), struct((PATCHES, PLEV * OUTS)), share, share],
        [
            pltpu.VMEM((TOKENS, D), F32),
            pltpu.VMEM((TOKENS, LANES), F32),
            pltpu.VMEM((TOKENS, D), F32),
            pltpu.VMEM((PLEV * PATCHES, D), BF),
            pltpu.VMEM((PLEV, (LEV - 1) * PATCHES, D), BF),
            pltpu.VMEM((PATCHES, PLEV * OUTS), F32),
            pltpu.VMEM((ROWS, D), F32),
        ],
        smem=12,
    )(core, main, north, west, corner, perm, w_kv, level_queries, up, dctx, dsum, both, base)
    mine, other = sum_over_all(keep, send)
    kv, query, out, pixels = call(
        final_kernel,
        [struct((D, 2 * D), F32), struct((PLEV, D), F32), struct((D, D), F32), struct((OUTS, D), F32)],
        smem=6,
    )(core, mine, other, w_kv, level_queries, w_o, head)
    shape = latents.shape
    return (owned.reshape(shape), fields.reshape(shape[1], shape[2], PLEV * OUTS), kv, query, out, pixels.T)


def solution(mesh):
    lats, lons = mesh.shape["lat"], mesh.shape["lon"]
    sizes = (lats // 2, 2, 2, lons // 4, 2)
    fine = jax.sharding.Mesh(mesh.devices.reshape(sizes), LAT + LON)
    in_specs = (
        P(None, LAT, LON, None),
        P(LAT, LON),
        P(),
        P(),
        P(),
        P(),
        P(),
        P(),
        P(LAT, LON, None),
    )
    out_specs = (P(None, LAT, LON, None), P(LAT, LON, None), P(), P(), P(), P())
    return jax.shard_map(per_device, mesh=fine, in_specs=in_specs, out_specs=out_specs, check_vma=False)
```

```python
import math

import jax
import jax.numpy as jnp
import numpy as np
from jax import lax
from jax.experimental import pallas as pl
from jax.experimental.pallas import tpu as pltpu
from jax.sharding import PartitionSpec as P

D = 512
HEADS = 8
LEV = 4
PLEV = 13
OUTS = 80
WL = 2
WH = 6
WW = 12
PATCHES = WH * 2 * WW
TOKENS = LEV * PATCHES
MAIN = 224
SIDE = 80
PACKED = 2 * MAIN + 2 * SIDE
ROWS = 768
BLOCK = 16
LANES = 128

SPAN = 256
PIECES = (
    {0: (0, 72, 0), 1: (72, 72, 0), 2: (144, 40, 0), 3: (184, 40, 0)},
    {0: (224, 72, 72), 1: (296, 72, 72), 2: (368, 40, 40), 3: (408, 40, 40)},
    {2: (448, 40, 80), 3: (488, 40, 80)},
    {2: (528, 40, 120), 3: (568, 40, 120)},
)

LAT = ("z", "x_hi")
LON = ("x_lo", "y", "core")
PLANE = ("x_hi", "x_lo", "y")

norm_eps = 1e-05
clip_eps = 1e-06
BF = jnp.bfloat16
F32 = jnp.float32


def window_order():
    level_pairs = ((1, 2), (3, 0))

    def rows_of(levels, rows, cols):
        return [(l * WH + r) * 2 * WW + c for l in levels for r in rows for c in cols]

    order = []
    for rows in ((3, 4, 5), (0, 1, 2)):
        for pair in level_pairs:
            order += rows_of(pair, rows, range(6, 18))
        for pair in level_pairs:
            order += rows_of(pair, rows, range(18, 24)) + [-1] * 4
    for rows in ((3, 4, 5), (0, 1, 2)):
        for pair in level_pairs:
            order += rows_of(pair, rows, range(0, 6)) + [-1] * 4
    return np.array(order)


def pack_matrix():
    order = window_order()
    return (order[:, None] == np.arange(TOKENS)[None, :]).astype(np.float32)


def label_tables():
    order = window_order()
    row, col, level = order // (2 * WW) % WH, order % (2 * WW), order // PATCHES
    columns = np.zeros((2 * WW, 12 * SPAN), np.float32)
    rows = np.zeros((8, 12 * SPAN), np.float32)
    extra = np.zeros((8, SPAN), np.float32)
    segment = 0
    for starts, far in zip(PIECES, (False, True, False, True)):
        for window, (at, count, place) in starts.items():
            for i in range(count):
                lane, token = place + i, at + i
                if order[token] < 0:
                    extra[window, lane] = -1
                    continue
                columns[col[token], segment * SPAN + lane] = 1
                rows[row[token], segment * SPAN + lane] = 1
                extra[window, lane] = 8 * (level[token] == 0)
                extra[4 + window, lane] = 4 * far
            segment += 1
    return columns, rows, extra


def dot(a, b, contract):
    return lax.dot_general(a, b, (contract, ((), ())), preferred_element_type=F32)


def mm(a, b):
    return dot(a, b, ((1,), (0,)))


def layer_norm(wide):
    center = wide - jnp.mean(wide, axis=-1, keepdims=True)
    spread = jnp.mean(center * center, axis=-1, keepdims=True)
    return (center * lax.rsqrt(spread + norm_eps)).astype(BF)


def pack_kernel(x_ref, ids_ref, perm_ref, columns_ref, rows_ref, main_ref, north_ref, west_ref, corner_ref):
    ids = ids_ref[...].astype(F32).astype(BF)
    lines = jnp.sum(mm(ids, columns_ref[...]) * rows_ref[:WH], axis=0, keepdims=True)
    x = x_ref[...]
    segment = 0
    for ref, windows in zip((main_ref, north_ref, west_ref, corner_ref), PIECES):
        height = ref.shape[0]
        first = min(at for at, _, _ in windows.values())
        packed = mm(perm_ref[first : first + height], x)
        bottom = [jnp.zeros((12, SPAN), F32)]
        for window in range(4):
            if window in windows:
                bottom.append(lines[:, segment * SPAN : (segment + 1) * SPAN])
                segment += 1
            else:
                bottom.append(jnp.zeros((1, SPAN), F32))
        bottom = jnp.concatenate(bottom, axis=0)
        bottom = jnp.concatenate([bottom, jnp.zeros((16, D - SPAN), F32)], axis=1)
        ref[: height - 16] = packed[: height - 16].astype(BF)
        ref[height - 16 :] = (packed[height - 16 :] + bottom).astype(BF)


def attention_kernel(
    flag_ref, extra_ref, main_ref, north_ref, west_ref, corner_ref, wqkv_ref, wout_ref,
    main_out, north_out, west_out, corner_out, proj, context,
):
    pieces = (main_ref, north_ref, west_ref, corner_ref)
    wide = jnp.concatenate([ref[...].astype(F32) for ref in pieces], axis=0)
    proj[...] = mm(layer_norm(wide), wqkv_ref[...])
    lines = sum(ref[ref.shape[0] - 16 :, :SPAN].astype(F32) for ref in pieces)[12:]
    lines = lines + extra_ref[:4] + jnp.where(flag_ref[0, 0] > 0, extra_ref[4:], 0.0)
    lines = jnp.concatenate([lines, lines], axis=0)
    i = lax.broadcasted_iota(jnp.int32, (SPAN, SPAN), 0)
    j = lax.broadcasted_iota(jnp.int32, (SPAN, SPAN), 1)
    standing = dot((i == j).astype(F32).astype(BF), lines.astype(BF), ((1,), (1,)))
    n, w, c = MAIN, 2 * MAIN, 2 * MAIN + SIDE
    windows = (
        (0, 144, ((0, 72), (n, 72))),
        (1, 144, ((72, 72), (n + 72, 72))),
        (2, 160, ((144, 40), (n + 144, 40), (w, 40), (c, 40))),
        (3, 160, ((184, 40), (n + 184, 40), (w + 40, 40), (c + 40, 40))),
    )
    low = lax.broadcasted_iota(jnp.int32, (1, LANES), 1) < D // HEADS
    for index, size, parts in windows:
        allowed = standing[:size, index : index + 1] == lines[index : index + 1, :size]
        bias = jnp.where(allowed, 0.0, -jnp.inf)
        bias = jnp.concatenate([bias, bias], axis=0)

        def take(start):
            return jnp.concatenate([proj[at : at + count, start : start + LANES] for at, count in parts], axis=0)

        for pair in range(HEADS // 2):
            lane = pair * LANES
            query = take(lane).astype(BF).astype(F32) * 0.125
            key = take(D + lane).astype(BF)
            value = take(2 * D + lane).astype(BF)
            both = jnp.concatenate([jnp.where(low, query, 0.0), jnp.where(low, 0.0, query)], axis=0).astype(BF)
            scores = dot(both, key, ((1,), (1,))) + bias
            weights = jnp.exp(scores - jnp.max(scores, axis=-1, keepdims=True))
            scale = 1.0 / jnp.sum(weights, axis=-1, keepdims=True)
            mixed = mm(weights.astype(BF), value) * scale
            result = jnp.where(low, mixed[:size], mixed[size:])
            start = 0
            for at, count in parts:
                context[at : at + count, lane : lane + LANES] = result[start : start + count]
                start += count
    mixed = wide + mm(context[...].astype(BF), wout_ref[...])
    mixed = mixed.astype(BF)
    main_out[...] = mixed[:n]
    north_out[...] = mixed[n:w]
    west_out[...] = mixed[w:c]
    corner_out[...] = mixed[c:]


def expand_matrices():
    c = lax.broadcasted_iota(jnp.int32, (LANES, D), 0)
    j = lax.broadcasted_iota(jnp.int32, (LANES, D), 1)
    gap = c - j // (D // HEADS)
    return [jnp.where(gap == level * HEADS, 1.0, 0.0).astype(BF) for level in range(PLEV)]


def shift_matrix(offset, width):
    i = lax.broadcasted_iota(jnp.int32, (width, LANES), 0)
    j = lax.broadcasted_iota(jnp.int32, (width, LANES), 1)
    return ((i - offset == j) & (j < OUTS)).astype(F32).astype(BF)


def spot(level):
    first = level * OUTS // LANES * LANES
    return first, level * OUTS - first, min(2 * LANES, PLEV * OUTS - first)


def spread_queries(queries):
    parts = [jnp.broadcast_to(queries[a : a + 1], (HEADS, D)) for a in range(PLEV)]
    parts.append(jnp.zeros((LANES - HEADS * PLEV, D), F32))
    tall = jnp.concatenate(parts, axis=0)
    c = lax.broadcasted_iota(jnp.int32, (LANES, D), 0)
    j = lax.broadcasted_iota(jnp.int32, (LANES, D), 1)
    return jnp.where(c % HEADS == j // (D // HEADS), tall, 0.0)


def pre_kernel(cot_ref, queries_ref, wo_ref, whead_ref, up_ref, dctx_ref, dsum_ref, map_ref, base_ref):
    head = whead_ref[...]
    both = dot(wo_ref[...], head, ((1,), (1,))).astype(BF)
    map_ref[...] = both
    base_ref[...] = jnp.concatenate(
        [dot(queries_ref[...], head, ((1,), (1,))), jnp.zeros((16 - PLEV, LANES), F32)], axis=0
    )
    dsum = jnp.zeros((PATCHES, D), F32)
    for level in range(PLEV):
        first, offset, width = spot(level)
        up = mm(cot_ref[:, first : first + width], shift_matrix(offset, width)).astype(BF)
        up_ref[level] = up
        dctx = dot(up, both, ((1,), (1,))).astype(BF)
        dctx_ref[level] = dctx
        dsum = dsum + dctx.astype(F32)
    dsum_ref[...] = dsum


def decode_kernel(
    flag_ref, main_ref, north_ref, west_ref, corner_ref, perm_ref, wkv_ref, queries_ref, up_ref, dctx_ref, dsum_ref,
    map_ref, base_ref,
    owned_ref, fields_ref, keep_ref, send_ref,
    value, weights, dvalues, context, products, fields, sums,
):
    pieces = (main_ref, north_ref, west_ref, corner_ref)
    packed = jnp.concatenate([ref[...] for ref in pieces], axis=0)
    wide = mm(perm_ref[...], packed)
    owned_ref[...] = wide.astype(BF)
    normed = layer_norm(wide)
    key = mm(normed, wkv_ref[:, :D]).astype(BF)
    value[...] = mm(normed, wkv_ref[:, D:]).astype(BF).astype(F32)
    queries = spread_queries(queries_ref[...].astype(F32)).astype(BF)
    scores = dot(key, queries, ((1,), (1,))) * 0.125
    slabs = [scores[l * PATCHES : (l + 1) * PATCHES] for l in range(LEV)]
    top = jnp.maximum(jnp.maximum(slabs[0], slabs[1]), jnp.maximum(slabs[2], slabs[3]))
    slabs = [jnp.exp(s - top) for s in slabs]
    scale = 1.0 / (slabs[0] + slabs[1] + slabs[2] + slabs[3])
    slabs = [s * scale for s in slabs]
    for l in range(LEV):
        weights[l * PATCHES : (l + 1) * PATCHES] = slabs[l]
    half = lax.broadcasted_iota(jnp.int32, (BLOCK, LANES), 1) // (D // HEADS)
    for tile in range(D // LANES):
        lanes = slice(tile * LANES, (tile + 1) * LANES)
        for start in range(0, PATCHES, BLOCK):
            at = [slice(l * PATCHES + start, l * PATCHES + start + BLOCK) for l in range(LEV)]
            last = value[at[LEV - 1], lanes]
            gaps = [value[at[l], lanes] - last for l in range(LEV - 1)]
            heads = [weights[at[l]] for l in range(LEV - 1)]
            found = [jnp.zeros((BLOCK, LANES), F32) for _ in range(LEV - 1)]
            for level in range(PLEV):
                index = half + (level * HEADS + 2 * tile)
                upstream = dctx_ref[level, start : start + BLOCK, lanes].astype(F32)
                total = last
                for l in range(LEV - 1):
                    spread = jnp.take_along_axis(heads[l], index, axis=1)
                    total = total + spread * gaps[l]
                    found[l] = found[l] + spread * upstream
                    products[level, at[l], lanes] = (upstream * gaps[l]).astype(BF)
                context[level * PATCHES + start : level * PATCHES + start + BLOCK, lanes] = total.astype(BF)
            for l in range(LEV - 1):
                dvalues[at[l], lanes] = found[l]
            dvalues[at[LEV - 1], lanes] = dsum_ref[start : start + BLOCK, lanes] - (found[0] + found[1] + found[2])
    fields[...] = jnp.zeros_like(fields)
    slopes = jnp.zeros(((LEV - 1) * PATCHES, LANES), F32)
    expand = expand_matrices()
    for level in range(PLEV):
        slopes = slopes + dot(products[level], expand[level], ((1,), (1,)))
        first, offset, width = spot(level)
        decoded = mm(context[level * PATCHES : (level + 1) * PATCHES], map_ref[...]) + base_ref[level : level + 1]
        fields[:, first : first + width] += dot(decoded.astype(BF), shift_matrix(offset, width), ((1,), (1,)))
    fields_ref[...] = fields[...].astype(BF)
    slopes = [slopes[l * PATCHES : (l + 1) * PATCHES] for l in range(LEV - 1)]
    mean = sum(p * d for p, d in zip(slabs, slopes))
    dscores = [p * (d - mean) * 0.125 for p, d in zip(slabs, slopes)]
    dscores.append(slabs[LEV - 1] * mean * -0.125)
    dscores = jnp.concatenate(dscores, axis=0).astype(BF)
    sums[:D] = dot(normed, dvalues[...].astype(BF), ((0,), (0,)))
    sums[D : D + LANES] = dot(dscores, normed, ((0,), (0,)))
    up = jnp.concatenate([up_ref[a] for a in range(PLEV)], axis=0)
    outer = dot(up, context[...], ((0,), (0,)))
    sums[D + LANES : D + LANES + OUTS] = outer[:OUTS]
    totals = [jnp.sum(up_ref[a].astype(F32), axis=0, keepdims=True) for a in range(PLEV)]
    totals.append(jnp.zeros((LANES - OUTS - PLEV, LANES), F32))
    totals = jnp.concatenate(totals, axis=0)
    sums[D + LANES + OUTS :] = jnp.concatenate([totals, jnp.zeros((LANES - OUTS, D - LANES), F32)], axis=1)
    second = flag_ref[0, 0] > 0
    top, bottom = sums[: ROWS // 2], sums[ROWS // 2 :]
    keep_ref[...] = jnp.where(second, bottom, top).astype(BF)
    send_ref[...] = jnp.where(second, top, bottom).astype(BF)


def add_kernel(left_ref, right_ref, out_ref):
    out_ref[...] = (left_ref[...].astype(F32) + right_ref[...].astype(F32)).astype(BF)


def final_kernel(flag_ref, mine_ref, other_ref, wkv_ref, queries_ref, wo_ref, whead_ref, kv_ref, query_ref, o_ref, head_ref):
    second = flag_ref[0, 0] > 0
    mine, other = mine_ref[...].astype(F32), other_ref[...].astype(F32)
    sums = jnp.concatenate([jnp.where(second, other, mine), jnp.where(second, mine, other)], axis=0).astype(BF)
    queries = queries_ref[...]
    head = whead_ref[...]
    keyed = sums[D : D + LANES]
    outer = sums[D + LANES :]
    level_sums = outer[OUTS : OUTS + 16, :LANES]
    spread = spread_queries(queries.astype(F32)).astype(BF)
    values = sums[:D].astype(F32)
    keys = dot(keyed, spread, ((0,), (0,)))
    c = lax.broadcasted_iota(jnp.int32, (LANES, D), 0)
    j = lax.broadcasted_iota(jnp.int32, (LANES, D), 1)
    grouped = jnp.where(c % HEADS == j // (D // HEADS), mm(keyed, wkv_ref[:, :D]), 0.0)
    grouped = jnp.sum(grouped.reshape(LANES // HEADS, HEADS, D), axis=1)
    level = grouped[:PLEV] + mm(level_sums, head)[:PLEV]
    clean = outer[:OUTS]
    out = dot(clean, head[:OUTS], ((0,), (0,)))
    pixels = mm(clean, wo_ref[...])
    pixels = pixels + dot(level_sums[:PLEV, :OUTS], queries, ((0,), (0,)))
    squares = jnp.sum(values * values) + jnp.sum(keys * keys) + jnp.sum(level * level)
    squares = squares + jnp.sum(out * out) + jnp.sum(pixels * pixels)
    limit = math.sqrt(2 * D * D + PLEV * D + D * D + D * OUTS)
    factor = jnp.minimum(1.0, limit * lax.rsqrt(jnp.full((1, 1), squares + clip_eps, F32)))
    kv_ref[:, :D] = keys * factor
    kv_ref[:, D:] = values * factor
    query_ref[...] = level * factor
    o_ref[...] = out * factor
    head_ref[...] = pixels * factor


def call(kernel, outs, spaces, scratch=(), limit=40):
    where = {"V": pltpu.VMEM, "H": pltpu.HBM}
    whole, scalar = pl.BlockSpec(memory_space=pltpu.VMEM), pl.BlockSpec(memory_space=pltpu.SMEM)
    run = pl.pallas_call(
        kernel,
        in_specs=[scalar if space == "S" else whole for space in spaces],
        out_shape=outs,
        scratch_shapes=list(scratch),
        compiler_params=pltpu.CompilerParams(vmem_limit_bytes=limit * 2**20),
    )

    def close(*operands):
        held = [
            pltpu.with_memory_space_constraint(x, where[space]) if space in where else x
            for space, x in zip(spaces, operands, strict=True)
        ]
        return run(*held)

    return close


def struct(shape, dtype=BF):
    return jax.ShapeDtypeStruct(shape, dtype)


def far_struct(shape, dtype=BF):
    return pltpu.HBM(shape, dtype)


def move(array, lat_step, lon_step):
    lats, lons = lax.axis_size(LAT), lax.axis_size(LON)
    route = [
        (i * lons + j, (i + lat_step) % lats * lons + (j + lon_step) % lons)
        for i in range(lats)
        for j in range(lons)
    ]
    return lax.ppermute(array, LAT + LON, route)


def swap(array):
    count = lax.axis_size("core")
    return lax.ppermute(array, "core", [(i, (i + 1) % count) for i in range(count)])


def add_up(blocks):
    return jnp.sum(blocks.astype(F32), axis=0).astype(BF)


def copies(block, axes):
    return jnp.broadcast_to(block[None], (lax.axis_size(axes),) + block.shape)


def sum_over_all(keep, send):
    rows, width = keep.shape
    mine = call(add_kernel, struct((rows, width)), "VV", limit=8)(keep, swap(send))
    chips = lax.axis_size(PLANE)
    mine = add_up(lax.all_to_all(mine.reshape(chips, rows // chips, width), PLANE, 0, 0, tiled=True))
    mine = add_up(lax.all_to_all(copies(mine, "z"), "z", 0, 0, tiled=True))
    mine = lax.all_to_all(copies(mine, PLANE), PLANE, 0, 0, tiled=True).reshape(rows, width)
    return mine, swap(mine)


def per_device(latents, mask_ids, w_qkv, w_out, w_kv, level_queries, w_o, w_head, field_cotangent):
    perm = pack_matrix()
    columns, rows, extra = label_tables()
    flag = (lax.axis_index(LAT) == lax.axis_size(LAT) - 1).astype(jnp.int32).reshape(1, 1)
    shapes = [far_struct((MAIN, D)), struct((MAIN, D)), struct((SIDE, D)), struct((SIDE, D))]
    main, north, west, corner = call(pack_kernel, shapes, "HHHHH", limit=56)(
        latents.reshape(TOKENS, D), mask_ids, jnp.asarray(perm, BF), jnp.asarray(columns, BF), jnp.asarray(rows)
    )
    north, west, corner = move(north, -1, 0), move(west, 0, -1), move(corner, -1, -1)
    head = jnp.pad(w_head.T, ((0, LANES - OUTS), (0, 0)))
    up, dctx, dsum, both, base = call(
        pre_kernel,
        [
            struct((PLEV, PATCHES, LANES)),
            struct((PLEV, PATCHES, D)),
            struct((PATCHES, D), F32),
            struct((D, LANES)),
            struct((16, LANES), F32),
        ],
        "VVVV",
    )(field_cotangent.reshape(PATCHES, PLEV * OUTS), level_queries, w_o, head)
    main, north, west, corner = call(
        attention_kernel,
        shapes,
        "SHHHHHVV",
        [pltpu.VMEM((PACKED, 3 * D), F32), pltpu.VMEM((PACKED, D), F32)],
        limit=48,
    )(flag, jnp.asarray(extra), main, north, west, corner, w_qkv, w_out)
    north, west, corner = move(north, 1, 0), move(west, 0, 1), move(corner, 1, 1)
    core = lax.axis_index("core").astype(jnp.int32).reshape(1, 1)
    share = struct((ROWS // 2, D))
    owned, fields, keep, send = call(
        decode_kernel,
        [struct((TOKENS, D)), struct((PATCHES, PLEV * OUTS)), share, share],
        "SHVVVHVVVVVVV",
        [
            pltpu.VMEM((TOKENS, D), F32),
            pltpu.VMEM((TOKENS, LANES), F32),
            pltpu.VMEM((TOKENS, D), F32),
            pltpu.VMEM((PLEV * PATCHES, D), BF),
            pltpu.VMEM((PLEV, (LEV - 1) * PATCHES, D), BF),
            pltpu.VMEM((PATCHES, PLEV * OUTS), F32),
            pltpu.VMEM((ROWS, D), F32),
        ],
    )(core, main, north, west, corner, jnp.asarray(perm.T, BF), w_kv, level_queries, up, dctx, dsum, both, base)
    mine, other = sum_over_all(keep, send)
    kv, query, out, pixels = call(
        final_kernel,
        [struct((D, 2 * D), F32), struct((PLEV, D), F32), struct((D, D), F32), struct((OUTS, D), F32)],
        "SVVVVVV",
    )(core, mine, other, w_kv, level_queries, w_o, head)
    shape = latents.shape
    return (owned.reshape(shape), fields.reshape(shape[1], shape[2], PLEV * OUTS), kv, query, out, pixels.T)


def solution(mesh):
    lats, lons = mesh.shape["lat"], mesh.shape["lon"]
    sizes = (lats // 2, 2, 2, lons // 4, 2)
    fine = jax.sharding.Mesh(mesh.devices.reshape(sizes), LAT + LON)
    in_specs = (
        P(None, LAT, LON, None),
        P(LAT, LON),
        P(),
        P(),
        P(),
        P(),
        P(),
        P(),
        P(LAT, LON, None),
    )
    out_specs = (P(None, LAT, LON, None), P(LAT, LON, None), P(), P(), P(), P())
    return jax.shard_map(per_device, mesh=fine, in_specs=in_specs, out_specs=out_specs, check_vma=False)
```

```python
import functools
import math

import jax
import jax.numpy as jnp
import numpy as np
from jax import lax
from jax.experimental import pallas as pl
from jax.experimental.pallas import tpu as pltpu
from jax.sharding import PartitionSpec as P

D = 512
HEADS = 8
LEV = 4
PLEV = 13
OUTS = 80
WL = 2
WH = 6
WW = 12
PATCHES = WH * 2 * WW
TOKENS = LEV * PATCHES
MAIN = 224
SIDE = 80
PACKED = 2 * MAIN + 2 * SIDE
ROWS = 768
BLOCK = 16
LANES = 128

SPAN = 256
PIECES = (
    {0: (0, 72, 0), 1: (72, 72, 0), 2: (144, 40, 0), 3: (184, 40, 0)},
    {0: (224, 72, 72), 1: (296, 72, 72), 2: (368, 40, 40), 3: (408, 40, 40)},
    {2: (448, 40, 80), 3: (488, 40, 80)},
    {2: (528, 40, 120), 3: (568, 40, 120)},
)

LAT = ("z", "x_hi")
LON = ("x_lo", "y", "core")
PLANE = ("x_hi", "x_lo", "y")

norm_eps = 1e-05
clip_eps = 1e-06
BF = jnp.bfloat16
F32 = jnp.float32


def window_order():
    level_pairs = ((1, 2), (3, 0))

    def rows_of(levels, rows, cols):
        return [(l * WH + r) * 2 * WW + c for l in levels for r in rows for c in cols]

    order = []
    for rows in ((3, 4, 5), (0, 1, 2)):
        for pair in level_pairs:
            order += rows_of(pair, rows, range(6, 18))
        for pair in level_pairs:
            order += rows_of(pair, rows, range(18, 24)) + [-1] * 4
    for rows in ((3, 4, 5), (0, 1, 2)):
        for pair in level_pairs:
            order += rows_of(pair, rows, range(0, 6)) + [-1] * 4
    return np.array(order)


def pack_matrix():
    order = window_order()
    return (order[:, None] == np.arange(TOKENS)[None, :]).astype(np.float32)


def label_tables():
    order = window_order()
    row, col, level = order // (2 * WW) % WH, order % (2 * WW), order // PATCHES
    columns = np.zeros((2 * WW, 12 * SPAN), np.float32)
    rows = np.zeros((8, 12 * SPAN), np.float32)
    extra = np.zeros((8, SPAN), np.float32)
    segment = 0
    for starts, far in zip(PIECES, (False, True, False, True)):
        for window, (at, count, place) in starts.items():
            for i in range(count):
                lane, token = place + i, at + i
                if order[token] < 0:
                    extra[window, lane] = -1
                    continue
                columns[col[token], segment * SPAN + lane] = 1
                rows[row[token], segment * SPAN + lane] = 1
                extra[window, lane] = 8 * (level[token] == 0)
                extra[4 + window, lane] = 4 * far
            segment += 1
    return columns, rows, extra


def dot(a, b, contract):
    return lax.dot_general(a, b, (contract, ((), ())), preferred_element_type=F32)


def mm(a, b):
    return dot(a, b, ((1,), (0,)))


def layer_norm(wide):
    center = wide - jnp.mean(wide, axis=-1, keepdims=True)
    spread = jnp.mean(center * center, axis=-1, keepdims=True)
    return (center * lax.rsqrt(spread + norm_eps)).astype(BF)


def pack_kernel(pieces, x_ref, ids_ref, perm_ref, columns_ref, rows_ref, *piece_refs):
    ids = ids_ref[...].astype(F32).astype(BF)
    lines = jnp.sum(mm(ids, columns_ref[...]) * rows_ref[:WH], axis=0, keepdims=True)
    x = x_ref[...]
    segment = 0
    first = 0
    for ref, windows in zip(piece_refs, pieces, strict=True):
        height = ref.shape[0]
        packed = mm(perm_ref[first : first + height], x)
        first += height
        bottom = [jnp.zeros((12, SPAN), F32)]
        for window in range(4):
            if window in windows:
                bottom.append(lines[:, segment * SPAN : (segment + 1) * SPAN])
                segment += 1
            else:
                bottom.append(jnp.zeros((1, SPAN), F32))
        bottom = jnp.concatenate(bottom, axis=0)
        bottom = jnp.concatenate([bottom, jnp.zeros((16, D - SPAN), F32)], axis=1)
        ref[: height - 16] = packed[: height - 16].astype(BF)
        ref[height - 16 :] = (packed[height - 16 :] + bottom).astype(BF)


def attention_kernel(
    flag_ref, extra_ref, main_ref, north_ref, west_ref, corner_ref, wqkv_ref, wout_ref,
    main_out, north_out, west_out, corner_out, proj, context,
):
    pieces = (main_ref, north_ref, west_ref, corner_ref)
    wide = jnp.concatenate([ref[...].astype(F32) for ref in pieces], axis=0)
    proj[...] = mm(layer_norm(wide), wqkv_ref[...])
    lines = sum(ref[ref.shape[0] - 16 :, :SPAN].astype(F32) for ref in pieces)[12:]
    lines = lines + extra_ref[:4] + jnp.where(flag_ref[0, 0] > 0, extra_ref[4:], 0.0)
    lines = jnp.concatenate([lines, lines], axis=0)
    i = lax.broadcasted_iota(jnp.int32, (SPAN, SPAN), 0)
    j = lax.broadcasted_iota(jnp.int32, (SPAN, SPAN), 1)
    standing = dot((i == j).astype(F32).astype(BF), lines.astype(BF), ((1,), (1,)))
    n, w, c = MAIN, 2 * MAIN, 2 * MAIN + SIDE
    windows = (
        (0, 144, ((0, 72), (n, 72))),
        (1, 144, ((72, 72), (n + 72, 72))),
        (2, 160, ((144, 40), (n + 144, 40), (w, 40), (c, 40))),
        (3, 160, ((184, 40), (n + 184, 40), (w + 40, 40), (c + 40, 40))),
    )
    low = lax.broadcasted_iota(jnp.int32, (1, LANES), 1) < D // HEADS
    for index, size, parts in windows:
        allowed = standing[:size, index : index + 1] == lines[index : index + 1, :size]
        bias = jnp.where(allowed, 0.0, -jnp.inf)
        bias = jnp.concatenate([bias, bias], axis=0)

        def take(start):
            return jnp.concatenate([proj[at : at + count, start : start + LANES] for at, count in parts], axis=0)

        for pair in range(HEADS // 2):
            lane = pair * LANES
            query = take(lane).astype(BF).astype(F32) * 0.125
            key = take(D + lane).astype(BF)
            value = take(2 * D + lane).astype(BF)
            both = jnp.concatenate([jnp.where(low, query, 0.0), jnp.where(low, 0.0, query)], axis=0).astype(BF)
            scores = dot(both, key, ((1,), (1,))) + bias
            weights = jnp.exp(scores - jnp.max(scores, axis=-1, keepdims=True))
            scale = 1.0 / jnp.sum(weights, axis=-1, keepdims=True)
            mixed = mm(weights.astype(BF), value) * scale
            result = jnp.where(low, mixed[:size], mixed[size:])
            start = 0
            for at, count in parts:
                context[at : at + count, lane : lane + LANES] = result[start : start + count]
                start += count
    mixed = wide + mm(context[...].astype(BF), wout_ref[...])
    mixed = mixed.astype(BF)
    main_out[...] = mixed[:n]
    north_out[...] = mixed[n:w]
    west_out[...] = mixed[w:c]
    corner_out[...] = mixed[c:]


def shift_matrix(offset, width):
    i = lax.broadcasted_iota(jnp.int32, (width, LANES), 0)
    j = lax.broadcasted_iota(jnp.int32, (width, LANES), 1)
    return ((i - offset == j) & (j < OUTS)).astype(F32).astype(BF)


def spot(level):
    first = level * OUTS // LANES * LANES
    return first, level * OUTS - first, min(2 * LANES, PLEV * OUTS - first)


def spread_queries(queries):
    parts = [jnp.broadcast_to(queries[a : a + 1], (HEADS, D)) for a in range(PLEV)]
    parts.append(jnp.zeros((LANES - HEADS * PLEV, D), F32))
    tall = jnp.concatenate(parts, axis=0)
    c = lax.broadcasted_iota(jnp.int32, (LANES, D), 0)
    j = lax.broadcasted_iota(jnp.int32, (LANES, D), 1)
    return jnp.where(c % HEADS == j // (D // HEADS), tall, 0.0)


def feature_order():
    j = lax.broadcasted_iota(jnp.int32, (D, D), 0)
    lane = lax.broadcasted_iota(jnp.int32, (D, D), 1)
    size = D // HEADS
    wanted = j % size // 16 * LANES + j // size * 16 + j % 16
    return jnp.where(wanted == lane, 1.0, 0.0).astype(BF)


def pre_kernel(
    cot_ref, queries_ref, wo_ref, whead_ref, wkv_ref,
    up_ref, dctx_ref, dsum_ref, map_ref, base_ref, wv_ref, order_ref,
):
    order = feature_order()
    order_ref[...] = order
    wv_ref[...] = mm(wkv_ref[:, D:], order).astype(BF)
    head = whead_ref[...]
    both = dot(wo_ref[...], head, ((1,), (1,))).astype(BF)
    both = dot(order, both, ((0,), (0,))).astype(BF)
    map_ref[...] = both
    base_ref[...] = jnp.concatenate(
        [dot(queries_ref[...], head, ((1,), (1,))), jnp.zeros((16 - PLEV, LANES), F32)], axis=0
    )
    dsum = jnp.zeros((PATCHES, D), F32)
    for level in range(PLEV):
        first, offset, width = spot(level)
        up = mm(cot_ref[:, first : first + width], shift_matrix(offset, width)).astype(BF)
        up_ref[level] = up
        dctx = dot(up, both, ((1,), (1,))).astype(BF)
        dctx_ref[level] = dctx
        dsum = dsum + dctx.astype(F32)
    dsum_ref[...] = dsum


def decode_kernel(
    flag_ref, main_ref, north_ref, west_ref, corner_ref, perm_ref, wkv_ref, queries_ref, up_ref, dctx_ref, dsum_ref,
    map_ref, base_ref, wv_ref,
    owned_ref, fields_ref, keep_ref, send_ref,
    value, weights, dvalues, context, products, fields, sums,
):
    pieces = (main_ref, north_ref, west_ref, corner_ref)
    packed = jnp.concatenate([ref[...] for ref in pieces], axis=0)
    wide = mm(perm_ref[...], packed)
    owned_ref[...] = wide.astype(BF)
    normed = layer_norm(wide)
    key = mm(normed, wkv_ref[:, :D]).astype(BF)
    value[...] = mm(normed, wv_ref[...]).astype(BF).astype(F32)
    queries = spread_queries(queries_ref[...].astype(F32)).astype(BF)
    scores = dot(key, queries, ((1,), (1,))) * 0.125
    slabs = [scores[l * PATCHES : (l + 1) * PATCHES] for l in range(LEV)]
    top = jnp.maximum(jnp.maximum(slabs[0], slabs[1]), jnp.maximum(slabs[2], slabs[3]))
    slabs = [jnp.exp(s - top) for s in slabs]
    scale = 1.0 / (slabs[0] + slabs[1] + slabs[2] + slabs[3])
    slabs = [s * scale for s in slabs]
    for l in range(LEV):
        weights[l * PATCHES : (l + 1) * PATCHES] = slabs[l]
    head_of = lax.broadcasted_iota(jnp.int32, (BLOCK, LANES), 1) // 16
    for start in range(0, PATCHES, BLOCK):
        at = [slice(l * PATCHES + start, l * PATCHES + start + BLOCK) for l in range(LEV)]
        last = value[at[LEV - 1]]
        gaps = [value[at[l]] - last for l in range(LEV - 1)]
        heads = [weights[at[l]] for l in range(LEV - 1)]
        found = [jnp.zeros((BLOCK, D), F32) for _ in range(LEV - 1)]
        for level in range(PLEV):
            index = head_of + level * HEADS
            upstream = dctx_ref[level, start : start + BLOCK].astype(F32)
            total = last
            for l in range(LEV - 1):
                spread = jnp.take_along_axis(heads[l], index, axis=1)
                spread = jnp.concatenate([spread] * (D // LANES), axis=1)
                total = total + spread * gaps[l]
                found[l] = found[l] + spread * upstream
                product = upstream * gaps[l]
                folded = (product[:, :LANES] + product[:, LANES : 2 * LANES]) + (
                    product[:, 2 * LANES : 3 * LANES] + product[:, 3 * LANES :]
                )
                products[at[l], level * LANES : (level + 1) * LANES] = folded.astype(BF)
            context[level * PATCHES + start : level * PATCHES + start + BLOCK] = total.astype(BF)
        for l in range(LEV - 1):
            dvalues[at[l]] = found[l]
        dvalues[at[LEV - 1]] = dsum_ref[start : start + BLOCK] - (found[0] + found[1] + found[2])
    fields[...] = jnp.zeros_like(fields)
    row = lax.broadcasted_iota(jnp.int32, (PLEV * LANES, LANES), 0)
    c = lax.broadcasted_iota(jnp.int32, (PLEV * LANES, LANES), 1)
    slopes = mm(products[...], jnp.where(row // 16 == c, 1.0, 0.0).astype(BF))
    for level in range(PLEV):
        first, offset, width = spot(level)
        decoded = mm(context[level * PATCHES : (level + 1) * PATCHES], map_ref[...]) + base_ref[level : level + 1]
        fields[:, first : first + width] += dot(decoded.astype(BF), shift_matrix(offset, width), ((1,), (1,)))
    fields_ref[...] = fields[...].astype(BF)
    slopes = [slopes[l * PATCHES : (l + 1) * PATCHES] for l in range(LEV - 1)]
    mean = sum(p * d for p, d in zip(slabs, slopes))
    dscores = [p * (d - mean) * 0.125 for p, d in zip(slabs, slopes)]
    dscores.append(slabs[LEV - 1] * mean * -0.125)
    dscores = jnp.concatenate(dscores, axis=0).astype(BF)
    sums[:D] = dot(normed, dvalues[...].astype(BF), ((0,), (0,)))
    sums[D : D + LANES] = dot(dscores, normed, ((0,), (0,)))
    up = jnp.concatenate([up_ref[a] for a in range(PLEV)], axis=0)
    outer = dot(up, context[...], ((0,), (0,)))
    sums[D + LANES : D + LANES + OUTS] = outer[:OUTS]
    totals = [jnp.sum(up_ref[a].astype(F32), axis=0, keepdims=True) for a in range(PLEV)]
    totals.append(jnp.zeros((LANES - OUTS - PLEV, LANES), F32))
    totals = jnp.concatenate(totals, axis=0)
    sums[D + LANES + OUTS :] = jnp.concatenate([totals, jnp.zeros((LANES - OUTS, D - LANES), F32)], axis=1)
    second = flag_ref[0, 0] > 0
    top, bottom = sums[: ROWS // 2], sums[ROWS // 2 :]
    keep_ref[...] = jnp.where(second, bottom, top).astype(BF)
    send_ref[...] = jnp.where(second, top, bottom).astype(BF)


def add_kernel(left_ref, right_ref, out_ref):
    out_ref[...] = (left_ref[...].astype(F32) + right_ref[...].astype(F32)).astype(BF)


def final_kernel(flag_ref, mine_ref, other_ref, order_ref, wkv_ref, queries_ref, wo_ref, whead_ref, kv_ref, query_ref, o_ref, head_ref):
    second = flag_ref[0, 0] > 0
    mine, other = mine_ref[...].astype(F32), other_ref[...].astype(F32)
    sums = jnp.concatenate([jnp.where(second, other, mine), jnp.where(second, mine, other)], axis=0).astype(BF)
    queries = queries_ref[...]
    head = whead_ref[...]
    keyed = sums[D : D + LANES]
    outer = sums[D + LANES :]
    level_sums = outer[OUTS : OUTS + 16, :LANES]
    spread = spread_queries(queries.astype(F32)).astype(BF)
    values = dot(sums[:D], order_ref[...], ((1,), (1,)))
    keys = dot(keyed, spread, ((0,), (0,)))
    c = lax.broadcasted_iota(jnp.int32, (LANES, D), 0)
    j = lax.broadcasted_iota(jnp.int32, (LANES, D), 1)
    grouped = jnp.where(c % HEADS == j // (D // HEADS), mm(keyed, wkv_ref[:, :D]), 0.0)
    grouped = jnp.sum(grouped.reshape(LANES // HEADS, HEADS, D), axis=1)
    level = grouped[:PLEV] + mm(level_sums, head)[:PLEV]
    clean = dot(outer[:OUTS], order_ref[...], ((1,), (1,))).astype(BF)
    out = dot(clean, head[:OUTS], ((0,), (0,)))
    pixels = mm(clean, wo_ref[...])
    pixels = pixels + dot(level_sums[:PLEV, :OUTS], queries, ((0,), (0,)))
    squares = jnp.sum(values * values) + jnp.sum(keys * keys) + jnp.sum(level * level)
    squares = squares + jnp.sum(out * out) + jnp.sum(pixels * pixels)
    limit = math.sqrt(2 * D * D + PLEV * D + D * D + D * OUTS)
    factor = jnp.minimum(1.0, limit * lax.rsqrt(jnp.full((1, 1), squares + clip_eps, F32)))
    kv_ref[:, :D] = keys * factor
    kv_ref[:, D:] = values * factor
    query_ref[...] = level * factor
    o_ref[...] = out * factor
    head_ref[...] = pixels * factor


def call(kernel, outs, spaces, scratch=(), limit=40):
    where = {"V": pltpu.VMEM, "H": pltpu.HBM}
    whole, scalar = pl.BlockSpec(memory_space=pltpu.VMEM), pl.BlockSpec(memory_space=pltpu.SMEM)
    run = pl.pallas_call(
        kernel,
        in_specs=[scalar if space == "S" else whole for space in spaces],
        out_shape=outs,
        scratch_shapes=list(scratch),
        compiler_params=pltpu.CompilerParams(vmem_limit_bytes=limit * 2**20),
    )

    def close(*operands):
        held = [
            pltpu.with_memory_space_constraint(x, where[space]) if space in where else x
            for space, x in zip(spaces, operands, strict=True)
        ]
        return run(*held)

    return close


def struct(shape, dtype=BF):
    return jax.ShapeDtypeStruct(shape, dtype)


def far_struct(shape, dtype=BF):
    return pltpu.HBM(shape, dtype)


def move(array, lat_step, lon_step):
    lats, lons = lax.axis_size(LAT), lax.axis_size(LON)
    route = [
        (i * lons + j, (i + lat_step) % lats * lons + (j + lon_step) % lons)
        for i in range(lats)
        for j in range(lons)
    ]
    return lax.ppermute(array, LAT + LON, route)


def swap(array):
    count = lax.axis_size("core")
    return lax.ppermute(array, "core", [(i, (i + 1) % count) for i in range(count)])


def add_up(blocks):
    return jnp.sum(blocks.astype(F32), axis=0).astype(BF)


def copies(block, axes):
    return jnp.broadcast_to(block[None], (lax.axis_size(axes),) + block.shape)


def sum_over_all(keep, send):
    rows, width = keep.shape
    mine = call(add_kernel, struct((rows, width)), "VV", limit=8)(keep, swap(send))
    chips = lax.axis_size(PLANE)
    mine = add_up(lax.all_to_all(mine.reshape(chips, rows // chips, width), PLANE, 0, 0, tiled=True))
    mine = lax.psum(mine, "z")
    mine = lax.all_to_all(copies(mine, PLANE), PLANE, 0, 0, tiled=True).reshape(rows, width)
    return mine, swap(mine)


def per_device(latents, mask_ids, w_qkv, w_out, w_kv, level_queries, w_o, w_head, field_cotangent):
    perm = pack_matrix()
    columns, rows, extra = label_tables()
    flag = (lax.axis_index(LAT) == lax.axis_size(LAT) - 1).astype(jnp.int32).reshape(1, 1)
    shapes = [far_struct((MAIN, D)), struct((MAIN, D)), struct((SIDE, D)), struct((SIDE, D))]
    split = 4 * SPAN
    flat = latents.reshape(TOKENS, D)
    north, west, corner = call(functools.partial(pack_kernel, PIECES[1:]), shapes[1:], "HHHHH", limit=56)(
        flat, mask_ids, jnp.asarray(perm[MAIN:], BF), jnp.asarray(columns[:, split:], BF), jnp.asarray(rows[:, split:])
    )
    (main,) = call(functools.partial(pack_kernel, PIECES[:1]), shapes[:1], "HHHHH", limit=56)(
        flat, mask_ids, jnp.asarray(perm[:MAIN], BF), jnp.asarray(columns[:, :split], BF), jnp.asarray(rows[:, :split])
    )
    north, west, corner = move(north, -1, 0), move(west, 0, -1), move(corner, -1, -1)
    head = jnp.pad(w_head.T, ((0, LANES - OUTS), (0, 0)))
    up, dctx, dsum, both, base, wv, feature = call(
        pre_kernel,
        [
            struct((PLEV, PATCHES, LANES)),
            struct((PLEV, PATCHES, D)),
            struct((PATCHES, D), F32),
            struct((D, LANES)),
            struct((16, LANES), F32),
            struct((D, D)),
            far_struct((D, D)),
        ],
        "VVVVV",
    )(field_cotangent.reshape(PATCHES, PLEV * OUTS), level_queries, w_o, head, w_kv)
    main, north, west, corner = call(
        attention_kernel,
        shapes,
        "SHHHHHVH",
        [pltpu.VMEM((PACKED, 3 * D), F32), pltpu.VMEM((PACKED, D), F32)],
        limit=48,
    )(flag, jnp.asarray(extra), main, north, west, corner, w_qkv, w_out)
    north, west, corner = move(north, 1, 0), move(west, 0, 1), move(corner, 1, 1)
    core = lax.axis_index("core").astype(jnp.int32).reshape(1, 1)
    share = struct((ROWS // 2, D))
    owned, fields, keep, send = call(
        decode_kernel,
        [struct((TOKENS, D)), struct((PATCHES, PLEV * OUTS)), share, share],
        "SHVVVHVVVVVVVV",
        [
            pltpu.VMEM((TOKENS, D), F32),
            pltpu.VMEM((TOKENS, LANES), F32),
            pltpu.VMEM((TOKENS, D), F32),
            pltpu.VMEM((PLEV * PATCHES, D), BF),
            pltpu.VMEM(((LEV - 1) * PATCHES, PLEV * LANES), BF),
            pltpu.VMEM((PATCHES, PLEV * OUTS), F32),
            pltpu.VMEM((ROWS, D), F32),
        ],
    )(core, main, north, west, corner, jnp.asarray(perm.T, BF), w_kv, level_queries, up, dctx, dsum, both, base, wv)
    mine, other = sum_over_all(keep, send)
    kv, query, out, pixels = call(
        final_kernel,
        [struct((D, 2 * D), F32), struct((PLEV, D), F32), struct((D, D), F32), struct((OUTS, D), F32)],
        "SVVHVVVV",
    )(core, mine, other, feature, w_kv, level_queries, w_o, head)
    shape = latents.shape
    return (owned.reshape(shape), fields.reshape(shape[1], shape[2], PLEV * OUTS), kv, query, out, pixels.T)


def solution(mesh):
    lats, lons = mesh.shape["lat"], mesh.shape["lon"]
    sizes = (lats // 2, 2, 2, lons // 4, 2)
    fine = jax.sharding.Mesh(mesh.devices.reshape(sizes), LAT + LON)
    in_specs = (
        P(None, LAT, LON, None),
        P(LAT, LON),
        P(),
        P(),
        P(),
        P(),
        P(),
        P(),
        P(LAT, LON, None),
    )
    out_specs = (P(None, LAT, LON, None), P(LAT, LON, None), P(), P(), P(), P())
    return jax.shard_map(per_device, mesh=fine, in_specs=in_specs, out_specs=out_specs, check_vma=False)
```

```python
import functools
import math

import jax
import jax.numpy as jnp
import numpy as np
from jax import lax
from jax.experimental import pallas as pl
from jax.experimental.pallas import tpu as pltpu
from jax.sharding import PartitionSpec as P

D = 512
HEADS = 8
LEV = 4
PLEV = 13
OUTS = 80
WL = 2
WH = 6
WW = 12
PATCHES = WH * 2 * WW
TOKENS = LEV * PATCHES
MAIN = 224
SIDE = 80
PACKED = 2 * MAIN + 2 * SIDE
ROWS = 768
BLOCK = 16
LANES = 128

SPAN = 256
PIECES = (
    {0: (0, 72, 0), 1: (72, 72, 0), 2: (144, 40, 0), 3: (184, 40, 0)},
    {0: (224, 72, 72), 1: (296, 72, 72), 2: (368, 40, 40), 3: (408, 40, 40)},
    {2: (448, 40, 80), 3: (488, 40, 80)},
    {2: (528, 40, 120), 3: (568, 40, 120)},
)

LAT = ("z", "x_hi")
LON = ("x_lo", "y", "core")
PLANE = ("x_hi", "x_lo", "y")

norm_eps = 1e-05
clip_eps = 1e-06
BF = jnp.bfloat16
F32 = jnp.float32


def window_order():
    level_pairs = ((1, 2), (3, 0))

    def rows_of(levels, rows, cols):
        return [(l * WH + r) * 2 * WW + c for l in levels for r in rows for c in cols]

    order = []
    for rows in ((3, 4, 5), (0, 1, 2)):
        for pair in level_pairs:
            order += rows_of(pair, rows, range(6, 18))
        for pair in level_pairs:
            order += rows_of(pair, rows, range(18, 24)) + [-1] * 4
    for rows in ((3, 4, 5), (0, 1, 2)):
        for pair in level_pairs:
            order += rows_of(pair, rows, range(0, 6)) + [-1] * 4
    return np.array(order)


def pack_matrix():
    order = window_order()
    return (order[:, None] == np.arange(TOKENS)[None, :]).astype(np.float32)


def label_tables():
    order = window_order()
    row, col, level = order // (2 * WW) % WH, order % (2 * WW), order // PATCHES
    columns = np.zeros((2 * WW, 12 * SPAN), np.float32)
    rows = np.zeros((8, 12 * SPAN), np.float32)
    extra = np.zeros((8, SPAN), np.float32)
    segment = 0
    for starts, far in zip(PIECES, (False, True, False, True)):
        for window, (at, count, place) in starts.items():
            for i in range(count):
                lane, token = place + i, at + i
                if order[token] < 0:
                    extra[window, lane] = -1
                    continue
                columns[col[token], segment * SPAN + lane] = 1
                rows[row[token], segment * SPAN + lane] = 1
                extra[window, lane] = 8 * (level[token] == 0)
                extra[4 + window, lane] = 4 * far
            segment += 1
    return columns, rows, extra


def dot(a, b, contract):
    return lax.dot_general(a, b, (contract, ((), ())), preferred_element_type=F32)


def mm(a, b):
    return dot(a, b, ((1,), (0,)))


def layer_norm(wide):
    center = wide - jnp.mean(wide, axis=-1, keepdims=True)
    spread = jnp.mean(center * center, axis=-1, keepdims=True)
    return (center * lax.rsqrt(spread + norm_eps)).astype(BF)


def pack_kernel(pieces, x_ref, ids_ref, perm_ref, columns_ref, rows_ref, *piece_refs):
    ids = ids_ref[...].astype(F32).astype(BF)
    lines = jnp.sum(mm(ids, columns_ref[...]) * rows_ref[:WH], axis=0, keepdims=True)
    x = x_ref[...]
    segment = 0
    first = 0
    for ref, windows in zip(piece_refs, pieces, strict=True):
        height = ref.shape[0]
        packed = mm(perm_ref[first : first + height], x)
        first += height
        bottom = [jnp.zeros((12, SPAN), F32)]
        for window in range(4):
            if window in windows:
                bottom.append(lines[:, segment * SPAN : (segment + 1) * SPAN])
                segment += 1
            else:
                bottom.append(jnp.zeros((1, SPAN), F32))
        bottom = jnp.concatenate(bottom, axis=0)
        bottom = jnp.concatenate([bottom, jnp.zeros((16, D - SPAN), F32)], axis=1)
        ref[: height - 16] = packed[: height - 16].astype(BF)
        ref[height - 16 :] = (packed[height - 16 :] + bottom).astype(BF)


def attention_kernel(
    flag_ref, extra_ref, main_ref, north_ref, west_ref, corner_ref, wqkv_ref, wout_ref,
    main_out, north_out, west_out, corner_out, proj, context,
):
    pieces = (main_ref, north_ref, west_ref, corner_ref)
    wide = jnp.concatenate([ref[...].astype(F32) for ref in pieces], axis=0)
    proj[...] = mm(layer_norm(wide), wqkv_ref[...])
    lines = sum(ref[ref.shape[0] - 16 :, :SPAN].astype(F32) for ref in pieces)[12:]
    lines = lines + extra_ref[:4] + jnp.where(flag_ref[0, 0] > 0, extra_ref[4:], 0.0)
    lines = jnp.concatenate([lines, lines], axis=0)
    i = lax.broadcasted_iota(jnp.int32, (SPAN, SPAN), 0)
    j = lax.broadcasted_iota(jnp.int32, (SPAN, SPAN), 1)
    standing = dot((i == j).astype(F32).astype(BF), lines.astype(BF), ((1,), (1,)))
    n, w, c = MAIN, 2 * MAIN, 2 * MAIN + SIDE
    windows = (
        (0, 144, ((0, 72), (n, 72))),
        (1, 144, ((72, 72), (n + 72, 72))),
        (2, 160, ((144, 40), (n + 144, 40), (w, 40), (c, 40))),
        (3, 160, ((184, 40), (n + 184, 40), (w + 40, 40), (c + 40, 40))),
    )
    low = lax.broadcasted_iota(jnp.int32, (1, LANES), 1) < D // HEADS
    for index, size, parts in windows:
        allowed = standing[:size, index : index + 1] == lines[index : index + 1, :size]
        bias = jnp.where(allowed, 0.0, -jnp.inf)
        bias = jnp.concatenate([bias, bias], axis=0)

        def take(start):
            return jnp.concatenate([proj[at : at + count, start : start + LANES] for at, count in parts], axis=0)

        for pair in range(HEADS // 2):
            lane = pair * LANES
            query = take(lane).astype(BF).astype(F32) * 0.125
            key = take(D + lane).astype(BF)
            value = take(2 * D + lane).astype(BF)
            both = jnp.concatenate([jnp.where(low, query, 0.0), jnp.where(low, 0.0, query)], axis=0).astype(BF)
            scores = dot(both, key, ((1,), (1,))) + bias
            weights = jnp.exp(scores - jnp.max(scores, axis=-1, keepdims=True))
            scale = 1.0 / jnp.sum(weights, axis=-1, keepdims=True)
            mixed = mm(weights.astype(BF), value) * scale
            result = jnp.where(low, mixed[:size], mixed[size:])
            start = 0
            for at, count in parts:
                context[at : at + count, lane : lane + LANES] = result[start : start + count]
                start += count
    mixed = wide + mm(context[...].astype(BF), wout_ref[...])
    mixed = mixed.astype(BF)
    main_out[...] = mixed[:n]
    north_out[...] = mixed[n:w]
    west_out[...] = mixed[w:c]
    corner_out[...] = mixed[c:]


def shift_matrix(offset, width):
    i = lax.broadcasted_iota(jnp.int32, (width, LANES), 0)
    j = lax.broadcasted_iota(jnp.int32, (width, LANES), 1)
    return ((i - offset == j) & (j < OUTS)).astype(F32).astype(BF)


def spot(level):
    first = level * OUTS // LANES * LANES
    return first, level * OUTS - first, min(2 * LANES, PLEV * OUTS - first)


def spread_queries(queries):
    parts = [jnp.broadcast_to(queries[a : a + 1], (HEADS, D)) for a in range(PLEV)]
    parts.append(jnp.zeros((LANES - HEADS * PLEV, D), F32))
    tall = jnp.concatenate(parts, axis=0)
    c = lax.broadcasted_iota(jnp.int32, (LANES, D), 0)
    j = lax.broadcasted_iota(jnp.int32, (LANES, D), 1)
    return jnp.where(c % HEADS == j // (D // HEADS), tall, 0.0)


def lane_of(j):
    size = D // HEADS
    return j % size // 16 * LANES + j // size * 16 + j % 16


def feature_order():
    wanted = lane_of(lax.broadcasted_iota(jnp.int32, (D, LANES), 0))
    lane = lax.broadcasted_iota(jnp.int32, (D, LANES), 1)
    tiles = [jnp.where(wanted == lane + start, 1.0, 0.0) for start in range(0, D, LANES)]
    return jnp.concatenate(tiles, axis=1).astype(BF)


def natural_order():
    wanted = lane_of(lax.broadcasted_iota(jnp.int32, (8, D), 1))
    lane = lax.broadcasted_iota(jnp.int32, (8, D), 0)
    tiles = [jnp.where(wanted == lane + start, 1.0, 0.0) for start in range(0, D, 8)]
    return jnp.concatenate(tiles, axis=0).astype(BF)


def pre_kernel(
    cot_ref, queries_ref, wo_ref, whead_ref, wkv_ref,
    up_ref, dctx_ref, dsum_ref, map_ref, base_ref, wv_ref,
):
    order = feature_order()
    wv_ref[...] = mm(wkv_ref[:, D:], order).astype(BF)
    head = whead_ref[...]
    both = dot(wo_ref[...], head, ((1,), (1,))).astype(BF)
    both = dot(order, both, ((0,), (0,))).astype(BF)
    map_ref[...] = both
    base_ref[...] = jnp.concatenate(
        [dot(queries_ref[...], head, ((1,), (1,))), jnp.zeros((16 - PLEV, LANES), F32)], axis=0
    )
    dsum = jnp.zeros((PATCHES, D), F32)
    for level in range(PLEV):
        first, offset, width = spot(level)
        up = mm(cot_ref[:, first : first + width], shift_matrix(offset, width)).astype(BF)
        up_ref[level] = up
        dctx = dot(up, both, ((1,), (1,))).astype(BF)
        dctx_ref[level] = dctx
        dsum = dsum + dctx.astype(F32)
    dsum_ref[...] = dsum


def decode_kernel(
    flag_ref, main_ref, north_ref, west_ref, corner_ref, perm_ref, wkv_ref, queries_ref, up_ref, dctx_ref, dsum_ref,
    map_ref, base_ref, wv_ref,
    owned_ref, fields_ref, keep_ref, send_ref,
    value, weights, dvalues, context, products, fields, sums, owned, decoded_out, sems,
):
    pieces = (main_ref, north_ref, west_ref, corner_ref)
    packed = jnp.concatenate([ref[...] for ref in pieces], axis=0)
    wide = mm(perm_ref[...], packed)
    owned[...] = wide.astype(BF)
    owned_copy = pltpu.make_async_copy(owned, owned_ref, sems.at[0])
    owned_copy.start()
    normed = layer_norm(wide)
    key = mm(normed, wkv_ref[:, :D]).astype(BF)
    value[...] = mm(normed, wv_ref[...]).astype(BF).astype(F32)
    queries = spread_queries(queries_ref[...].astype(F32)).astype(BF)
    scores = dot(key, queries, ((1,), (1,))) * 0.125
    slabs = [scores[l * PATCHES : (l + 1) * PATCHES] for l in range(LEV)]
    top = jnp.maximum(jnp.maximum(slabs[0], slabs[1]), jnp.maximum(slabs[2], slabs[3]))
    slabs = [jnp.exp(s - top) for s in slabs]
    scale = 1.0 / (slabs[0] + slabs[1] + slabs[2] + slabs[3])
    slabs = [s * scale for s in slabs]
    for l in range(LEV):
        weights[l * PATCHES : (l + 1) * PATCHES] = slabs[l]
    head_of = lax.broadcasted_iota(jnp.int32, (BLOCK, LANES), 1) // 16
    for start in range(0, PATCHES, BLOCK):
        at = [slice(l * PATCHES + start, l * PATCHES + start + BLOCK) for l in range(LEV)]
        last = value[at[LEV - 1]]
        gaps = [value[at[l]] - last for l in range(LEV - 1)]
        heads = [weights[at[l]] for l in range(LEV - 1)]
        found = [jnp.zeros((BLOCK, D), F32) for _ in range(LEV - 1)]
        for level in range(PLEV):
            index = head_of + level * HEADS
            upstream = dctx_ref[level, start : start + BLOCK].astype(F32)
            total = last
            for l in range(LEV - 1):
                spread = jnp.take_along_axis(heads[l], index, axis=1)
                spread = jnp.concatenate([spread] * (D // LANES), axis=1)
                total = total + spread * gaps[l]
                found[l] = found[l] + spread * upstream
                product = upstream * gaps[l]
                folded = (product[:, :LANES] + product[:, LANES : 2 * LANES]) + (
                    product[:, 2 * LANES : 3 * LANES] + product[:, 3 * LANES :]
                )
                products[at[l], level * LANES : (level + 1) * LANES] = folded.astype(BF)
            context[level * PATCHES + start : level * PATCHES + start + BLOCK] = total.astype(BF)
        for l in range(LEV - 1):
            dvalues[at[l]] = found[l]
        dvalues[at[LEV - 1]] = dsum_ref[start : start + BLOCK] - (found[0] + found[1] + found[2])
    fields[...] = jnp.zeros_like(fields)
    row = lax.broadcasted_iota(jnp.int32, (PLEV * LANES, LANES), 0)
    c = lax.broadcasted_iota(jnp.int32, (PLEV * LANES, LANES), 1)
    slopes = mm(products[...], jnp.where(row // 16 == c, 1.0, 0.0).astype(BF))
    for level in range(PLEV):
        first, offset, width = spot(level)
        decoded = mm(context[level * PATCHES : (level + 1) * PATCHES], map_ref[...]) + base_ref[level : level + 1]
        fields[:, first : first + width] += dot(decoded.astype(BF), shift_matrix(offset, width), ((1,), (1,)))
    decoded_out[...] = fields[...].astype(BF)
    fields_copy = pltpu.make_async_copy(decoded_out, fields_ref, sems.at[1])
    fields_copy.start()
    slopes = [slopes[l * PATCHES : (l + 1) * PATCHES] for l in range(LEV - 1)]
    mean = sum(p * d for p, d in zip(slabs, slopes))
    dscores = [p * (d - mean) * 0.125 for p, d in zip(slabs, slopes)]
    dscores.append(slabs[LEV - 1] * mean * -0.125)
    dscores = jnp.concatenate(dscores, axis=0).astype(BF)
    sums[:D] = dot(normed, dvalues[...].astype(BF), ((0,), (0,)))
    sums[D : D + LANES] = dot(dscores, normed, ((0,), (0,)))
    up = jnp.concatenate([up_ref[a] for a in range(PLEV)], axis=0)
    outer = dot(up, context[...], ((0,), (0,)))
    sums[D + LANES : D + LANES + OUTS] = outer[:OUTS]
    totals = [jnp.sum(up_ref[a].astype(F32), axis=0, keepdims=True) for a in range(PLEV)]
    totals.append(jnp.zeros((LANES - OUTS - PLEV, LANES), F32))
    totals = jnp.concatenate(totals, axis=0)
    sums[D + LANES + OUTS :] = jnp.concatenate([totals, jnp.zeros((LANES - OUTS, D - LANES), F32)], axis=1)
    second = flag_ref[0, 0] > 0
    top, bottom = sums[: ROWS // 2], sums[ROWS // 2 :]
    keep_ref[...] = jnp.where(second, bottom, top).astype(BF)
    send_ref[...] = jnp.where(second, top, bottom).astype(BF)
    owned_copy.wait()
    fields_copy.wait()


def add_kernel(left_ref, right_ref, out_ref):
    out_ref[...] = (left_ref[...].astype(F32) + right_ref[...].astype(F32)).astype(BF)


def final_kernel(flag_ref, mine_ref, other_ref, wkv_ref, queries_ref, wo_ref, whead_ref, kv_ref, query_ref, o_ref, head_ref):
    second = flag_ref[0, 0] > 0
    mine, other = mine_ref[...].astype(F32), other_ref[...].astype(F32)
    sums = jnp.concatenate([jnp.where(second, other, mine), jnp.where(second, mine, other)], axis=0).astype(BF)
    queries = queries_ref[...]
    head = whead_ref[...]
    keyed = sums[D : D + LANES]
    outer = sums[D + LANES :]
    level_sums = outer[OUTS : OUTS + 16, :LANES]
    spread = spread_queries(queries.astype(F32)).astype(BF)
    natural = natural_order()
    values = mm(sums[:D], natural)
    keys = dot(keyed, spread, ((0,), (0,)))
    c = lax.broadcasted_iota(jnp.int32, (LANES, D), 0)
    j = lax.broadcasted_iota(jnp.int32, (LANES, D), 1)
    grouped = jnp.where(c % HEADS == j // (D // HEADS), mm(keyed, wkv_ref[:, :D]), 0.0)
    grouped = jnp.sum(grouped.reshape(LANES // HEADS, HEADS, D), axis=1)
    level = grouped[:PLEV] + mm(level_sums, head)[:PLEV]
    clean = mm(outer[:OUTS], natural).astype(BF)
    out = dot(clean, head[:OUTS], ((0,), (0,)))
    pixels = mm(clean, wo_ref[...])
    pixels = pixels + dot(level_sums[:PLEV, :OUTS], queries, ((0,), (0,)))
    squares = jnp.sum(values * values) + jnp.sum(keys * keys) + jnp.sum(level * level)
    squares = squares + jnp.sum(out * out) + jnp.sum(pixels * pixels)
    limit = math.sqrt(2 * D * D + PLEV * D + D * D + D * OUTS)
    factor = jnp.minimum(1.0, limit * lax.rsqrt(jnp.full((1, 1), squares + clip_eps, F32)))
    kv_ref[:, :D] = keys * factor
    kv_ref[:, D:] = values * factor
    query_ref[...] = level * factor
    o_ref[...] = out * factor
    head_ref[...] = pixels * factor


def call(kernel, outs, spaces, scratch=(), limit=40, out_specs=None):
    where = {"V": pltpu.VMEM, "H": pltpu.HBM}
    whole, scalar = pl.BlockSpec(memory_space=pltpu.VMEM), pl.BlockSpec(memory_space=pltpu.SMEM)
    more = {} if out_specs is None else {"out_specs": out_specs}
    run = pl.pallas_call(
        kernel,
        **more,
        in_specs=[scalar if space == "S" else whole for space in spaces],
        out_shape=outs,
        scratch_shapes=list(scratch),
        compiler_params=pltpu.CompilerParams(vmem_limit_bytes=limit * 2**20),
    )

    def close(*operands):
        held = [
            pltpu.with_memory_space_constraint(x, where[space]) if space in where else x
            for space, x in zip(spaces, operands, strict=True)
        ]
        return run(*held)

    return close


def struct(shape, dtype=BF):
    return jax.ShapeDtypeStruct(shape, dtype)


def far_struct(shape, dtype=BF):
    return pltpu.HBM(shape, dtype)


def move(array, lat_step, lon_step):
    lats, lons = lax.axis_size(LAT), lax.axis_size(LON)
    route = [
        (i * lons + j, (i + lat_step) % lats * lons + (j + lon_step) % lons)
        for i in range(lats)
        for j in range(lons)
    ]
    return lax.ppermute(array, LAT + LON, route)


def swap(array):
    count = lax.axis_size("core")
    return lax.ppermute(array, "core", [(i, (i + 1) % count) for i in range(count)])


def add_up(blocks):
    return jnp.sum(blocks.astype(F32), axis=0).astype(BF)


def copies(block, axes):
    return jnp.broadcast_to(block[None], (lax.axis_size(axes),) + block.shape)


def sum_over_all(keep, send):
    rows, width = keep.shape
    mine = call(add_kernel, struct((rows, width)), "VV", limit=8)(keep, swap(send))
    chips = lax.axis_size(PLANE)
    mine = add_up(lax.all_to_all(mine.reshape(chips, rows // chips, width), PLANE, 0, 0, tiled=True))
    mine = add_up(lax.all_to_all(copies(mine, "z"), "z", 0, 0, tiled=True))
    mine = lax.all_to_all(copies(mine, PLANE), PLANE, 0, 0, tiled=True).reshape(rows, width)
    return mine, swap(mine)


def per_device(latents, mask_ids, w_qkv, w_out, w_kv, level_queries, w_o, w_head, field_cotangent):
    perm = pack_matrix()
    columns, rows, extra = label_tables()
    flag = (lax.axis_index(LAT) == lax.axis_size(LAT) - 1).astype(jnp.int32).reshape(1, 1)
    shapes = [far_struct((MAIN, D)), struct((MAIN, D)), struct((SIDE, D)), struct((SIDE, D))]
    split = 4 * SPAN
    flat = latents.reshape(TOKENS, D)
    north, west, corner = call(functools.partial(pack_kernel, PIECES[1:]), shapes[1:], "HHHHH", limit=56)(
        flat, mask_ids, jnp.asarray(perm[MAIN:], BF), jnp.asarray(columns[:, split:], BF), jnp.asarray(rows[:, split:])
    )
    (main,) = call(functools.partial(pack_kernel, PIECES[:1]), shapes[:1], "HHHHH", limit=56)(
        flat, mask_ids, jnp.asarray(perm[:MAIN], BF), jnp.asarray(columns[:, :split], BF), jnp.asarray(rows[:, :split])
    )
    north, west, corner = move(north, -1, 0), move(west, 0, -1), move(corner, -1, -1)
    head = jnp.pad(w_head.T, ((0, LANES - OUTS), (0, 0)))
    up, dctx, dsum, both, base, wv = call(
        pre_kernel,
        [
            struct((PLEV, PATCHES, LANES)),
            struct((PLEV, PATCHES, D)),
            struct((PATCHES, D), F32),
            struct((D, LANES)),
            struct((16, LANES), F32),
            struct((D, D)),
        ],
        "VVVVV",
    )(field_cotangent.reshape(PATCHES, PLEV * OUTS), level_queries, w_o, head, w_kv)
    main, north, west, corner = call(
        attention_kernel,
        shapes,
        "SHHHHHVH",
        [pltpu.VMEM((PACKED, 3 * D), F32), pltpu.VMEM((PACKED, D), F32)],
        limit=48,
    )(flag, jnp.asarray(extra), main, north, west, corner, w_qkv, w_out)
    north, west, corner = move(north, 1, 0), move(west, 0, 1), move(corner, 1, 1)
    core = lax.axis_index("core").astype(jnp.int32).reshape(1, 1)
    share = struct((ROWS // 2, D))
    owned, fields, keep, send = call(
        decode_kernel,
        [struct((TOKENS, D)), struct((PATCHES, PLEV * OUTS)), share, share],
        "SHVVVHVVVVVVVV",
        [
            pltpu.VMEM((TOKENS, D), F32),
            pltpu.VMEM((TOKENS, LANES), F32),
            pltpu.VMEM((TOKENS, D), F32),
            pltpu.VMEM((PLEV * PATCHES, D), BF),
            pltpu.VMEM(((LEV - 1) * PATCHES, PLEV * LANES), BF),
            pltpu.VMEM((PATCHES, PLEV * OUTS), F32),
            pltpu.VMEM((ROWS, D), F32),
            pltpu.VMEM((TOKENS, D), BF),
            pltpu.VMEM((PATCHES, PLEV * OUTS), BF),
            pltpu.SemaphoreType.DMA((2,)),
        ],
        out_specs=[pl.BlockSpec(memory_space=pl.ANY)] * 2 + [pl.BlockSpec(memory_space=pltpu.VMEM)] * 2,
    )(core, main, north, west, corner, jnp.asarray(perm.T, BF), w_kv, level_queries, up, dctx, dsum, both, base, wv)
    mine, other = sum_over_all(keep, send)
    kv, query, out, pixels = call(
        final_kernel,
        [struct((D, 2 * D), F32), struct((PLEV, D), F32), struct((D, D), F32), struct((OUTS, D), F32)],
        "SVVVVVV",
    )(core, mine, other, w_kv, level_queries, w_o, head)
    shape = latents.shape
    return (owned.reshape(shape), fields.reshape(shape[1], shape[2], PLEV * OUTS), kv, query, out, pixels.T)


def solution(mesh):
    lats, lons = mesh.shape["lat"], mesh.shape["lon"]
    sizes = (lats // 2, 2, 2, lons // 4, 2)
    fine = jax.sharding.Mesh(mesh.devices.reshape(sizes), LAT + LON)
    in_specs = (
        P(None, LAT, LON, None),
        P(LAT, LON),
        P(),
        P(),
        P(),
        P(),
        P(),
        P(),
        P(LAT, LON, None),
    )
    out_specs = (P(None, LAT, LON, None), P(LAT, LON, None), P(), P(), P(), P())
    return jax.shard_map(per_device, mesh=fine, in_specs=in_specs, out_specs=out_specs, check_vma=False)
```

```python
import functools
import math

import jax
import jax.numpy as jnp
import numpy as np
from jax import lax
from jax.experimental import pallas as pl
from jax.experimental.pallas import tpu as pltpu
from jax.sharding import PartitionSpec as P

D = 512
HEADS = 8
LEV = 4
PLEV = 13
OUTS = 80
WL = 2
WH = 6
WW = 12
PATCHES = WH * 2 * WW
TOKENS = LEV * PATCHES
MAIN = 224
SIDE = 80
PACKED = 2 * MAIN + 2 * SIDE
ROWS = 768
BLOCK = 16
LANES = 128

SPAN = 256
PIECES = (
    {0: (0, 72, 0), 1: (72, 72, 0), 2: (144, 40, 0), 3: (184, 40, 0)},
    {0: (224, 72, 72), 1: (296, 72, 72), 2: (368, 40, 40), 3: (408, 40, 40)},
    {2: (448, 40, 80), 3: (488, 40, 80)},
    {2: (528, 40, 120), 3: (568, 40, 120)},
)

LAT = ("z", "x_hi")
LON = ("x_lo", "y", "core")
PLANE = ("x_hi", "x_lo", "y")

norm_eps = 1e-05
clip_eps = 1e-06
BF = jnp.bfloat16
F32 = jnp.float32


def window_order():
    level_pairs = ((1, 2), (3, 0))

    def rows_of(levels, rows, cols):
        return [(l * WH + r) * 2 * WW + c for l in levels for r in rows for c in cols]

    order = []
    for rows in ((3, 4, 5), (0, 1, 2)):
        for pair in level_pairs:
            order += rows_of(pair, rows, range(6, 18))
        for pair in level_pairs:
            order += rows_of(pair, rows, range(18, 24)) + [-1] * 4
    for rows in ((0, 1, 2), (3, 4, 5)):
        for pair in level_pairs:
            order += rows_of(pair, rows, range(0, 6)) + [-1] * 4
    return np.array(order)


def pack_matrix():
    order = window_order()
    return (order[:, None] == np.arange(TOKENS)[None, :]).astype(np.float32)


def label_tables():
    order = window_order()
    row, col, level = order // (2 * WW) % WH, order % (2 * WW), order // PATCHES
    columns = np.zeros((2 * WW, 12 * SPAN), np.float32)
    rows = np.zeros((8, 12 * SPAN), np.float32)
    extra = np.zeros((8, SPAN), np.float32)
    segment = 0
    for starts, far in zip(PIECES, (False, True, True, False)):
        for window, (at, count, place) in starts.items():
            for i in range(count):
                lane, token = place + i, at + i
                if order[token] < 0:
                    extra[window, lane] = -1
                    continue
                columns[col[token], segment * SPAN + lane] = 1
                rows[row[token], segment * SPAN + lane] = 1
                extra[window, lane] = 8 * (level[token] == 0)
                extra[4 + window, lane] = 4 * far
            segment += 1
    return columns, rows, extra


def dot(a, b, contract):
    return lax.dot_general(a, b, (contract, ((), ())), preferred_element_type=F32)


def mm(a, b):
    return dot(a, b, ((1,), (0,)))


def layer_norm(wide):
    center = wide - jnp.mean(wide, axis=-1, keepdims=True)
    spread = jnp.mean(center * center, axis=-1, keepdims=True)
    return (center * lax.rsqrt(spread + norm_eps)).astype(BF)


def pack_kernel(pieces, x_ref, ids_ref, perm_ref, columns_ref, rows_ref, *piece_refs):
    ids = ids_ref[...].astype(F32).astype(BF)
    lines = jnp.sum(mm(ids, columns_ref[...]) * rows_ref[:WH], axis=0, keepdims=True)
    x = x_ref[...]
    segment = 0
    first = 0
    for ref, windows in zip(piece_refs, pieces, strict=True):
        height = ref.shape[0]
        packed = mm(perm_ref[first : first + height], x)
        first += height
        bottom = [jnp.zeros((12, SPAN), F32)]
        for window in range(4):
            if window in windows:
                bottom.append(lines[:, segment * SPAN : (segment + 1) * SPAN])
                segment += 1
            else:
                bottom.append(jnp.zeros((1, SPAN), F32))
        bottom = jnp.concatenate(bottom, axis=0)
        bottom = jnp.concatenate([bottom, jnp.zeros((16, D - SPAN), F32)], axis=1)
        ref[: height - 16] = packed[: height - 16].astype(BF)
        ref[height - 16 :] = (packed[height - 16 :] + bottom).astype(BF)


def attention_kernel(
    flag_ref, extra_ref, main_ref, north_ref, corner_ref, west_ref, wqkv_ref, wout_ref,
    main_out, north_out, corner_out, west_out, proj, context,
):
    pieces = (main_ref, north_ref, corner_ref, west_ref)
    wide = jnp.concatenate([ref[...].astype(F32) for ref in pieces], axis=0)
    proj[...] = mm(layer_norm(wide), wqkv_ref[...])
    lines = sum(ref[ref.shape[0] - 16 :, :SPAN].astype(F32) for ref in pieces)[12:]
    lines = lines + extra_ref[:4] + jnp.where(flag_ref[0, 0] > 0, extra_ref[4:], 0.0)
    lines = jnp.concatenate([lines, lines], axis=0)
    i = lax.broadcasted_iota(jnp.int32, (SPAN, SPAN), 0)
    j = lax.broadcasted_iota(jnp.int32, (SPAN, SPAN), 1)
    standing = dot((i == j).astype(F32).astype(BF), lines.astype(BF), ((1,), (1,)))
    n, w, c = MAIN, 2 * MAIN, 2 * MAIN + SIDE
    windows = (
        (0, 144, ((0, 72), (n, 72))),
        (1, 144, ((72, 72), (n + 72, 72))),
        (2, 160, ((144, 40), (n + 144, 40), (w, 40), (c, 40))),
        (3, 160, ((184, 40), (n + 184, 40), (w + 40, 40), (c + 40, 40))),
    )
    low = lax.broadcasted_iota(jnp.int32, (1, LANES), 1) < D // HEADS
    for index, size, parts in windows:
        allowed = standing[:size, index : index + 1] == lines[index : index + 1, :size]
        bias = jnp.where(allowed, 0.0, -jnp.inf)
        bias = jnp.concatenate([bias, bias], axis=0)

        def take(start):
            return jnp.concatenate([proj[at : at + count, start : start + LANES] for at, count in parts], axis=0)

        for pair in range(HEADS // 2):
            lane = pair * LANES
            query = take(lane).astype(BF).astype(F32) * 0.125
            key = take(D + lane).astype(BF)
            value = take(2 * D + lane).astype(BF).astype(F32)
            both = jnp.concatenate([jnp.where(low, query, 0.0), jnp.where(low, 0.0, query)], axis=0).astype(BF)
            scores = dot(both, key, ((1,), (1,))) + bias
            weights = jnp.exp(scores - jnp.max(scores, axis=-1, keepdims=True)).astype(BF)
            even = mm(weights[:size], jnp.where(low, value, 1.0).astype(BF))
            odd = mm(weights[size:], jnp.where(low, 1.0, value).astype(BF))
            sums = pltpu.roll(jnp.where(low, odd, even), LANES // 2, 1)
            result = jnp.where(low, even, odd) / sums
            start = 0
            for at, count in parts:
                context[at : at + count, lane : lane + LANES] = result[start : start + count]
                start += count
    mixed = wide + mm(context[...].astype(BF), wout_ref[...])
    mixed = mixed.astype(BF)
    main_out[...] = mixed[:n]
    north_out[...] = mixed[n:w]
    corner_out[...] = mixed[w:c]
    west_out[...] = mixed[c:]


def shift_matrix(offset, width):
    i = lax.broadcasted_iota(jnp.int32, (width, LANES), 0)
    j = lax.broadcasted_iota(jnp.int32, (width, LANES), 1)
    return ((i - offset == j) & (j < OUTS)).astype(F32).astype(BF)


def spot(level):
    first = level * OUTS // LANES * LANES
    return first, level * OUTS - first, min(2 * LANES, PLEV * OUTS - first)


def spread_queries(queries):
    parts = [jnp.broadcast_to(queries[a : a + 1], (HEADS, D)) for a in range(PLEV)]
    parts.append(jnp.zeros((LANES - HEADS * PLEV, D), F32))
    tall = jnp.concatenate(parts, axis=0)
    c = lax.broadcasted_iota(jnp.int32, (LANES, D), 0)
    j = lax.broadcasted_iota(jnp.int32, (LANES, D), 1)
    return jnp.where(c % HEADS == j // (D // HEADS), tall, 0.0)


def lane_of(j):
    size = D // HEADS
    return j % size // 16 * LANES + j // size * 16 + j % 16


def feature_order():
    wanted = lane_of(lax.broadcasted_iota(jnp.int32, (D, LANES), 0))
    lane = lax.broadcasted_iota(jnp.int32, (D, LANES), 1)
    tiles = [jnp.where(wanted == lane + start, 1.0, 0.0) for start in range(0, D, LANES)]
    return jnp.concatenate(tiles, axis=1).astype(BF)


def natural_order():
    wanted = lane_of(lax.broadcasted_iota(jnp.int32, (8, D), 1))
    lane = lax.broadcasted_iota(jnp.int32, (8, D), 0)
    tiles = [jnp.where(wanted == lane + start, 1.0, 0.0) for start in range(0, D, 8)]
    return jnp.concatenate(tiles, axis=0).astype(BF)


def pre_kernel(
    cot_ref, queries_ref, wo_ref, whead_ref, wkv_ref,
    up_ref, dctx_ref, dsum_ref, map_ref, base_ref, wv_ref,
):
    order = feature_order()
    wv_ref[...] = mm(wkv_ref[:, D:], order).astype(BF)
    head = whead_ref[...]
    both = dot(wo_ref[...], head, ((1,), (1,))).astype(BF)
    both = dot(order, both, ((0,), (0,))).astype(BF)
    map_ref[...] = both
    base_ref[...] = jnp.concatenate(
        [dot(queries_ref[...], head, ((1,), (1,))), jnp.zeros((16 - PLEV, LANES), F32)], axis=0
    )
    dsum = jnp.zeros((PATCHES, D), F32)
    for level in range(PLEV):
        first, offset, width = spot(level)
        up = mm(cot_ref[:, first : first + width], shift_matrix(offset, width)).astype(BF)
        up_ref[level] = up
        dctx = dot(up, both, ((1,), (1,))).astype(BF)
        dctx_ref[level] = dctx
        dsum = dsum + dctx.astype(F32)
    dsum_ref[...] = dsum


def decode_kernel(
    flag_ref, main_ref, north_ref, corner_ref, west_ref, perm_ref, wkv_ref, queries_ref, up_ref, dctx_ref, dsum_ref,
    map_ref, base_ref, wv_ref,
    owned_ref, fields_ref, keep_ref, send_ref,
    value, weights, dvalues, context, products, fields, sums, owned, decoded_out, sems,
):
    pieces = (main_ref, north_ref, corner_ref, west_ref)
    packed = jnp.concatenate([ref[...] for ref in pieces], axis=0)
    wide = mm(perm_ref[...], packed)
    owned[...] = wide.astype(BF)
    owned_copy = pltpu.make_async_copy(owned, owned_ref, sems.at[0])
    owned_copy.start()
    normed = layer_norm(wide)
    key = mm(normed, wkv_ref[:, :D]).astype(BF)
    value[...] = mm(normed, wv_ref[...]).astype(BF).astype(F32)
    queries = spread_queries(queries_ref[...].astype(F32)).astype(BF)
    scores = dot(key, queries, ((1,), (1,))) * 0.125
    slabs = [scores[l * PATCHES : (l + 1) * PATCHES] for l in range(LEV)]
    top = jnp.maximum(jnp.maximum(slabs[0], slabs[1]), jnp.maximum(slabs[2], slabs[3]))
    slabs = [jnp.exp(s - top) for s in slabs]
    scale = 1.0 / (slabs[0] + slabs[1] + slabs[2] + slabs[3])
    slabs = [s * scale for s in slabs]
    for l in range(LEV):
        weights[l * PATCHES : (l + 1) * PATCHES] = slabs[l]
    head_of = lax.broadcasted_iota(jnp.int32, (BLOCK, LANES), 1) // 16
    for start in range(0, PATCHES, BLOCK):
        at = [slice(l * PATCHES + start, l * PATCHES + start + BLOCK) for l in range(LEV)]
        last = value[at[LEV - 1]]
        gaps = [value[at[l]] - last for l in range(LEV - 1)]
        heads = [weights[at[l]] for l in range(LEV - 1)]
        found = [jnp.zeros((BLOCK, D), F32) for _ in range(LEV - 1)]
        for level in range(PLEV):
            index = head_of + level * HEADS
            upstream = dctx_ref[level, start : start + BLOCK].astype(F32)
            total = last
            for l in range(LEV - 1):
                spread = jnp.take_along_axis(heads[l], index, axis=1)
                spread = jnp.concatenate([spread] * (D // LANES), axis=1)
                total = total + spread * gaps[l]
                found[l] = found[l] + spread * upstream
                product = upstream * gaps[l]
                folded = (product[:, :LANES] + product[:, LANES : 2 * LANES]) + (
                    product[:, 2 * LANES : 3 * LANES] + product[:, 3 * LANES :]
                )
                products[at[l], level * LANES : (level + 1) * LANES] = folded.astype(BF)
            context[level * PATCHES + start : level * PATCHES + start + BLOCK] = total.astype(BF)
        for l in range(LEV - 1):
            dvalues[at[l]] = found[l]
        dvalues[at[LEV - 1]] = dsum_ref[start : start + BLOCK] - (found[0] + found[1] + found[2])
    fields[...] = jnp.zeros_like(fields)
    row = lax.broadcasted_iota(jnp.int32, (PLEV * LANES, LANES), 0)
    c = lax.broadcasted_iota(jnp.int32, (PLEV * LANES, LANES), 1)
    slopes = mm(products[...], jnp.where(row // 16 == c, 1.0, 0.0).astype(BF))
    for level in range(PLEV):
        first, offset, width = spot(level)
        decoded = mm(context[level * PATCHES : (level + 1) * PATCHES], map_ref[...]) + base_ref[level : level + 1]
        fields[:, first : first + width] += dot(decoded.astype(BF), shift_matrix(offset, width), ((1,), (1,)))
    decoded_out[...] = fields[...].astype(BF)
    fields_copy = pltpu.make_async_copy(decoded_out, fields_ref, sems.at[1])
    fields_copy.start()
    slopes = [slopes[l * PATCHES : (l + 1) * PATCHES] for l in range(LEV - 1)]
    mean = sum(p * d for p, d in zip(slabs, slopes))
    dscores = [p * (d - mean) * 0.125 for p, d in zip(slabs, slopes)]
    dscores.append(slabs[LEV - 1] * mean * -0.125)
    dscores = jnp.concatenate(dscores, axis=0).astype(BF)
    sums[:D] = dot(normed, dvalues[...].astype(BF), ((0,), (0,)))
    sums[D : D + LANES] = dot(dscores, normed, ((0,), (0,)))
    up = jnp.concatenate([up_ref[a] for a in range(PLEV)], axis=0)
    outer = dot(up, context[...], ((0,), (0,)))
    sums[D + LANES : D + LANES + OUTS] = outer[:OUTS]
    totals = [jnp.sum(up_ref[a].astype(F32), axis=0, keepdims=True) for a in range(PLEV)]
    totals.append(jnp.zeros((LANES - OUTS - PLEV, LANES), F32))
    totals = jnp.concatenate(totals, axis=0)
    sums[D + LANES + OUTS :] = jnp.concatenate([totals, jnp.zeros((LANES - OUTS, D - LANES), F32)], axis=1)
    second = flag_ref[0, 0] > 0
    top, bottom = sums[: ROWS // 2], sums[ROWS // 2 :]
    keep_ref[...] = jnp.where(second, bottom, top).astype(BF)
    send_ref[...] = jnp.where(second, top, bottom).astype(BF)
    owned_copy.wait()
    fields_copy.wait()


def add_kernel(left_ref, right_ref, out_ref):
    out_ref[...] = (left_ref[...].astype(F32) + right_ref[...].astype(F32)).astype(BF)


def final_kernel(flag_ref, mine_ref, other_ref, wkv_ref, queries_ref, wo_ref, whead_ref, kv_ref, query_ref, o_ref, head_ref, kv, o, sems):
    second = flag_ref[0, 0] > 0
    mine, other = mine_ref[...].astype(F32), other_ref[...].astype(F32)
    sums = jnp.concatenate([jnp.where(second, other, mine), jnp.where(second, mine, other)], axis=0).astype(BF)
    queries = queries_ref[...]
    head = whead_ref[...]
    keyed = sums[D : D + LANES]
    outer = sums[D + LANES :]
    level_sums = outer[OUTS : OUTS + 16, :LANES]
    spread = spread_queries(queries.astype(F32)).astype(BF)
    natural = natural_order()
    values = mm(sums[:D], natural)
    keys = dot(keyed, spread, ((0,), (0,)))
    c = lax.broadcasted_iota(jnp.int32, (LANES, D), 0)
    j = lax.broadcasted_iota(jnp.int32, (LANES, D), 1)
    grouped = jnp.where(c % HEADS == j // (D // HEADS), mm(keyed, wkv_ref[:, :D]), 0.0)
    grouped = jnp.sum(grouped.reshape(LANES // HEADS, HEADS, D), axis=1)
    level = grouped[:PLEV] + mm(level_sums, head)[:PLEV]
    clean = mm(outer[:OUTS], natural).astype(BF)
    out = dot(clean, head[:OUTS], ((0,), (0,)))
    pixels = mm(clean, wo_ref[...])
    pixels = pixels + dot(level_sums[:PLEV, :OUTS], queries, ((0,), (0,)))
    squares = jnp.sum(values * values) + jnp.sum(keys * keys) + jnp.sum(level * level)
    squares = squares + jnp.sum(out * out) + jnp.sum(pixels * pixels)
    limit = math.sqrt(2 * D * D + PLEV * D + D * D + D * OUTS)
    factor = jnp.minimum(1.0, limit * lax.rsqrt(jnp.full((1, 1), squares + clip_eps, F32)))
    values_half, keys_half = (slice(None), slice(D, None)), (slice(None), slice(None, D))
    kv[values_half] = values * factor
    values_copy = pltpu.make_async_copy(kv.at[values_half], kv_ref.at[values_half], sems.at[0])
    values_copy.start()
    kv[keys_half] = keys * factor
    keys_copy = pltpu.make_async_copy(kv.at[keys_half], kv_ref.at[keys_half], sems.at[1])
    keys_copy.start()
    o[...] = out * factor
    o_copy = pltpu.make_async_copy(o, o_ref, sems.at[2])
    o_copy.start()
    query_ref[...] = level * factor
    head_ref[...] = pixels * factor
    values_copy.wait()
    keys_copy.wait()
    o_copy.wait()


def call(kernel, outs, spaces, scratch=(), limit=40, out_specs=None):
    where = {"V": pltpu.VMEM, "H": pltpu.HBM}
    whole, scalar = pl.BlockSpec(memory_space=pltpu.VMEM), pl.BlockSpec(memory_space=pltpu.SMEM)
    more = {} if out_specs is None else {"out_specs": out_specs}
    run = pl.pallas_call(
        kernel,
        **more,
        in_specs=[scalar if space == "S" else whole for space in spaces],
        out_shape=outs,
        scratch_shapes=list(scratch),
        compiler_params=pltpu.CompilerParams(vmem_limit_bytes=limit * 2**20),
    )

    def close(*operands):
        held = [
            pltpu.with_memory_space_constraint(x, where[space]) if space in where else x
            for space, x in zip(spaces, operands, strict=True)
        ]
        return run(*held)

    return close


def struct(shape, dtype=BF):
    return jax.ShapeDtypeStruct(shape, dtype)


def far_struct(shape, dtype=BF):
    return pltpu.HBM(shape, dtype)


def move(array, lat_step, lon_step):
    lats, lons = lax.axis_size(LAT), lax.axis_size(LON)
    route = [
        (i * lons + j, (i + lat_step) % lats * lons + (j + lon_step) % lons)
        for i in range(lats)
        for j in range(lons)
    ]
    return lax.ppermute(array, LAT + LON, route)


def swap(array):
    count = lax.axis_size("core")
    return lax.ppermute(array, "core", [(i, (i + 1) % count) for i in range(count)])


def add_up(blocks):
    return jnp.sum(blocks.astype(F32), axis=0).astype(BF)


def copies(block, axes):
    return jnp.broadcast_to(block[None], (lax.axis_size(axes),) + block.shape)


def sum_over_all(keep, send):
    rows, width = keep.shape
    mine = call(add_kernel, struct((rows, width)), "VV", limit=8)(keep, swap(send))
    chips = lax.axis_size(PLANE)
    mine = add_up(lax.all_to_all(mine.reshape(chips, rows // chips, width), PLANE, 0, 0, tiled=True))
    mine = add_up(lax.all_to_all(copies(mine, "z"), "z", 0, 0, tiled=True))
    mine = lax.all_to_all(copies(mine, PLANE), PLANE, 0, 0, tiled=True).reshape(rows, width)
    return mine, swap(mine)


def per_device(latents, mask_ids, w_qkv, w_out, w_kv, level_queries, w_o, w_head, field_cotangent):
    perm = pack_matrix()
    columns, rows, extra = label_tables()
    flag = (lax.axis_index(LAT) == lax.axis_size(LAT) - 1).astype(jnp.int32).reshape(1, 1)
    shapes = [far_struct((MAIN, D)), struct((MAIN, D)), struct((SIDE, D)), struct((SIDE, D))]
    split = 4 * SPAN
    flat = latents.reshape(TOKENS, D)
    north, corner, west = call(functools.partial(pack_kernel, PIECES[1:]), shapes[1:], "HHHHH", limit=56)(
        flat, mask_ids, jnp.asarray(perm[MAIN:], BF), jnp.asarray(columns[:, split:], BF), jnp.asarray(rows[:, split:])
    )
    (main,) = call(functools.partial(pack_kernel, PIECES[:1]), shapes[:1], "HHHHH", limit=56)(
        flat, mask_ids, jnp.asarray(perm[:MAIN], BF), jnp.asarray(columns[:, :split], BF), jnp.asarray(rows[:, :split])
    )
    north, corner, west = move(north, -1, 0), move(corner, -1, -1), move(west, 0, -1)
    head = jnp.pad(w_head.T, ((0, LANES - OUTS), (0, 0)))
    up, dctx, dsum, both, base, wv = call(
        pre_kernel,
        [
            struct((PLEV, PATCHES, LANES)),
            struct((PLEV, PATCHES, D)),
            struct((PATCHES, D), F32),
            struct((D, LANES)),
            struct((16, LANES), F32),
            struct((D, D)),
        ],
        "VVVVV",
    )(field_cotangent.reshape(PATCHES, PLEV * OUTS), level_queries, w_o, head, w_kv)
    main, north, corner, west = call(
        attention_kernel,
        shapes,
        "SHHHHHVH",
        [pltpu.VMEM((PACKED, 3 * D), F32), pltpu.VMEM((PACKED, D), F32)],
        limit=48,
    )(flag, jnp.asarray(extra), main, north, corner, west, w_qkv, w_out)
    north, corner, west = move(north, 1, 0), move(corner, 1, 1), move(west, 0, 1)
    core = lax.axis_index("core").astype(jnp.int32).reshape(1, 1)
    share = struct((ROWS // 2, D))
    owned, fields, keep, send = call(
        decode_kernel,
        [struct((TOKENS, D)), struct((PATCHES, PLEV * OUTS)), share, share],
        "SHVVVHVVVVVVVV",
        [
            pltpu.VMEM((TOKENS, D), F32),
            pltpu.VMEM((TOKENS, LANES), F32),
            pltpu.VMEM((TOKENS, D), F32),
            pltpu.VMEM((PLEV * PATCHES, D), BF),
            pltpu.VMEM(((LEV - 1) * PATCHES, PLEV * LANES), BF),
            pltpu.VMEM((PATCHES, PLEV * OUTS), F32),
            pltpu.VMEM((ROWS, D), F32),
            pltpu.VMEM((TOKENS, D), BF),
            pltpu.VMEM((PATCHES, PLEV * OUTS), BF),
            pltpu.SemaphoreType.DMA((2,)),
        ],
        out_specs=[pl.BlockSpec(memory_space=pl.ANY)] * 2 + [pl.BlockSpec(memory_space=pltpu.VMEM)] * 2,
    )(core, main, north, corner, west, jnp.asarray(perm.T, BF), w_kv, level_queries, up, dctx, dsum, both, base, wv)
    mine, other = sum_over_all(keep, send)
    kv, query, out, pixels = call(
        final_kernel,
        [struct((D, 2 * D), F32), struct((PLEV, D), F32), struct((D, D), F32), struct((OUTS, D), F32)],
        "SVVVVVV",
        [pltpu.VMEM((D, 2 * D), F32), pltpu.VMEM((D, D), F32), pltpu.SemaphoreType.DMA((3,))],
        out_specs=[pl.BlockSpec(memory_space=space) for space in (pl.ANY, pltpu.VMEM, pl.ANY, pltpu.VMEM)],
    )(core, mine, other, w_kv, level_queries, w_o, head)
    shape = latents.shape
    return (owned.reshape(shape), fields.reshape(shape[1], shape[2], PLEV * OUTS), kv, query, out, pixels.T)


def solution(mesh):
    lats, lons = mesh.shape["lat"], mesh.shape["lon"]
    sizes = (lats // 2, 2, 2, lons // 4, 2)
    fine = jax.sharding.Mesh(mesh.devices.reshape(sizes), LAT + LON)
    in_specs = (
        P(None, LAT, LON, None),
        P(LAT, LON),
        P(),
        P(),
        P(),
        P(),
        P(),
        P(),
        P(LAT, LON, None),
    )
    out_specs = (P(None, LAT, LON, None), P(LAT, LON, None), P(), P(), P(), P())
    return jax.shard_map(per_device, mesh=fine, in_specs=in_specs, out_specs=out_specs, check_vma=False)
```

```python
import functools
import math

import jax
import jax.numpy as jnp
import numpy as np
from jax import lax
from jax.experimental import pallas as pl
from jax.experimental.pallas import tpu as pltpu
from jax.sharding import PartitionSpec as P

D = 512
HEADS = 8
LEV = 4
PLEV = 13
OUTS = 80
WL = 2
WH = 6
WW = 12
PATCHES = WH * 2 * WW
TOKENS = LEV * PATCHES
MAIN = 224
SIDE = 80
PACKED = 2 * MAIN + 2 * SIDE
ROWS = 768
BLOCK = 16
LANES = 128

SPAN = 256
PIECES = (
    {0: (0, 72, 0), 1: (72, 72, 0), 2: (144, 40, 0), 3: (184, 40, 0)},
    {0: (224, 72, 72), 1: (296, 72, 72), 2: (368, 40, 40), 3: (408, 40, 40)},
    {2: (448, 40, 80), 3: (488, 40, 80)},
    {2: (528, 40, 120), 3: (568, 40, 120)},
)

LAT = ("z", "x_hi")
LON = ("x_lo", "y", "core")
PLANE = ("x_hi", "x_lo", "y")

norm_eps = 1e-05
clip_eps = 1e-06
BF = jnp.bfloat16
F32 = jnp.float32


def window_order():
    level_pairs = ((1, 2), (3, 0))

    def rows_of(levels, rows, cols):
        return [(l * WH + r) * 2 * WW + c for l in levels for r in rows for c in cols]

    order = []
    for rows in ((3, 4, 5), (0, 1, 2)):
        for pair in level_pairs:
            order += rows_of(pair, rows, range(6, 18))
        for pair in level_pairs:
            order += rows_of(pair, rows, range(18, 24)) + [-1] * 4
    for rows in ((0, 1, 2), (3, 4, 5)):
        for pair in level_pairs:
            order += rows_of(pair, rows, range(0, 6)) + [-1] * 4
    return np.array(order)


def pack_matrix():
    order = window_order()
    return (order[:, None] == np.arange(TOKENS)[None, :]).astype(np.float32)


def label_tables():
    order = window_order()
    row, col, level = order // (2 * WW) % WH, order % (2 * WW), order // PATCHES
    columns = np.zeros((2 * WW, 12 * SPAN), np.float32)
    rows = np.zeros((8, 12 * SPAN), np.float32)
    extra = np.zeros((8, SPAN), np.float32)
    segment = 0
    for starts, far in zip(PIECES, (False, True, True, False)):
        for window, (at, count, place) in starts.items():
            for i in range(count):
                lane, token = place + i, at + i
                if order[token] < 0:
                    extra[window, lane] = -1
                    continue
                columns[col[token], segment * SPAN + lane] = 1
                rows[row[token], segment * SPAN + lane] = 1
                extra[window, lane] = 8 * (level[token] == 0)
                extra[4 + window, lane] = 4 * far
            segment += 1
    return columns, rows, extra


def dot(a, b, contract):
    return lax.dot_general(a, b, (contract, ((), ())), preferred_element_type=F32)


def mm(a, b):
    return dot(a, b, ((1,), (0,)))


def layer_norm(wide):
    center = wide - jnp.mean(wide, axis=-1, keepdims=True)
    spread = jnp.mean(center * center, axis=-1, keepdims=True)
    return (center * lax.rsqrt(spread + norm_eps)).astype(BF)


def pack_kernel(pieces, x_ref, ids_ref, perm_ref, columns_ref, rows_ref, *piece_refs):
    ids = ids_ref[...].astype(F32).astype(BF)
    lines = jnp.sum(mm(ids, columns_ref[...]) * rows_ref[:WH], axis=0, keepdims=True)
    x = x_ref[...]
    segment = 0
    first = 0
    for ref, windows in zip(piece_refs, pieces, strict=True):
        height = ref.shape[0]
        packed = mm(perm_ref[first : first + height], x)
        first += height
        bottom = [jnp.zeros((12, SPAN), F32)]
        for window in range(4):
            if window in windows:
                bottom.append(lines[:, segment * SPAN : (segment + 1) * SPAN])
                segment += 1
            else:
                bottom.append(jnp.zeros((1, SPAN), F32))
        bottom = jnp.concatenate(bottom, axis=0)
        bottom = jnp.concatenate([bottom, jnp.zeros((16, D - SPAN), F32)], axis=1)
        ref[: height - 16] = packed[: height - 16].astype(BF)
        ref[height - 16 :] = (packed[height - 16 :] + bottom).astype(BF)


def own_kernel(x_ref, ids_ref, perm_ref, columns_ref, rows_ref, wout_ref, main_ref, wout_out):
    wout_out[...] = wout_ref[...]
    pack_kernel(PIECES[:1], x_ref, ids_ref, perm_ref, columns_ref, rows_ref, main_ref)


def attention_kernel(
    flag_ref, extra_ref, main_ref, north_ref, corner_ref, west_ref, wqkv_ref, wout_ref,
    main_out, north_out, corner_out, west_out, proj, context,
):
    pieces = (main_ref, north_ref, corner_ref, west_ref)
    wide = jnp.concatenate([ref[...].astype(F32) for ref in pieces], axis=0)
    proj[...] = mm(layer_norm(wide), wqkv_ref[...])
    lines = sum(ref[ref.shape[0] - 16 :, :SPAN].astype(F32) for ref in pieces)[12:]
    lines = lines + extra_ref[:4] + jnp.where(flag_ref[0, 0] > 0, extra_ref[4:], 0.0)
    lines = jnp.concatenate([lines, lines], axis=0)
    i = lax.broadcasted_iota(jnp.int32, (SPAN, SPAN), 0)
    j = lax.broadcasted_iota(jnp.int32, (SPAN, SPAN), 1)
    standing = dot((i == j).astype(F32).astype(BF), lines.astype(BF), ((1,), (1,)))
    n, w, c = MAIN, 2 * MAIN, 2 * MAIN + SIDE
    windows = (
        (0, 144, ((0, 72), (n, 72))),
        (1, 144, ((72, 72), (n + 72, 72))),
        (2, 160, ((144, 40), (n + 144, 40), (w, 40), (c, 40))),
        (3, 160, ((184, 40), (n + 184, 40), (w + 40, 40), (c + 40, 40))),
    )
    low = lax.broadcasted_iota(jnp.int32, (1, LANES), 1) < D // HEADS
    for index, size, parts in windows:
        allowed = standing[:size, index : index + 1] == lines[index : index + 1, :size]
        bias = jnp.where(allowed, 0.0, -jnp.inf)
        bias = jnp.concatenate([bias, bias], axis=0)

        def take(start):
            return jnp.concatenate([proj[at : at + count, start : start + LANES] for at, count in parts], axis=0)

        for pair in range(HEADS // 2):
            lane = pair * LANES
            query = take(lane).astype(BF).astype(F32) * 0.125
            key = take(D + lane).astype(BF)
            value = take(2 * D + lane).astype(BF).astype(F32)
            both = jnp.concatenate([jnp.where(low, query, 0.0), jnp.where(low, 0.0, query)], axis=0).astype(BF)
            scores = dot(both, key, ((1,), (1,))) + bias
            weights = jnp.exp(scores - jnp.max(scores, axis=-1, keepdims=True)).astype(BF)
            even = mm(weights[:size], jnp.where(low, value, 1.0).astype(BF))
            odd = mm(weights[size:], jnp.where(low, 1.0, value).astype(BF))
            sums = pltpu.roll(jnp.where(low, odd, even), LANES // 2, 1)
            result = jnp.where(low, even, odd) / sums
            start = 0
            for at, count in parts:
                context[at : at + count, lane : lane + LANES] = result[start : start + count]
                start += count
    mixed = wide + mm(context[...].astype(BF), wout_ref[...])
    mixed = mixed.astype(BF)
    main_out[...] = mixed[:n]
    north_out[...] = mixed[n:w]
    corner_out[...] = mixed[w:c]
    west_out[...] = mixed[c:]


def shift_matrix(offset, width):
    i = lax.broadcasted_iota(jnp.int32, (width, LANES), 0)
    j = lax.broadcasted_iota(jnp.int32, (width, LANES), 1)
    return ((i - offset == j) & (j < OUTS)).astype(F32).astype(BF)


def spot(level):
    first = level * OUTS // LANES * LANES
    return first, level * OUTS - first, min(2 * LANES, PLEV * OUTS - first)


def spread_queries(queries):
    parts = [jnp.broadcast_to(queries[a : a + 1], (HEADS, D)) for a in range(PLEV)]
    parts.append(jnp.zeros((LANES - HEADS * PLEV, D), F32))
    tall = jnp.concatenate(parts, axis=0)
    c = lax.broadcasted_iota(jnp.int32, (LANES, D), 0)
    j = lax.broadcasted_iota(jnp.int32, (LANES, D), 1)
    return jnp.where(c % HEADS == j // (D // HEADS), tall, 0.0)


def lane_of(j):
    size = D // HEADS
    return j % size // 16 * LANES + j // size * 16 + j % 16


def feature_order():
    wanted = lane_of(lax.broadcasted_iota(jnp.int32, (D, LANES), 0))
    lane = lax.broadcasted_iota(jnp.int32, (D, LANES), 1)
    tiles = [jnp.where(wanted == lane + start, 1.0, 0.0) for start in range(0, D, LANES)]
    return jnp.concatenate(tiles, axis=1).astype(BF)


def natural_order():
    wanted = lane_of(lax.broadcasted_iota(jnp.int32, (8, D), 1))
    lane = lax.broadcasted_iota(jnp.int32, (8, D), 0)
    tiles = [jnp.where(wanted == lane + start, 1.0, 0.0) for start in range(0, D, 8)]
    return jnp.concatenate(tiles, axis=0).astype(BF)


def pre_kernel(
    cot_ref, queries_ref, wo_ref, whead_ref, wkv_ref, main_ref, main_perm, far_perm,
    up_ref, dctx_ref, dsum_ref, map_ref, base_ref, wv_ref, own_ref, far_perm_out,
):
    own_ref[...] = mm(main_perm[...], main_ref[...]).astype(BF)
    far_perm_out[...] = far_perm[...]
    order = feature_order()
    wv_ref[...] = mm(wkv_ref[:, D:], order).astype(BF)
    head = whead_ref[...]
    both = dot(wo_ref[...], head, ((1,), (1,))).astype(BF)
    both = dot(order, both, ((0,), (0,))).astype(BF)
    map_ref[...] = both
    base_ref[...] = jnp.concatenate(
        [dot(queries_ref[...], head, ((1,), (1,))), jnp.zeros((16 - PLEV, LANES), F32)], axis=0
    )
    dsum = jnp.zeros((PATCHES, D), F32)
    for level in range(PLEV):
        first, offset, width = spot(level)
        up = mm(cot_ref[:, first : first + width], shift_matrix(offset, width)).astype(BF)
        up_ref[level] = up
        dctx = dot(up, both, ((1,), (1,))).astype(BF)
        dctx_ref[level] = dctx
        dsum = dsum + dctx.astype(F32)
    dsum_ref[...] = dsum


def decode_kernel(
    flag_ref, own_ref, north_ref, corner_ref, west_ref, perm_ref, wkv_ref, queries_ref, up_ref, dctx_ref, dsum_ref,
    map_ref, base_ref, wv_ref,
    owned_ref, fields_ref, keep_ref, send_ref,
    value, weights, dvalues, context, products, fields, sums, owned, decoded_out, sems,
):
    far = jnp.concatenate([ref[...] for ref in (north_ref, corner_ref, west_ref)], axis=0)
    wide = own_ref[...].astype(F32) + mm(perm_ref[...], far)
    owned[...] = wide.astype(BF)
    owned_copy = pltpu.make_async_copy(owned, owned_ref, sems.at[0])
    owned_copy.start()
    normed = layer_norm(wide)
    key = mm(normed, wkv_ref[:, :D]).astype(BF)
    value[...] = mm(normed, wv_ref[...]).astype(BF).astype(F32)
    queries = spread_queries(queries_ref[...].astype(F32)).astype(BF)
    scores = dot(key, queries, ((1,), (1,))) * 0.125
    slabs = [scores[l * PATCHES : (l + 1) * PATCHES] for l in range(LEV)]
    top = jnp.maximum(jnp.maximum(slabs[0], slabs[1]), jnp.maximum(slabs[2], slabs[3]))
    slabs = [jnp.exp(s - top) for s in slabs]
    scale = 1.0 / (slabs[0] + slabs[1] + slabs[2] + slabs[3])
    slabs = [s * scale for s in slabs]
    for l in range(LEV):
        weights[l * PATCHES : (l + 1) * PATCHES] = slabs[l]
    head_of = lax.broadcasted_iota(jnp.int32, (BLOCK, LANES), 1) // 16
    for start in range(0, PATCHES, BLOCK):
        at = [slice(l * PATCHES + start, l * PATCHES + start + BLOCK) for l in range(LEV)]
        last = value[at[LEV - 1]]
        gaps = [value[at[l]] - last for l in range(LEV - 1)]
        heads = [weights[at[l]] for l in range(LEV - 1)]
        found = [jnp.zeros((BLOCK, D), F32) for _ in range(LEV - 1)]
        for level in range(PLEV):
            index = head_of + level * HEADS
            upstream = dctx_ref[level, start : start + BLOCK].astype(F32)
            total = last
            for l in range(LEV - 1):
                spread = jnp.take_along_axis(heads[l], index, axis=1)
                spread = jnp.concatenate([spread] * (D // LANES), axis=1)
                total = total + spread * gaps[l]
                found[l] = found[l] + spread * upstream
                product = upstream * gaps[l]
                folded = (product[:, :LANES] + product[:, LANES : 2 * LANES]) + (
                    product[:, 2 * LANES : 3 * LANES] + product[:, 3 * LANES :]
                )
                products[at[l], level * LANES : (level + 1) * LANES] = folded.astype(BF)
            context[level * PATCHES + start : level * PATCHES + start + BLOCK] = total.astype(BF)
        for l in range(LEV - 1):
            dvalues[at[l]] = found[l]
        dvalues[at[LEV - 1]] = dsum_ref[start : start + BLOCK] - (found[0] + found[1] + found[2])
    fields[...] = jnp.zeros_like(fields)
    row = lax.broadcasted_iota(jnp.int32, (PLEV * LANES, LANES), 0)
    c = lax.broadcasted_iota(jnp.int32, (PLEV * LANES, LANES), 1)
    slopes = mm(products[...], jnp.where(row // 16 == c, 1.0, 0.0).astype(BF))
    for level in range(PLEV):
        first, offset, width = spot(level)
        decoded = mm(context[level * PATCHES : (level + 1) * PATCHES], map_ref[...]) + base_ref[level : level + 1]
        fields[:, first : first + width] += dot(decoded.astype(BF), shift_matrix(offset, width), ((1,), (1,)))
    decoded_out[...] = fields[...].astype(BF)
    fields_copy = pltpu.make_async_copy(decoded_out, fields_ref, sems.at[1])
    fields_copy.start()
    slopes = [slopes[l * PATCHES : (l + 1) * PATCHES] for l in range(LEV - 1)]
    mean = sum(p * d for p, d in zip(slabs, slopes))
    dscores = [p * (d - mean) * 0.125 for p, d in zip(slabs, slopes)]
    dscores.append(slabs[LEV - 1] * mean * -0.125)
    dscores = jnp.concatenate(dscores, axis=0).astype(BF)
    sums[:D] = dot(normed, dvalues[...].astype(BF), ((0,), (0,)))
    sums[D : D + LANES] = dot(dscores, normed, ((0,), (0,)))
    up = jnp.concatenate([up_ref[a] for a in range(PLEV)], axis=0)
    outer = dot(up, context[...], ((0,), (0,)))
    sums[D + LANES : D + LANES + OUTS] = outer[:OUTS]
    totals = [jnp.sum(up_ref[a].astype(F32), axis=0, keepdims=True) for a in range(PLEV)]
    totals.append(jnp.zeros((LANES - OUTS - PLEV, LANES), F32))
    totals = jnp.concatenate(totals, axis=0)
    sums[D + LANES + OUTS :] = jnp.concatenate([totals, jnp.zeros((LANES - OUTS, D - LANES), F32)], axis=1)
    second = flag_ref[0, 0] > 0
    top, bottom = sums[: ROWS // 2], sums[ROWS // 2 :]
    keep_ref[...] = jnp.where(second, bottom, top).astype(BF)
    send_ref[...] = jnp.where(second, top, bottom).astype(BF)
    owned_copy.wait()
    fields_copy.wait()


def add_kernel(left_ref, right_ref, out_ref):
    out_ref[...] = (left_ref[...].astype(F32) + right_ref[...].astype(F32)).astype(BF)


def final_kernel(flag_ref, mine_ref, other_ref, wkv_ref, queries_ref, wo_ref, whead_ref, kv_ref, query_ref, o_ref, head_ref):
    second = flag_ref[0, 0] > 0
    mine, other = mine_ref[...].astype(F32), other_ref[...].astype(F32)
    sums = jnp.concatenate([jnp.where(second, other, mine), jnp.where(second, mine, other)], axis=0).astype(BF)
    queries = queries_ref[...]
    head = whead_ref[...]
    keyed = sums[D : D + LANES]
    outer = sums[D + LANES :]
    level_sums = outer[OUTS : OUTS + 16, :LANES]
    spread = spread_queries(queries.astype(F32)).astype(BF)
    natural = natural_order()
    values = mm(sums[:D], natural)
    keys = dot(keyed, spread, ((0,), (0,)))
    c = lax.broadcasted_iota(jnp.int32, (LANES, D), 0)
    j = lax.broadcasted_iota(jnp.int32, (LANES, D), 1)
    grouped = jnp.where(c % HEADS == j // (D // HEADS), mm(keyed, wkv_ref[:, :D]), 0.0)
    grouped = jnp.sum(grouped.reshape(LANES // HEADS, HEADS, D), axis=1)
    level = grouped[:PLEV] + mm(level_sums, head)[:PLEV]
    clean = mm(outer[:OUTS], natural).astype(BF)
    out = dot(clean, head[:OUTS], ((0,), (0,)))
    pixels = mm(clean, wo_ref[...])
    pixels = pixels + dot(level_sums[:PLEV, :OUTS], queries, ((0,), (0,)))
    squares = jnp.sum(values * values) + jnp.sum(keys * keys) + jnp.sum(level * level)
    squares = squares + jnp.sum(out * out) + jnp.sum(pixels * pixels)
    limit = math.sqrt(2 * D * D + PLEV * D + D * D + D * OUTS)
    factor = jnp.minimum(1.0, limit * lax.rsqrt(jnp.full((1, 1), squares + clip_eps, F32)))
    kv_ref[:, :D] = keys * factor
    kv_ref[:, D:] = values * factor
    query_ref[...] = level * factor
    o_ref[...] = out * factor
    head_ref[...] = pixels * factor


def call(kernel, outs, spaces, scratch=(), limit=40, out_specs=None):
    where = {"V": pltpu.VMEM, "H": pltpu.HBM}
    whole, scalar = pl.BlockSpec(memory_space=pltpu.VMEM), pl.BlockSpec(memory_space=pltpu.SMEM)
    more = {} if out_specs is None else {"out_specs": out_specs}
    run = pl.pallas_call(
        kernel,
        **more,
        in_specs=[scalar if space == "S" else whole for space in spaces],
        out_shape=outs,
        scratch_shapes=list(scratch),
        compiler_params=pltpu.CompilerParams(vmem_limit_bytes=limit * 2**20),
    )

    def close(*operands):
        held = [
            pltpu.with_memory_space_constraint(x, where[space]) if space in where else x
            for space, x in zip(spaces, operands, strict=True)
        ]
        return run(*held)

    return close


def struct(shape, dtype=BF):
    return jax.ShapeDtypeStruct(shape, dtype)


def far_struct(shape, dtype=BF):
    return pltpu.HBM(shape, dtype)


def move(array, lat_step, lon_step):
    lats, lons = lax.axis_size(LAT), lax.axis_size(LON)
    route = [
        (i * lons + j, (i + lat_step) % lats * lons + (j + lon_step) % lons)
        for i in range(lats)
        for j in range(lons)
    ]
    return lax.ppermute(array, LAT + LON, route)


def swap(array):
    count = lax.axis_size("core")
    return lax.ppermute(array, "core", [(i, (i + 1) % count) for i in range(count)])


def add_up(blocks):
    return jnp.sum(blocks.astype(F32), axis=0).astype(BF)


def copies(block, axes):
    return jnp.broadcast_to(block[None], (lax.axis_size(axes),) + block.shape)


def sum_over_all(keep, send):
    rows, width = keep.shape
    mine = call(add_kernel, struct((rows, width)), "VV", limit=8)(keep, swap(send))
    chips = lax.axis_size(PLANE)
    mine = add_up(lax.all_to_all(mine.reshape(chips, rows // chips, width), PLANE, 0, 0, tiled=True))
    mine = add_up(lax.all_to_all(copies(mine, "z"), "z", 0, 0, tiled=True))
    mine = lax.all_to_all(copies(mine, PLANE), PLANE, 0, 0, tiled=True).reshape(rows, width)
    return mine, swap(mine)


def per_device(latents, mask_ids, w_qkv, w_out, w_kv, level_queries, w_o, w_head, field_cotangent):
    perm = pack_matrix()
    columns, rows, extra = label_tables()
    flag = (lax.axis_index(LAT) == lax.axis_size(LAT) - 1).astype(jnp.int32).reshape(1, 1)
    shapes = [far_struct((MAIN, D)), struct((MAIN, D)), struct((SIDE, D)), struct((SIDE, D))]
    split = 4 * SPAN
    flat = latents.reshape(TOKENS, D)
    north, corner, west = call(functools.partial(pack_kernel, PIECES[1:]), shapes[1:], "HHHHH", limit=56)(
        flat, mask_ids, jnp.asarray(perm[MAIN:], BF), jnp.asarray(columns[:, split:], BF), jnp.asarray(rows[:, split:])
    )
    main, w_out = call(own_kernel, [struct((MAIN, D)), struct((D, D))], "HHHHHH", limit=40)(
        flat,
        mask_ids,
        jnp.asarray(perm[:MAIN], BF),
        jnp.asarray(columns[:, :split], BF),
        jnp.asarray(rows[:, :split]),
        w_out,
    )
    north, corner, west = move(north, -1, 0), move(corner, -1, -1), move(west, 0, -1)
    head = jnp.pad(w_head.T, ((0, LANES - OUTS), (0, 0)))
    main, north, corner, west = call(
        attention_kernel,
        shapes,
        "SHVHHHVV",
        [pltpu.VMEM((PACKED, 3 * D), F32), pltpu.VMEM((PACKED, D), F32)],
        limit=48,
    )(flag, jnp.asarray(extra), main, north, corner, west, w_qkv, w_out)
    north, corner, west = move(north, 1, 0), move(corner, 1, 1), move(west, 0, 1)
    up, dctx, dsum, both, base, wv, own, far_perm = call(
        pre_kernel,
        [
            struct((PLEV, PATCHES, LANES)),
            struct((PLEV, PATCHES, D)),
            struct((PATCHES, D), F32),
            struct((D, LANES)),
            struct((16, LANES), F32),
            struct((D, D)),
            struct((TOKENS, D)),
            struct((TOKENS, PACKED - MAIN)),
        ],
        "VVVVVHHH",
    )(
        field_cotangent.reshape(PATCHES, PLEV * OUTS),
        level_queries,
        w_o,
        head,
        w_kv,
        main,
        jnp.asarray(perm[:MAIN].T, BF),
        jnp.asarray(perm[MAIN:].T, BF),
    )
    core = lax.axis_index("core").astype(jnp.int32).reshape(1, 1)
    share = struct((ROWS // 2, D))
    owned, fields, keep, send = call(
        decode_kernel,
        [struct((TOKENS, D)), struct((PATCHES, PLEV * OUTS)), share, share],
        "SVVVVVVVVVVVVV",
        [
            pltpu.VMEM((TOKENS, D), F32),
            pltpu.VMEM((TOKENS, LANES), F32),
            pltpu.VMEM((TOKENS, D), F32),
            pltpu.VMEM((PLEV * PATCHES, D), BF),
            pltpu.VMEM(((LEV - 1) * PATCHES, PLEV * LANES), BF),
            pltpu.VMEM((PATCHES, PLEV * OUTS), F32),
            pltpu.VMEM((ROWS, D), F32),
            pltpu.VMEM((TOKENS, D), BF),
            pltpu.VMEM((PATCHES, PLEV * OUTS), BF),
            pltpu.SemaphoreType.DMA((2,)),
        ],
        out_specs=[pl.BlockSpec(memory_space=pl.ANY)] * 2 + [pl.BlockSpec(memory_space=pltpu.VMEM)] * 2,
    )(core, own, north, corner, west, far_perm, w_kv, level_queries, up, dctx, dsum, both, base, wv)
    mine, other = sum_over_all(keep, send)
    kv, query, out, pixels = call(
        final_kernel,
        [struct((D, 2 * D), F32), struct((PLEV, D), F32), struct((D, D), F32), struct((OUTS, D), F32)],
        "SVVVVVV",
    )(core, mine, other, w_kv, level_queries, w_o, head)
    shape = latents.shape
    return (owned.reshape(shape), fields.reshape(shape[1], shape[2], PLEV * OUTS), kv, query, out, pixels.T)


def solution(mesh):
    lats, lons = mesh.shape["lat"], mesh.shape["lon"]
    sizes = (lats // 2, 2, 2, lons // 4, 2)
    fine = jax.sharding.Mesh(mesh.devices.reshape(sizes), LAT + LON)
    in_specs = (
        P(None, LAT, LON, None),
        P(LAT, LON),
        P(),
        P(),
        P(),
        P(),
        P(),
        P(),
        P(LAT, LON, None),
    )
    out_specs = (P(None, LAT, LON, None), P(LAT, LON, None), P(), P(), P(), P())
    return jax.shard_map(per_device, mesh=fine, in_specs=in_specs, out_specs=out_specs, check_vma=False)
```

```python
import functools
import math

import jax
import jax.numpy as jnp
import numpy as np
from jax import lax
from jax.experimental import pallas as pl
from jax.experimental.pallas import tpu as pltpu
from jax.sharding import PartitionSpec as P

D = 512
HEADS = 8
LEV = 4
PLEV = 13
OUTS = 80
WL = 2
WH = 6
WW = 12
PATCHES = WH * 2 * WW
TOKENS = LEV * PATCHES
MAIN = 224
SIDE = 80
PACKED = 2 * MAIN + 2 * SIDE
ROWS = 768
BLOCK = 16
LANES = 128

SPAN = 256
PIECES = (
    {0: (0, 72, 0), 1: (72, 72, 0), 2: (144, 40, 0), 3: (184, 40, 0)},
    {0: (224, 72, 72), 1: (296, 72, 72), 2: (368, 40, 40), 3: (408, 40, 40)},
    {2: (448, 40, 80), 3: (488, 40, 80)},
    {2: (528, 40, 120), 3: (568, 40, 120)},
)

LAT = ("z", "x_hi")
LON = ("x_lo", "y", "core")
PLANE = ("x_hi", "x_lo", "y")

norm_eps = 1e-05
clip_eps = 1e-06
BF = jnp.bfloat16
F32 = jnp.float32


def window_order():
    level_pairs = ((1, 2), (3, 0))

    def rows_of(levels, rows, cols):
        return [(l * WH + r) * 2 * WW + c for l in levels for r in rows for c in cols]

    order = []
    for rows in ((3, 4, 5), (0, 1, 2)):
        for pair in level_pairs:
            order += rows_of(pair, rows, range(6, 18))
        for pair in level_pairs:
            order += rows_of(pair, rows, range(18, 24)) + [-1] * 4
    for rows in ((0, 1, 2), (3, 4, 5)):
        for pair in level_pairs:
            order += rows_of(pair, rows, range(0, 6)) + [-1] * 4
    return np.array(order)


def pack_matrix():
    order = window_order()
    return (order[:, None] == np.arange(TOKENS)[None, :]).astype(np.float32)


def label_tables():
    order = window_order()
    row, col, level = order // (2 * WW) % WH, order % (2 * WW), order // PATCHES
    columns = np.zeros((2 * WW, 12 * SPAN), np.float32)
    rows = np.zeros((8, 12 * SPAN), np.float32)
    extra = np.zeros((8, SPAN), np.float32)
    segment = 0
    for starts, far in zip(PIECES, (False, True, True, False)):
        for window, (at, count, place) in starts.items():
            for i in range(count):
                lane, token = place + i, at + i
                if order[token] < 0:
                    extra[window, lane] = -1
                    continue
                columns[col[token], segment * SPAN + lane] = 1
                rows[row[token], segment * SPAN + lane] = 1
                extra[window, lane] = 8 * (level[token] == 0)
                extra[4 + window, lane] = 4 * far
            segment += 1
    return columns, rows, extra


def dot(a, b, contract):
    return lax.dot_general(a, b, (contract, ((), ())), preferred_element_type=F32)


def mm(a, b):
    return dot(a, b, ((1,), (0,)))


def layer_norm(wide):
    center = wide - jnp.mean(wide, axis=-1, keepdims=True)
    spread = jnp.mean(center * center, axis=-1, keepdims=True)
    return (center * lax.rsqrt(spread + norm_eps)).astype(BF)


def pack_kernel(pieces, x_ref, ids_ref, perm_ref, columns_ref, rows_ref, *piece_refs):
    ids = ids_ref[...].astype(F32).astype(BF)
    lines = jnp.sum(mm(ids, columns_ref[...]) * rows_ref[:WH], axis=0, keepdims=True)
    x = x_ref[...]
    segment = 0
    first = 0
    for ref, windows in zip(piece_refs, pieces, strict=True):
        height = ref.shape[0]
        packed = mm(perm_ref[first : first + height], x)
        first += height
        bottom = [jnp.zeros((12, SPAN), F32)]
        for window in range(4):
            if window in windows:
                bottom.append(lines[:, segment * SPAN : (segment + 1) * SPAN])
                segment += 1
            else:
                bottom.append(jnp.zeros((1, SPAN), F32))
        bottom = jnp.concatenate(bottom, axis=0)
        bottom = jnp.concatenate([bottom, jnp.zeros((16, D - SPAN), F32)], axis=1)
        ref[: height - 16] = packed[: height - 16].astype(BF)
        ref[height - 16 :] = (packed[height - 16 :] + bottom).astype(BF)


def own_kernel(x_ref, ids_ref, perm_ref, columns_ref, rows_ref, wout_ref, main_ref, wout_out):
    wout_out[...] = wout_ref[...]
    pack_kernel(PIECES[:1], x_ref, ids_ref, perm_ref, columns_ref, rows_ref, main_ref)


def attention_kernel(
    flag_ref, extra_ref, main_ref, north_ref, corner_ref, west_ref, wqkv_ref, wout_ref,
    main_out, north_out, corner_out, west_out, proj, context,
):
    pieces = (main_ref, north_ref, corner_ref, west_ref)
    wide = jnp.concatenate([ref[...].astype(F32) for ref in pieces], axis=0)
    proj[...] = mm(layer_norm(wide), wqkv_ref[...])
    lines = sum(ref[ref.shape[0] - 16 :, :SPAN].astype(F32) for ref in pieces)[12:]
    lines = lines + extra_ref[:4] + jnp.where(flag_ref[0, 0] > 0, extra_ref[4:], 0.0)
    lines = jnp.concatenate([lines, lines], axis=0)
    i = lax.broadcasted_iota(jnp.int32, (SPAN, SPAN), 0)
    j = lax.broadcasted_iota(jnp.int32, (SPAN, SPAN), 1)
    standing = dot((i == j).astype(F32).astype(BF), lines.astype(BF), ((1,), (1,)))
    n, w, c = MAIN, 2 * MAIN, 2 * MAIN + SIDE
    windows = (
        (0, 144, ((0, 72), (n, 72))),
        (1, 144, ((72, 72), (n + 72, 72))),
        (2, 160, ((144, 40), (n + 144, 40), (w, 40), (c, 40))),
        (3, 160, ((184, 40), (n + 184, 40), (w + 40, 40), (c + 40, 40))),
    )
    low = lax.broadcasted_iota(jnp.int32, (1, LANES), 1) < D // HEADS
    for index, size, parts in windows:
        allowed = standing[:size, index : index + 1] == lines[index : index + 1, :size]
        bias = jnp.where(allowed, 0.0, -jnp.inf)
        bias = jnp.concatenate([bias, bias], axis=0)

        def take(start):
            return jnp.concatenate([proj[at : at + count, start : start + LANES] for at, count in parts], axis=0)

        for pair in range(HEADS // 2):
            lane = pair * LANES
            query = take(lane).astype(BF).astype(F32) * 0.125
            key = take(D + lane).astype(BF)
            value = take(2 * D + lane).astype(BF).astype(F32)
            both = jnp.concatenate([jnp.where(low, query, 0.0), jnp.where(low, 0.0, query)], axis=0).astype(BF)
            scores = dot(both, key, ((1,), (1,))) + bias
            weights = jnp.exp(scores - jnp.max(scores, axis=-1, keepdims=True)).astype(BF)
            even = mm(weights[:size], jnp.where(low, value, 1.0).astype(BF))
            odd = mm(weights[size:], jnp.where(low, 1.0, value).astype(BF))
            sums = pltpu.roll(jnp.where(low, odd, even), LANES // 2, 1)
            result = jnp.where(low, even, odd) / sums
            start = 0
            for at, count in parts:
                context[at : at + count, lane : lane + LANES] = result[start : start + count]
                start += count
    mixed = wide + mm(context[...].astype(BF), wout_ref[...])
    mixed = mixed.astype(BF)
    main_out[...] = mixed[:n]
    north_out[...] = mixed[n:w]
    corner_out[...] = mixed[w:c]
    west_out[...] = mixed[c:]


def shift_matrix(offset, width):
    i = lax.broadcasted_iota(jnp.int32, (width, LANES), 0)
    j = lax.broadcasted_iota(jnp.int32, (width, LANES), 1)
    return ((i - offset == j) & (j < OUTS)).astype(F32).astype(BF)


def spot(level):
    first = level * OUTS // LANES * LANES
    return first, level * OUTS - first, min(2 * LANES, PLEV * OUTS - first)


def spread_queries(queries):
    parts = [jnp.broadcast_to(queries[a : a + 1], (HEADS, D)) for a in range(PLEV)]
    parts.append(jnp.zeros((LANES - HEADS * PLEV, D), F32))
    tall = jnp.concatenate(parts, axis=0)
    c = lax.broadcasted_iota(jnp.int32, (LANES, D), 0)
    j = lax.broadcasted_iota(jnp.int32, (LANES, D), 1)
    return jnp.where(c % HEADS == j // (D // HEADS), tall, 0.0)


def lane_of(j):
    size = D // HEADS
    return j % size // 16 * LANES + j // size * 16 + j % 16


def feature_order():
    wanted = lane_of(lax.broadcasted_iota(jnp.int32, (D, LANES), 0))
    lane = lax.broadcasted_iota(jnp.int32, (D, LANES), 1)
    tiles = [jnp.where(wanted == lane + start, 1.0, 0.0) for start in range(0, D, LANES)]
    return jnp.concatenate(tiles, axis=1).astype(BF)


def natural_order():
    wanted = lane_of(lax.broadcasted_iota(jnp.int32, (8, D), 1))
    lane = lax.broadcasted_iota(jnp.int32, (8, D), 0)
    tiles = [jnp.where(wanted == lane + start, 1.0, 0.0) for start in range(0, D, 8)]
    return jnp.concatenate(tiles, axis=0).astype(BF)


def pre_kernel(
    cot_ref, queries_ref, wo_ref, whead_ref, wkv_ref, main_ref, main_perm, far_perm,
    up_ref, dctx_ref, dsum_ref, map_ref, base_ref, wv_ref, own_ref, far_perm_out,
    spread_ref, gather_ref, shift_ref, totals_ref,
):
    spread_ref[...] = spread_queries(queries_ref[...].astype(F32)).astype(BF)
    row = lax.broadcasted_iota(jnp.int32, (PLEV * LANES, LANES), 0)
    c = lax.broadcasted_iota(jnp.int32, (PLEV * LANES, LANES), 1)
    gather_ref[...] = jnp.where(row // 16 == c, 1.0, 0.0).astype(BF)
    shift_ref[...] = shift_matrix(LANES, 3 * LANES)
    own_ref[...] = mm(main_perm[...], main_ref[...]).astype(BF)
    far_perm_out[...] = far_perm[...]
    order = feature_order()
    wv_ref[...] = mm(wkv_ref[:, D:], order).astype(BF)
    head = whead_ref[...]
    both = dot(wo_ref[...], head, ((1,), (1,))).astype(BF)
    both = dot(order, both, ((0,), (0,))).astype(BF)
    map_ref[...] = both
    base_ref[...] = jnp.concatenate(
        [dot(queries_ref[...], head, ((1,), (1,))), jnp.zeros((16 - PLEV, LANES), F32)], axis=0
    )
    totals = []
    dsum = jnp.zeros((PATCHES, D), F32)
    for level in range(PLEV):
        first, offset, width = spot(level)
        up = mm(cot_ref[:, first : first + width], shift_ref[LANES - offset : LANES - offset + width])
        totals.append(jnp.sum(up, axis=0, keepdims=True))
        up = up.astype(BF)
        up_ref[level * PATCHES : (level + 1) * PATCHES] = up
        dctx = dot(up, both, ((1,), (1,))).astype(BF)
        dctx_ref[level] = dctx
        dsum = dsum + dctx.astype(F32)
    dsum_ref[...] = dsum
    totals.append(jnp.zeros((LANES - OUTS - PLEV, LANES), F32))
    totals_ref[...] = jnp.concatenate(totals, axis=0)


def decode_kernel(
    flag_ref, own_ref, north_ref, corner_ref, west_ref, perm_ref, wkv_ref, up_ref, dctx_ref, dsum_ref,
    map_ref, base_ref, wv_ref, spread_ref, gather_ref, shift_ref, totals_ref,
    owned_ref, fields_ref, keep_ref, send_ref,
    value, weights, dvalues, context, products, fields, sums, owned, decoded_out, sems,
):
    far = jnp.concatenate([ref[...] for ref in (north_ref, corner_ref, west_ref)], axis=0)
    wide = own_ref[...].astype(F32) + mm(perm_ref[...], far)
    owned[...] = wide.astype(BF)
    owned_copy = pltpu.make_async_copy(owned, owned_ref, sems.at[0])
    owned_copy.start()
    normed = layer_norm(wide)
    key = mm(normed, wkv_ref[:, :D]).astype(BF)
    value[...] = mm(normed, wv_ref[...]).astype(BF).astype(F32)
    scores = dot(key, spread_ref[...], ((1,), (1,))) * 0.125
    slabs = [scores[l * PATCHES : (l + 1) * PATCHES] for l in range(LEV)]
    top = jnp.maximum(jnp.maximum(slabs[0], slabs[1]), jnp.maximum(slabs[2], slabs[3]))
    slabs = [jnp.exp(s - top) for s in slabs]
    scale = 1.0 / (slabs[0] + slabs[1] + slabs[2] + slabs[3])
    slabs = [s * scale for s in slabs]
    for l in range(LEV):
        weights[l * PATCHES : (l + 1) * PATCHES] = slabs[l]
    head_of = lax.broadcasted_iota(jnp.int32, (BLOCK, LANES), 1) // 16
    for start in range(0, PATCHES, BLOCK):
        at = [slice(l * PATCHES + start, l * PATCHES + start + BLOCK) for l in range(LEV)]
        last = value[at[LEV - 1]]
        gaps = [value[at[l]] - last for l in range(LEV - 1)]
        heads = [weights[at[l]] for l in range(LEV - 1)]
        found = [jnp.zeros((BLOCK, D), F32) for _ in range(LEV - 1)]
        for level in range(PLEV):
            index = head_of + level * HEADS
            upstream = dctx_ref[level, start : start + BLOCK].astype(F32)
            total = last
            for l in range(LEV - 1):
                spread = jnp.take_along_axis(heads[l], index, axis=1)
                spread = jnp.concatenate([spread] * (D // LANES), axis=1)
                total = total + spread * gaps[l]
                found[l] = found[l] + spread * upstream
                product = upstream * gaps[l]
                folded = (product[:, :LANES] + product[:, LANES : 2 * LANES]) + (
                    product[:, 2 * LANES : 3 * LANES] + product[:, 3 * LANES :]
                )
                products[at[l], level * LANES : (level + 1) * LANES] = folded.astype(BF)
            context[level * PATCHES + start : level * PATCHES + start + BLOCK] = total.astype(BF)
        for l in range(LEV - 1):
            dvalues[at[l]] = found[l]
        dvalues[at[LEV - 1]] = dsum_ref[start : start + BLOCK] - (found[0] + found[1] + found[2])
    fields[...] = jnp.zeros_like(fields)
    slopes = mm(products[...], gather_ref[...])
    for level in range(PLEV):
        first, offset, width = spot(level)
        decoded = mm(context[level * PATCHES : (level + 1) * PATCHES], map_ref[...]) + base_ref[level : level + 1]
        shift = shift_ref[LANES - offset : LANES - offset + width]
        fields[:, first : first + width] += dot(decoded.astype(BF), shift, ((1,), (1,)))
    decoded_out[...] = fields[...].astype(BF)
    fields_copy = pltpu.make_async_copy(decoded_out, fields_ref, sems.at[1])
    fields_copy.start()
    slopes = [slopes[l * PATCHES : (l + 1) * PATCHES] for l in range(LEV - 1)]
    mean = sum(p * d for p, d in zip(slabs, slopes))
    dscores = [p * (d - mean) * 0.125 for p, d in zip(slabs, slopes)]
    dscores.append(slabs[LEV - 1] * mean * -0.125)
    dscores = jnp.concatenate(dscores, axis=0).astype(BF)
    sums[:D] = dot(normed, dvalues[...].astype(BF), ((0,), (0,)))
    sums[D : D + LANES] = dot(dscores, normed, ((0,), (0,)))
    outer = dot(up_ref[...], context[...], ((0,), (0,)))
    sums[D + LANES : D + LANES + OUTS] = outer[:OUTS]
    sums[D + LANES + OUTS :] = jnp.concatenate([totals_ref[...], jnp.zeros((LANES - OUTS, D - LANES), F32)], axis=1)
    second = flag_ref[0, 0] > 0
    top, bottom = sums[: ROWS // 2], sums[ROWS // 2 :]
    keep_ref[...] = jnp.where(second, bottom, top).astype(BF)
    send_ref[...] = jnp.where(second, top, bottom).astype(BF)
    owned_copy.wait()
    fields_copy.wait()


def add_kernel(left_ref, right_ref, out_ref):
    out_ref[...] = (left_ref[...].astype(F32) + right_ref[...].astype(F32)).astype(BF)


def final_kernel(flag_ref, mine_ref, other_ref, wkv_ref, queries_ref, wo_ref, whead_ref, kv_ref, query_ref, o_ref, head_ref):
    second = flag_ref[0, 0] > 0
    mine, other = mine_ref[...].astype(F32), other_ref[...].astype(F32)
    sums = jnp.concatenate([jnp.where(second, other, mine), jnp.where(second, mine, other)], axis=0).astype(BF)
    queries = queries_ref[...]
    head = whead_ref[...]
    keyed = sums[D : D + LANES]
    outer = sums[D + LANES :]
    level_sums = outer[OUTS : OUTS + 16, :LANES]
    spread = spread_queries(queries.astype(F32)).astype(BF)
    natural = natural_order()
    values = mm(sums[:D], natural)
    keys = dot(keyed, spread, ((0,), (0,)))
    c = lax.broadcasted_iota(jnp.int32, (LANES, D), 0)
    j = lax.broadcasted_iota(jnp.int32, (LANES, D), 1)
    grouped = jnp.where(c % HEADS == j // (D // HEADS), mm(keyed, wkv_ref[:, :D]), 0.0)
    grouped = jnp.sum(grouped.reshape(LANES // HEADS, HEADS, D), axis=1)
    level = grouped[:PLEV] + mm(level_sums, head)[:PLEV]
    clean = mm(outer[:OUTS], natural).astype(BF)
    out = dot(clean, head[:OUTS], ((0,), (0,)))
    pixels = mm(clean, wo_ref[...])
    pixels = pixels + dot(level_sums[:PLEV, :OUTS], queries, ((0,), (0,)))
    squares = jnp.sum(values * values) + jnp.sum(keys * keys) + jnp.sum(level * level)
    squares = squares + jnp.sum(out * out) + jnp.sum(pixels * pixels)
    limit = math.sqrt(2 * D * D + PLEV * D + D * D + D * OUTS)
    factor = jnp.minimum(1.0, limit * lax.rsqrt(jnp.full((1, 1), squares + clip_eps, F32)))
    kv_ref[:, :D] = keys * factor
    kv_ref[:, D:] = values * factor
    query_ref[...] = level * factor
    o_ref[...] = out * factor
    head_ref[...] = pixels * factor


def call(kernel, outs, spaces, scratch=(), limit=40, out_specs=None):
    where = {"V": pltpu.VMEM, "H": pltpu.HBM}
    whole, scalar = pl.BlockSpec(memory_space=pltpu.VMEM), pl.BlockSpec(memory_space=pltpu.SMEM)
    more = {} if out_specs is None else {"out_specs": out_specs}
    run = pl.pallas_call(
        kernel,
        **more,
        in_specs=[scalar if space == "S" else whole for space in spaces],
        out_shape=outs,
        scratch_shapes=list(scratch),
        compiler_params=pltpu.CompilerParams(vmem_limit_bytes=limit * 2**20),
    )

    def close(*operands):
        held = [
            pltpu.with_memory_space_constraint(x, where[space]) if space in where else x
            for space, x in zip(spaces, operands, strict=True)
        ]
        return run(*held)

    return close


def struct(shape, dtype=BF):
    return jax.ShapeDtypeStruct(shape, dtype)


def far_struct(shape, dtype=BF):
    return pltpu.HBM(shape, dtype)


def move(array, lat_step, lon_step):
    lats, lons = lax.axis_size(LAT), lax.axis_size(LON)
    route = [
        (i * lons + j, (i + lat_step) % lats * lons + (j + lon_step) % lons)
        for i in range(lats)
        for j in range(lons)
    ]
    return lax.ppermute(array, LAT + LON, route)


def swap(array):
    count = lax.axis_size("core")
    return lax.ppermute(array, "core", [(i, (i + 1) % count) for i in range(count)])


def add_up(blocks):
    return jnp.sum(blocks.astype(F32), axis=0).astype(BF)


def copies(block, axes):
    return jnp.broadcast_to(block[None], (lax.axis_size(axes),) + block.shape)


def sum_over_all(keep, send):
    rows, width = keep.shape
    mine = call(add_kernel, struct((rows, width)), "VV", limit=8)(keep, swap(send))
    chips = lax.axis_size(PLANE)
    mine = add_up(lax.all_to_all(mine.reshape(chips, rows // chips, width), PLANE, 0, 0, tiled=True))
    mine = add_up(lax.all_to_all(copies(mine, "z"), "z", 0, 0, tiled=True))
    mine = lax.all_to_all(copies(mine, PLANE), PLANE, 0, 0, tiled=True).reshape(rows, width)
    return mine, swap(mine)


def per_device(latents, mask_ids, w_qkv, w_out, w_kv, level_queries, w_o, w_head, field_cotangent):
    perm = pack_matrix()
    columns, rows, extra = label_tables()
    flag = (lax.axis_index(LAT) == lax.axis_size(LAT) - 1).astype(jnp.int32).reshape(1, 1)
    shapes = [far_struct((MAIN, D)), struct((MAIN, D)), struct((SIDE, D)), struct((SIDE, D))]
    split = 4 * SPAN
    flat = latents.reshape(TOKENS, D)
    north, corner, west = call(functools.partial(pack_kernel, PIECES[1:]), shapes[1:], "HHHHH", limit=56)(
        flat, mask_ids, jnp.asarray(perm[MAIN:], BF), jnp.asarray(columns[:, split:], BF), jnp.asarray(rows[:, split:])
    )
    main, w_out = call(own_kernel, [struct((MAIN, D)), struct((D, D))], "HHHHHH", limit=40)(
        flat,
        mask_ids,
        jnp.asarray(perm[:MAIN], BF),
        jnp.asarray(columns[:, :split], BF),
        jnp.asarray(rows[:, :split]),
        w_out,
    )
    north, corner, west = move(north, -1, 0), move(corner, -1, -1), move(west, 0, -1)
    head = jnp.pad(w_head.T, ((0, LANES - OUTS), (0, 0)))
    main, north, corner, west = call(
        attention_kernel,
        shapes,
        "SHVHHHVV",
        [pltpu.VMEM((PACKED, 3 * D), F32), pltpu.VMEM((PACKED, D), F32)],
        limit=48,
    )(flag, jnp.asarray(extra), main, north, corner, west, w_qkv, w_out)
    north, corner, west = move(north, 1, 0), move(corner, 1, 1), move(west, 0, 1)
    up, dctx, dsum, both, base, wv, own, far_perm, spread, gather, shift, totals = call(
        pre_kernel,
        [
            struct((PLEV * PATCHES, LANES)),
            struct((PLEV, PATCHES, D)),
            struct((PATCHES, D), F32),
            struct((D, LANES)),
            struct((16, LANES), F32),
            struct((D, D)),
            struct((TOKENS, D)),
            struct((TOKENS, PACKED - MAIN)),
            struct((LANES, D)),
            struct((PLEV * LANES, LANES)),
            struct((3 * LANES, LANES)),
            struct((LANES - OUTS, LANES), F32),
        ],
        "VVVVVHHH",
    )(
        field_cotangent.reshape(PATCHES, PLEV * OUTS),
        level_queries,
        w_o,
        head,
        w_kv,
        main,
        jnp.asarray(perm[:MAIN].T, BF),
        jnp.asarray(perm[MAIN:].T, BF),
    )
    core = lax.axis_index("core").astype(jnp.int32).reshape(1, 1)
    share = struct((ROWS // 2, D))
    owned, fields, keep, send = call(
        decode_kernel,
        [struct((TOKENS, D)), struct((PATCHES, PLEV * OUTS)), share, share],
        "S" + "V" * 16,
        [
            pltpu.VMEM((TOKENS, D), F32),
            pltpu.VMEM((TOKENS, LANES), F32),
            pltpu.VMEM((TOKENS, D), F32),
            pltpu.VMEM((PLEV * PATCHES, D), BF),
            pltpu.VMEM(((LEV - 1) * PATCHES, PLEV * LANES), BF),
            pltpu.VMEM((PATCHES, PLEV * OUTS), F32),
            pltpu.VMEM((ROWS, D), F32),
            pltpu.VMEM((TOKENS, D), BF),
            pltpu.VMEM((PATCHES, PLEV * OUTS), BF),
            pltpu.SemaphoreType.DMA((2,)),
        ],
        out_specs=[pl.BlockSpec(memory_space=pl.ANY)] * 2 + [pl.BlockSpec(memory_space=pltpu.VMEM)] * 2,
    )(core, own, north, corner, west, far_perm, w_kv, up, dctx, dsum, both, base, wv, spread, gather, shift, totals)
    mine, other = sum_over_all(keep, send)
    kv, query, out, pixels = call(
        final_kernel,
        [struct((D, 2 * D), F32), struct((PLEV, D), F32), struct((D, D), F32), struct((OUTS, D), F32)],
        "SVVVVVV",
    )(core, mine, other, w_kv, level_queries, w_o, head)
    shape = latents.shape
    return (owned.reshape(shape), fields.reshape(shape[1], shape[2], PLEV * OUTS), kv, query, out, pixels.T)


def solution(mesh):
    lats, lons = mesh.shape["lat"], mesh.shape["lon"]
    sizes = (lats // 2, 2, 2, lons // 4, 2)
    fine = jax.sharding.Mesh(mesh.devices.reshape(sizes), LAT + LON)
    in_specs = (
        P(None, LAT, LON, None),
        P(LAT, LON),
        P(),
        P(),
        P(),
        P(),
        P(),
        P(),
        P(LAT, LON, None),
    )
    out_specs = (P(None, LAT, LON, None), P(LAT, LON, None), P(), P(), P(), P())
    return jax.shard_map(per_device, mesh=fine, in_specs=in_specs, out_specs=out_specs, check_vma=False)
```

```python
import functools
import math

import jax
import jax.numpy as jnp
import numpy as np
from jax import lax
from jax.experimental import pallas as pl
from jax.experimental.pallas import tpu as pltpu
from jax.sharding import PartitionSpec as P

D = 512
HEADS = 8
LEV = 4
PLEV = 13
OUTS = 80
WL = 2
WH = 6
WW = 12
PATCHES = WH * 2 * WW
TOKENS = LEV * PATCHES
MAIN = 224
SIDE = 80
PACKED = 2 * MAIN + 2 * SIDE
ROWS = 768
BLOCK = 16
LANES = 128

SPAN = 256
PIECES = (
    {0: (0, 72, 0), 1: (72, 72, 0), 2: (144, 40, 0), 3: (184, 40, 0)},
    {0: (224, 72, 72), 1: (296, 72, 72), 2: (368, 40, 40), 3: (408, 40, 40)},
    {2: (448, 40, 80), 3: (488, 40, 80)},
    {2: (528, 40, 120), 3: (568, 40, 120)},
)

LAT = ("z", "x_hi")
LON = ("x_lo", "y", "core")
PLANE = ("y", "x_hi", "x_lo")

norm_eps = 1e-05
clip_eps = 1e-06
BF = jnp.bfloat16
F32 = jnp.float32


def window_order():
    level_pairs = ((1, 2), (3, 0))

    def rows_of(levels, rows, cols):
        return [(l * WH + r) * 2 * WW + c for l in levels for r in rows for c in cols]

    order = []
    for rows in ((3, 4, 5), (0, 1, 2)):
        for pair in level_pairs:
            order += rows_of(pair, rows, range(6, 18))
        for pair in level_pairs:
            order += rows_of(pair, rows, range(18, 24)) + [-1] * 4
    for rows in ((0, 1, 2), (3, 4, 5)):
        for pair in level_pairs:
            order += rows_of(pair, rows, range(0, 6)) + [-1] * 4
    return np.array(order)


def pack_matrix():
    order = window_order()
    return (order[:, None] == np.arange(TOKENS)[None, :]).astype(np.float32)


def label_tables():
    order = window_order()
    row, col, level = order // (2 * WW) % WH, order % (2 * WW), order // PATCHES
    columns = np.zeros((2 * WW, 12 * SPAN), np.float32)
    rows = np.zeros((8, 12 * SPAN), np.float32)
    extra = np.zeros((8, SPAN), np.float32)
    segment = 0
    for starts, far in zip(PIECES, (False, True, True, False)):
        for window, (at, count, place) in starts.items():
            for i in range(count):
                lane, token = place + i, at + i
                if order[token] < 0:
                    extra[window, lane] = -1
                    continue
                columns[col[token], segment * SPAN + lane] = 1
                rows[row[token], segment * SPAN + lane] = 1
                extra[window, lane] = 8 * (level[token] == 0)
                extra[4 + window, lane] = 4 * far
            segment += 1
    return columns, rows, extra


def dot(a, b, contract):
    return lax.dot_general(a, b, (contract, ((), ())), preferred_element_type=F32)


def mm(a, b):
    return dot(a, b, ((1,), (0,)))


def layer_norm(wide):
    center = wide - jnp.mean(wide, axis=-1, keepdims=True)
    spread = jnp.mean(center * center, axis=-1, keepdims=True)
    return (center * lax.rsqrt(spread + norm_eps)).astype(BF)


def pack_kernel(pieces, x_ref, ids_ref, perm_ref, columns_ref, rows_ref, *piece_refs):
    ids = ids_ref[...].astype(F32).astype(BF)
    lines = jnp.sum(mm(ids, columns_ref[...]) * rows_ref[:WH], axis=0, keepdims=True)
    x = x_ref[...]
    segment = 0
    first = 0
    for ref, windows in zip(piece_refs, pieces, strict=True):
        height = ref.shape[0]
        packed = mm(perm_ref[first : first + height], x)
        first += height
        bottom = [jnp.zeros((12, SPAN), F32)]
        for window in range(4):
            if window in windows:
                bottom.append(lines[:, segment * SPAN : (segment + 1) * SPAN])
                segment += 1
            else:
                bottom.append(jnp.zeros((1, SPAN), F32))
        bottom = jnp.concatenate(bottom, axis=0)
        bottom = jnp.concatenate([bottom, jnp.zeros((16, D - SPAN), F32)], axis=1)
        ref[: height - 16] = packed[: height - 16].astype(BF)
        ref[height - 16 :] = (packed[height - 16 :] + bottom).astype(BF)


def own_kernel(x_ref, ids_ref, perm_ref, columns_ref, rows_ref, wout_ref, main_ref, wout_out):
    wout_out[...] = wout_ref[...]
    pack_kernel(PIECES[:1], x_ref, ids_ref, perm_ref, columns_ref, rows_ref, main_ref)


def attention_kernel(
    flag_ref, extra_ref, main_ref, north_ref, corner_ref, west_ref, wqkv_ref, wout_ref,
    main_out, north_out, corner_out, west_out, proj, context,
):
    pieces = (main_ref, north_ref, corner_ref, west_ref)
    wide = jnp.concatenate([ref[...].astype(F32) for ref in pieces], axis=0)
    proj[...] = mm(layer_norm(wide), wqkv_ref[...])
    lines = sum(ref[ref.shape[0] - 16 :, :SPAN].astype(F32) for ref in pieces)[12:]
    lines = lines + extra_ref[:4] + jnp.where(flag_ref[0, 0] > 0, extra_ref[4:], 0.0)
    lines = jnp.concatenate([lines, lines], axis=0)
    i = lax.broadcasted_iota(jnp.int32, (SPAN, SPAN), 0)
    j = lax.broadcasted_iota(jnp.int32, (SPAN, SPAN), 1)
    standing = dot((i == j).astype(F32).astype(BF), lines.astype(BF), ((1,), (1,)))
    n, w, c = MAIN, 2 * MAIN, 2 * MAIN + SIDE
    windows = (
        (0, 144, ((0, 72), (n, 72))),
        (1, 144, ((72, 72), (n + 72, 72))),
        (2, 160, ((144, 40), (n + 144, 40), (w, 40), (c, 40))),
        (3, 160, ((184, 40), (n + 184, 40), (w + 40, 40), (c + 40, 40))),
    )
    low = lax.broadcasted_iota(jnp.int32, (1, LANES), 1) < D // HEADS
    for index, size, parts in windows:
        allowed = standing[:size, index : index + 1] == lines[index : index + 1, :size]
        bias = jnp.where(allowed, 0.0, -jnp.inf)
        bias = jnp.concatenate([bias, bias], axis=0)

        def take(start):
            return jnp.concatenate([proj[at : at + count, start : start + LANES] for at, count in parts], axis=0)

        for pair in range(HEADS // 2):
            lane = pair * LANES
            query = take(lane).astype(BF).astype(F32) * 0.125
            key = take(D + lane).astype(BF)
            value = take(2 * D + lane).astype(BF).astype(F32)
            both = jnp.concatenate([jnp.where(low, query, 0.0), jnp.where(low, 0.0, query)], axis=0).astype(BF)
            scores = dot(both, key, ((1,), (1,))) + bias
            weights = jnp.exp(scores - jnp.max(scores, axis=-1, keepdims=True)).astype(BF)
            even = mm(weights[:size], jnp.where(low, value, 1.0).astype(BF))
            odd = mm(weights[size:], jnp.where(low, 1.0, value).astype(BF))
            sums = pltpu.roll(jnp.where(low, odd, even), LANES // 2, 1)
            result = jnp.where(low, even, odd) / sums
            start = 0
            for at, count in parts:
                context[at : at + count, lane : lane + LANES] = result[start : start + count]
                start += count
    mixed = wide + mm(context[...].astype(BF), wout_ref[...])
    mixed = mixed.astype(BF)
    main_out[...] = mixed[:n]
    north_out[...] = mixed[n:w]
    corner_out[...] = mixed[w:c]
    west_out[...] = mixed[c:]


def shift_matrix(offset, width):
    i = lax.broadcasted_iota(jnp.int32, (width, LANES), 0)
    j = lax.broadcasted_iota(jnp.int32, (width, LANES), 1)
    return ((i - offset == j) & (j < OUTS)).astype(F32).astype(BF)


def spot(level):
    first = level * OUTS // LANES * LANES
    return first, level * OUTS - first, min(2 * LANES, PLEV * OUTS - first)


def spread_queries(queries):
    parts = [jnp.broadcast_to(queries[a : a + 1], (HEADS, D)) for a in range(PLEV)]
    parts.append(jnp.zeros((LANES - HEADS * PLEV, D), F32))
    tall = jnp.concatenate(parts, axis=0)
    c = lax.broadcasted_iota(jnp.int32, (LANES, D), 0)
    j = lax.broadcasted_iota(jnp.int32, (LANES, D), 1)
    return jnp.where(c % HEADS == j // (D // HEADS), tall, 0.0)


def lane_of(j):
    size = D // HEADS
    return j % size // 16 * LANES + j // size * 16 + j % 16


def feature_order():
    wanted = lane_of(lax.broadcasted_iota(jnp.int32, (D, LANES), 0))
    lane = lax.broadcasted_iota(jnp.int32, (D, LANES), 1)
    tiles = [jnp.where(wanted == lane + start, 1.0, 0.0) for start in range(0, D, LANES)]
    return jnp.concatenate(tiles, axis=1).astype(BF)


def natural_order():
    wanted = lane_of(lax.broadcasted_iota(jnp.int32, (8, D), 1))
    lane = lax.broadcasted_iota(jnp.int32, (8, D), 0)
    tiles = [jnp.where(wanted == lane + start, 1.0, 0.0) for start in range(0, D, 8)]
    return jnp.concatenate(tiles, axis=0).astype(BF)


def pre_kernel(
    cot_ref, queries_ref, wo_ref, whead_ref, wkv_ref, main_ref, main_perm, far_perm,
    up_ref, dctx_ref, dsum_ref, map_ref, base_ref, wv_ref, own_ref, far_perm_out,
):
    own_ref[...] = mm(main_perm[...], main_ref[...]).astype(BF)
    far_perm_out[...] = far_perm[...]
    order = feature_order()
    wv_ref[...] = mm(wkv_ref[:, D:], order).astype(BF)
    head = whead_ref[...]
    both = dot(wo_ref[...], head, ((1,), (1,))).astype(BF)
    both = dot(order, both, ((0,), (0,))).astype(BF)
    map_ref[...] = both
    base_ref[...] = jnp.concatenate(
        [dot(queries_ref[...], head, ((1,), (1,))), jnp.zeros((16 - PLEV, LANES), F32)], axis=0
    )
    dsum = jnp.zeros((PATCHES, D), F32)
    for level in range(PLEV):
        first, offset, width = spot(level)
        up = mm(cot_ref[:, first : first + width], shift_matrix(offset, width)).astype(BF)
        up_ref[level] = up
        dctx = dot(up, both, ((1,), (1,))).astype(BF)
        dctx_ref[level] = dctx
        dsum = dsum + dctx.astype(F32)
    dsum_ref[...] = dsum


def decode_kernel(
    flag_ref, own_ref, north_ref, corner_ref, west_ref, perm_ref, wkv_ref, queries_ref, up_ref, dctx_ref, dsum_ref,
    map_ref, base_ref, wv_ref,
    owned_ref, fields_ref, keep_ref, send_ref,
    value, weights, dvalues, context, products, fields, sums, owned, decoded_out, sems,
):
    far = jnp.concatenate([ref[...] for ref in (north_ref, corner_ref, west_ref)], axis=0)
    wide = own_ref[...].astype(F32) + mm(perm_ref[...], far)
    owned[...] = wide.astype(BF)
    owned_copy = pltpu.make_async_copy(owned, owned_ref, sems.at[0])
    owned_copy.start()
    normed = layer_norm(wide)
    key = mm(normed, wkv_ref[:, :D]).astype(BF)
    value[...] = mm(normed, wv_ref[...]).astype(BF).astype(F32)
    queries = spread_queries(queries_ref[...].astype(F32)).astype(BF)
    scores = dot(key, queries, ((1,), (1,))) * 0.125
    slabs = [scores[l * PATCHES : (l + 1) * PATCHES] for l in range(LEV)]
    top = jnp.maximum(jnp.maximum(slabs[0], slabs[1]), jnp.maximum(slabs[2], slabs[3]))
    slabs = [jnp.exp(s - top) for s in slabs]
    scale = 1.0 / (slabs[0] + slabs[1] + slabs[2] + slabs[3])
    slabs = [s * scale for s in slabs]
    for l in range(LEV):
        weights[l * PATCHES : (l + 1) * PATCHES] = slabs[l]
    head_of = lax.broadcasted_iota(jnp.int32, (BLOCK, LANES), 1) // 16
    for start in range(0, PATCHES, BLOCK):
        at = [slice(l * PATCHES + start, l * PATCHES + start + BLOCK) for l in range(LEV)]
        last = value[at[LEV - 1]]
        gaps = [value[at[l]] - last for l in range(LEV - 1)]
        heads = [weights[at[l]] for l in range(LEV - 1)]
        found = [jnp.zeros((BLOCK, D), F32) for _ in range(LEV - 1)]
        for level in range(PLEV):
            index = head_of + level * HEADS
            upstream = dctx_ref[level, start : start + BLOCK].astype(F32)
            total = last
            for l in range(LEV - 1):
                spread = jnp.take_along_axis(heads[l], index, axis=1)
                spread = jnp.concatenate([spread] * (D // LANES), axis=1)
                total = total + spread * gaps[l]
                found[l] = found[l] + spread * upstream
                product = upstream * gaps[l]
                folded = (product[:, :LANES] + product[:, LANES : 2 * LANES]) + (
                    product[:, 2 * LANES : 3 * LANES] + product[:, 3 * LANES :]
                )
                products[at[l], level * LANES : (level + 1) * LANES] = folded.astype(BF)
            context[level * PATCHES + start : level * PATCHES + start + BLOCK] = total.astype(BF)
        for l in range(LEV - 1):
            dvalues[at[l]] = found[l]
        dvalues[at[LEV - 1]] = dsum_ref[start : start + BLOCK] - (found[0] + found[1] + found[2])
    fields[...] = jnp.zeros_like(fields)
    row = lax.broadcasted_iota(jnp.int32, (PLEV * LANES, LANES), 0)
    c = lax.broadcasted_iota(jnp.int32, (PLEV * LANES, LANES), 1)
    slopes = mm(products[...], jnp.where(row // 16 == c, 1.0, 0.0).astype(BF))
    for level in range(PLEV):
        first, offset, width = spot(level)
        decoded = mm(context[level * PATCHES : (level + 1) * PATCHES], map_ref[...]) + base_ref[level : level + 1]
        fields[:, first : first + width] += dot(decoded.astype(BF), shift_matrix(offset, width), ((1,), (1,)))
    decoded_out[...] = fields[...].astype(BF)
    fields_copy = pltpu.make_async_copy(decoded_out, fields_ref, sems.at[1])
    fields_copy.start()
    slopes = [slopes[l * PATCHES : (l + 1) * PATCHES] for l in range(LEV - 1)]
    mean = sum(p * d for p, d in zip(slabs, slopes))
    dscores = [p * (d - mean) * 0.125 for p, d in zip(slabs, slopes)]
    dscores.append(slabs[LEV - 1] * mean * -0.125)
    dscores = jnp.concatenate(dscores, axis=0).astype(BF)
    sums[:D] = dot(normed, dvalues[...].astype(BF), ((0,), (0,)))
    sums[D : D + LANES] = dot(dscores, normed, ((0,), (0,)))
    up = jnp.concatenate([up_ref[a] for a in range(PLEV)], axis=0)
    outer = dot(up, context[...], ((0,), (0,)))
    sums[D + LANES : D + LANES + OUTS] = outer[:OUTS]
    totals = [jnp.sum(up_ref[a].astype(F32), axis=0, keepdims=True) for a in range(PLEV)]
    totals.append(jnp.zeros((LANES - OUTS - PLEV, LANES), F32))
    totals = jnp.concatenate(totals, axis=0)
    sums[D + LANES + OUTS :] = jnp.concatenate([totals, jnp.zeros((LANES - OUTS, D - LANES), F32)], axis=1)
    second = flag_ref[0, 0] > 0
    top, bottom = sums[: ROWS // 2], sums[ROWS // 2 :]
    keep_ref[...] = jnp.where(second, bottom, top).astype(BF)
    send_ref[...] = jnp.where(second, top, bottom).astype(BF)
    owned_copy.wait()
    fields_copy.wait()


def add_kernel(left_ref, right_ref, out_ref):
    out_ref[...] = (left_ref[...].astype(F32) + right_ref[...].astype(F32)).astype(BF)


def final_kernel(flag_ref, mine_ref, other_ref, wkv_ref, queries_ref, wo_ref, whead_ref, kv_ref, query_ref, o_ref, head_ref):
    second = flag_ref[0, 0] > 0
    mine, other = mine_ref[...].astype(F32), other_ref[...].astype(F32)
    sums = jnp.concatenate([jnp.where(second, other, mine), jnp.where(second, mine, other)], axis=0).astype(BF)
    queries = queries_ref[...]
    head = whead_ref[...]
    keyed = sums[D : D + LANES]
    outer = sums[D + LANES :]
    level_sums = outer[OUTS : OUTS + 16, :LANES]
    spread = spread_queries(queries.astype(F32)).astype(BF)
    natural = natural_order()
    values = mm(sums[:D], natural)
    keys = dot(keyed, spread, ((0,), (0,)))
    c = lax.broadcasted_iota(jnp.int32, (LANES, D), 0)
    j = lax.broadcasted_iota(jnp.int32, (LANES, D), 1)
    grouped = jnp.where(c % HEADS == j // (D // HEADS), mm(keyed, wkv_ref[:, :D]), 0.0)
    grouped = jnp.sum(grouped.reshape(LANES // HEADS, HEADS, D), axis=1)
    level = grouped[:PLEV] + mm(level_sums, head)[:PLEV]
    clean = mm(outer[:OUTS], natural).astype(BF)
    out = dot(clean, head[:OUTS], ((0,), (0,)))
    pixels = mm(clean, wo_ref[...])
    pixels = pixels + dot(level_sums[:PLEV, :OUTS], queries, ((0,), (0,)))
    squares = jnp.sum(values * values) + jnp.sum(keys * keys) + jnp.sum(level * level)
    squares = squares + jnp.sum(out * out) + jnp.sum(pixels * pixels)
    limit = math.sqrt(2 * D * D + PLEV * D + D * D + D * OUTS)
    factor = jnp.minimum(1.0, limit * lax.rsqrt(jnp.full((1, 1), squares + clip_eps, F32)))
    kv_ref[:, :D] = keys * factor
    kv_ref[:, D:] = values * factor
    query_ref[...] = level * factor
    o_ref[...] = out * factor
    head_ref[...] = pixels * factor


def call(kernel, outs, spaces, scratch=(), limit=40, out_specs=None):
    where = {"V": pltpu.VMEM, "H": pltpu.HBM}
    whole, scalar = pl.BlockSpec(memory_space=pltpu.VMEM), pl.BlockSpec(memory_space=pltpu.SMEM)
    more = {} if out_specs is None else {"out_specs": out_specs}
    run = pl.pallas_call(
        kernel,
        **more,
        in_specs=[scalar if space == "S" else whole for space in spaces],
        out_shape=outs,
        scratch_shapes=list(scratch),
        compiler_params=pltpu.CompilerParams(vmem_limit_bytes=limit * 2**20),
    )

    def close(*operands):
        held = [
            pltpu.with_memory_space_constraint(x, where[space]) if space in where else x
            for space, x in zip(spaces, operands, strict=True)
        ]
        return run(*held)

    return close


def struct(shape, dtype=BF):
    return jax.ShapeDtypeStruct(shape, dtype)


def far_struct(shape, dtype=BF):
    return pltpu.HBM(shape, dtype)


def move(array, lat_step, lon_step):
    lats, lons = lax.axis_size(LAT), lax.axis_size(LON)
    route = [
        (i * lons + j, (i + lat_step) % lats * lons + (j + lon_step) % lons)
        for i in range(lats)
        for j in range(lons)
    ]
    return lax.ppermute(array, LAT + LON, route)


def swap(array):
    count = lax.axis_size("core")
    return lax.ppermute(array, "core", [(i, (i + 1) % count) for i in range(count)])


def add_up(blocks):
    return jnp.sum(blocks.astype(F32), axis=0).astype(BF)


def copies(block, axes):
    return jnp.broadcast_to(block[None], (lax.axis_size(axes),) + block.shape)


def sum_over_all(keep, send):
    rows, width = keep.shape
    mine = call(add_kernel, struct((rows, width)), "VV", limit=8)(keep, swap(send))
    chips = lax.axis_size(PLANE)
    mine = add_up(lax.all_to_all(mine.reshape(chips, rows // chips, width), PLANE, 0, 0, tiled=True))
    mine = add_up(lax.all_to_all(copies(mine, "z"), "z", 0, 0, tiled=True))
    mine = lax.all_to_all(copies(mine, PLANE), PLANE, 0, 0, tiled=True).reshape(rows, width)
    return mine, swap(mine)


def per_device(latents, mask_ids, w_qkv, w_out, w_kv, level_queries, w_o, w_head, field_cotangent):
    perm = pack_matrix()
    columns, rows, extra = label_tables()
    flag = (lax.axis_index(LAT) == lax.axis_size(LAT) - 1).astype(jnp.int32).reshape(1, 1)
    shapes = [far_struct((MAIN, D)), struct((MAIN, D)), struct((SIDE, D)), struct((SIDE, D))]
    split = 4 * SPAN
    flat = latents.reshape(TOKENS, D)
    north, corner, west = call(functools.partial(pack_kernel, PIECES[1:]), shapes[1:], "HHHHH", limit=56)(
        flat, mask_ids, jnp.asarray(perm[MAIN:], BF), jnp.asarray(columns[:, split:], BF), jnp.asarray(rows[:, split:])
    )
    main, w_out = call(own_kernel, [struct((MAIN, D)), struct((D, D))], "HHHHHH", limit=40)(
        flat,
        mask_ids,
        jnp.asarray(perm[:MAIN], BF),
        jnp.asarray(columns[:, :split], BF),
        jnp.asarray(rows[:, :split]),
        w_out,
    )
    north, corner, west = move(north, -1, 0), move(corner, -1, -1), move(west, 0, -1)
    head = jnp.pad(w_head.T, ((0, LANES - OUTS), (0, 0)))
    main, north, corner, west = call(
        attention_kernel,
        shapes,
        "SHVHHHVV",
        [pltpu.VMEM((PACKED, 3 * D), F32), pltpu.VMEM((PACKED, D), F32)],
        limit=48,
    )(flag, jnp.asarray(extra), main, north, corner, west, w_qkv, w_out)
    north, corner, west = move(north, 1, 0), move(corner, 1, 1), move(west, 0, 1)
    up, dctx, dsum, both, base, wv, own, far_perm = call(
        pre_kernel,
        [
            struct((PLEV, PATCHES, LANES)),
            struct((PLEV, PATCHES, D)),
            struct((PATCHES, D), F32),
            struct((D, LANES)),
            struct((16, LANES), F32),
            struct((D, D)),
            struct((TOKENS, D)),
            struct((TOKENS, PACKED - MAIN)),
        ],
        "VVVVVHHH",
    )(
        field_cotangent.reshape(PATCHES, PLEV * OUTS),
        level_queries,
        w_o,
        head,
        w_kv,
        main,
        jnp.asarray(perm[:MAIN].T, BF),
        jnp.asarray(perm[MAIN:].T, BF),
    )
    core = lax.axis_index("core").astype(jnp.int32).reshape(1, 1)
    share = struct((ROWS // 2, D))
    owned, fields, keep, send = call(
        decode_kernel,
        [struct((TOKENS, D)), struct((PATCHES, PLEV * OUTS)), share, share],
        "SVVVVVVVVVVVVV",
        [
            pltpu.VMEM((TOKENS, D), F32),
            pltpu.VMEM((TOKENS, LANES), F32),
            pltpu.VMEM((TOKENS, D), F32),
            pltpu.VMEM((PLEV * PATCHES, D), BF),
            pltpu.VMEM(((LEV - 1) * PATCHES, PLEV * LANES), BF),
            pltpu.VMEM((PATCHES, PLEV * OUTS), F32),
            pltpu.VMEM((ROWS, D), F32),
            pltpu.VMEM((TOKENS, D), BF),
            pltpu.VMEM((PATCHES, PLEV * OUTS), BF),
            pltpu.SemaphoreType.DMA((2,)),
        ],
        out_specs=[pl.BlockSpec(memory_space=pl.ANY)] * 2 + [pl.BlockSpec(memory_space=pltpu.VMEM)] * 2,
    )(core, own, north, corner, west, far_perm, w_kv, level_queries, up, dctx, dsum, both, base, wv)
    mine, other = sum_over_all(keep, send)
    kv, query, out, pixels = call(
        final_kernel,
        [struct((D, 2 * D), F32), struct((PLEV, D), F32), struct((D, D), F32), struct((OUTS, D), F32)],
        "SVVVVVV",
    )(core, mine, other, w_kv, level_queries, w_o, head)
    shape = latents.shape
    return (owned.reshape(shape), fields.reshape(shape[1], shape[2], PLEV * OUTS), kv, query, out, pixels.T)


def solution(mesh):
    lats, lons = mesh.shape["lat"], mesh.shape["lon"]
    sizes = (lats // 2, 2, 2, lons // 4, 2)
    fine = jax.sharding.Mesh(mesh.devices.reshape(sizes), LAT + LON)
    in_specs = (
        P(None, LAT, LON, None),
        P(LAT, LON),
        P(),
        P(),
        P(),
        P(),
        P(),
        P(),
        P(LAT, LON, None),
    )
    out_specs = (P(None, LAT, LON, None), P(LAT, LON, None), P(), P(), P(), P())
    return jax.shard_map(per_device, mesh=fine, in_specs=in_specs, out_specs=out_specs, check_vma=False)
```
